32 devices in a mesh: ctx: 16 (over z, y, core), fsdp: 2 (over x).
Axes of the slice: x: 2, y: 2, z: 4, core: 2. Of those that a mesh axis runs over, the one named last changes fastest.
Arguments:
- stream_in: bfloat16 [1, 4096, 1280], P(None, ('ctx', 'fsdp')), may hold values from -24 to 24
- pairing: int32 [16], replicated, may hold values from 0 to 15, each once
- w_query: bfloat16 [1280, 1280], P('fsdp'), may hold values from -0.15625 to 0.15625
- w_key: bfloat16 [1280, 1280], P('fsdp'), may hold values from -0.15625 to 0.15625
- w_value: bfloat16 [1280, 1280], P('fsdp'), may hold values from -0.15625 to 0.15625
- w_output: bfloat16 [1280, 1280], P('fsdp'), may hold values from -4 to 4
- w_hidden: bfloat16 [1280, 1280], P('fsdp'), may hold values from -0.15625 to 0.15625
- w_return: bfloat16 [1280, 1280], P('fsdp'), may hold values from -0.15625 to 0.15625
- gain_attn: bfloat16 [1280], P('fsdp'), may hold values from 0.099609375 to 1.8984375
- gain_mlp: bfloat16 [1280], P('fsdp'), may hold values from 0.099609375 to 1.8984375
- query_scale: bfloat16 [80], P('fsdp'), may hold values from 0.69921875 to 2.1875
- cotangent: bfloat16 [1, 4096, 1280], P(None, ('ctx', 'fsdp')), may hold values from -6 to 6
Outputs:
- stream_out: bfloat16 [1, 4096, 1280], P(None, ('ctx', 'fsdp'))
- grad_in: bfloat16 [1, 4096, 1280], P(None, ('ctx', 'fsdp'))
- grad_query: float32 [1280, 1280], P('fsdp')
- grad_key: float32 [1280, 1280], P('fsdp')
- value_weight_gradient: float32 [1280, 1280], P('fsdp')
- grad_output: float32 [1280, 1280], P('fsdp')
- grad_hidden: float32 [1280, 1280], P('fsdp')
- return_weight_gradient: float32 [1280, 1280], P('fsdp')
- grad_gain_attn: float32 [1280], P('fsdp')
- grad_gain_mlp: float32 [1280], P('fsdp')
- grad_query_scale: float32 [80], P('fsdp')
- root_means: float32 [2], replicated
The draws below stay inside these ranges and needn't reach their ends.
All inputs are finite; a program needn't handle non-finite values.
Results may differ from the reference program's by a relative error of at most 0.015.
Values may be sent and summed in bfloat16 or wider, within the bound.
No kernel may reach another device: no remote copies, remote signals or barrier semaphores. Data moves between devices by JAX's collectives and lax.ppermute only.
A program may use at most 576 MiB of HBM per device.

```python
import math
import jax
import jax.numpy as jnp
from jax import lax

D = 1280
H = 16
HD = 80
FF = 1280
BLK = 128
SEQS = 1
NB = 32
NP = 16
DPP = 2
QR = 64
LS = 4096


def draw_stream_in(key, part):
    key = jax.random.fold_in(key, 11)
    first_key, second_key = jax.random.split(key)
    position = jnp.arange(LS, dtype=jnp.float32) / LS
    base = jnp.clip(jax.random.normal(first_key, (SEQS, LS, D), jnp.float32), -4.0, 4.0)
    ramp = 4.0 ** position
    rough = jnp.exp(jax.random.uniform(second_key, (SEQS, LS, 1), jnp.float32, -0.35, 0.35))
    return (base * ramp[None, :, None] * rough).astype(jnp.bfloat16)


def level_of(stream_key, extent, pieces, low, high):
    gain, own = 1.0, jax.random.fold_in(stream_key, 6)
    for axis_at, shards_of in pieces:
        draws = jnp.exp(jax.random.uniform(jax.random.fold_in(own, axis_at), (shards_of,), jnp.float32, low / len(pieces), high / len(pieces)))
        gain = gain * jnp.repeat(draws, extent[axis_at] // shards_of).reshape([-1 if axis == axis_at else 1 for axis in range(len(extent))])
    return gain


def centred(key, dims, deviation, reach, cuts=(), kind=jnp.bfloat16):
    gain = level_of(key, dims, cuts, -0.22, 0.18) if cuts else 1.0
    entries = jax.random.normal(key, dims, jnp.float32) * deviation * gain
    return jnp.minimum(jnp.maximum(entries, -reach), reach).astype(kind)


def setup_inputs(seed: int = 0) -> dict:
    arg_keys = jax.random.split(jax.random.key(seed), 13)
    stream_in = draw_stream_in(jax.random.fold_in(arg_keys[12], 71), 0)
    pairing = jax.random.permutation(arg_keys[1], NP).astype(jnp.int32)
    w_query = centred(arg_keys[2], (D, D), D ** -0.5, 0.15625, ((0, 2),))
    w_key = centred(arg_keys[3], (D, D), D ** -0.5, 0.15625, ((0, 2),))
    w_value = centred(arg_keys[4], (D, D), D ** -0.5, 0.15625, ((0, 2),))
    w_output = centred(arg_keys[5], (D, D), (max(1, LS // 2048)) ** -0.5, 4.0, ((0, 2),))
    w_hidden = centred(arg_keys[6], (D, FF), D ** -0.5, 0.15625, ((0, 2),))
    w_return = centred(arg_keys[7], (FF, D), FF ** -0.5, 0.15625, ((0, 2),))
    gain_attn = jnp.clip(1.0 + 0.18 * jax.random.normal(arg_keys[8], (D,), jnp.float32), 0.099609375, 1.8984375).astype(jnp.bfloat16)
    gain_mlp = jnp.clip(1.0 + 0.18 * jax.random.normal(arg_keys[9], (D,), jnp.float32), 0.099609375, 1.8984375).astype(jnp.bfloat16)
    query_scale = jnp.clip(jnp.exp(math.log(2.1875) - 1.140551 * jax.random.uniform(arg_keys[10], (HD,), jnp.float32) ** level_of(arg_keys[10], (HD,), ((0, 2),), -0.2, 0.2)), 0.69921875, 2.1875).astype(jnp.bfloat16)
    cotangent = centred(arg_keys[11], (SEQS, LS, D), 1.0, 6.0, ((1, 32),))
    return {"stream_in": stream_in, "pairing": pairing, "w_query": w_query, "w_key": w_key, "w_value": w_value, "w_output": w_output, "w_hidden": w_hidden, "w_return": w_return, "gain_attn": gain_attn, "gain_mlp": gain_mlp, "query_scale": query_scale, "cotangent": cotangent}


EPSILON = 1e-06
LOWEST = -1e+30
HIGHEST_ACCURACY = lax.Precision.HIGHEST

@jax.custom_vjp
def low(v):
    return lax.optimization_barrier(v.astype(jnp.bfloat16)).astype(jnp.float32)

@jax.custom_vjp
def low_back(v):
    return v

def low_keep(v):
    return (low(v), None)

def low_pass(kept, grad):
    return (grad,)

def back_keep(v):
    return (v, None)

def back_low(kept, grad):
    return (low(grad),)
low.defvjp(low_keep, low_pass)
low_back.defvjp(back_keep, back_low)

def block_table(pairing):
    rows_all = jnp.arange(LS, dtype=jnp.int32)
    owner = rows_all // (2 * QR)
    which_half = rows_all % (2 * QR) // QR
    chosen = jnp.take(pairing, owner // DPP)
    return jnp.where(which_half == 0, chosen, NB - 1 - chosen).astype(jnp.int32)

def attention(queries, keys, values, blocks):
    sequences = queries.shape[0]
    block_rows = 2 * BLK
    block_count = LS // block_rows
    query_blocks = queries.reshape(sequences, block_count, block_rows, H, HD).transpose(1, 0, 2, 3, 4)
    id_blocks = blocks.reshape(block_count, block_rows)

    def attend_block(inputs):
        query_block, block_ids = inputs
        scores = jnp.einsum('sqhd,skhd->shqk', query_block, keys, precision=HIGHEST_ACCURACY)
        scores = low_back(scores)
        seen = blocks[None, :] <= block_ids[:, None]
        scores = jnp.where(seen[None, None], scores, LOWEST)
        maxima = lax.optimization_barrier(jnp.max(scores, axis=-1, keepdims=True))
        weights = low(jnp.exp(scores - maxima))
        totals = lax.optimization_barrier(jnp.sum(weights, axis=-1, keepdims=True))
        summed = jnp.einsum('shqk,skhd->shqd', weights, values, precision=HIGHEST_ACCURACY)
        return (summed / totals).transpose(0, 2, 1, 3)
    result = lax.map(jax.checkpoint(attend_block), (query_blocks, id_blocks))
    return result.transpose(1, 0, 2, 3, 4).reshape(sequences, LS, H, HD)

def matmul_high(left_operand, right_operand):
    return jnp.einsum('tvh,hm->tvm', left_operand, right_operand, precision=HIGHEST_ACCURACY)

def reference(stream_in, pairing, w_query, w_key, w_value, w_output, w_hidden, w_return, gain_attn, gain_mlp, query_scale, cotangent):
    blocks = block_table(pairing)
    params = tuple((a.astype(jnp.float32) for a in (w_query, w_key, w_value, w_output, w_hidden, w_return, gain_attn, gain_mlp, query_scale)))
    stream = stream_in.astype(jnp.float32)

    def forward(inputs, wq, wk, wv, wo, w_in, w_out, gain_one, gain_two, scale_in):
        inv_one = lax.rsqrt(lax.optimization_barrier(jnp.mean(inputs * inputs, axis=-1, keepdims=True)) + EPSILON)
        norm_one = low(inputs * inv_one * gain_one)
        scale_vec = jnp.tile(scale_in, H) * HD ** (-0.5)
        queries = low(low_back(matmul_high(norm_one, wq)) * scale_vec)
        keys = low(low_back(matmul_high(norm_one, wk)))
        values = low(low_back(matmul_high(norm_one, wv)))
        shape_heads = (SEQS, LS, H, HD)
        attended = attention(queries.reshape(shape_heads), keys.reshape(shape_heads), values.reshape(shape_heads), blocks)
        attended = low(low_back(attended.reshape(SEQS, LS, D)))
        attn = low_back(matmul_high(attended, wo))
        middle = inputs + attn
        inv_two = lax.rsqrt(lax.optimization_barrier(jnp.mean(middle * middle, axis=-1, keepdims=True)) + EPSILON)
        norm_two = low(middle * inv_two * gain_two)
        hidden = low_back(matmul_high(norm_two, w_in))
        active = low(jax.nn.silu(hidden))
        mlp = matmul_high(active, w_out)
        return (middle + mlp, attn)
    output, pull, attn = jax.vjp(forward, stream, *params, has_aux=True)
    grads = pull(cotangent.astype(jnp.float32))
    root_means = jnp.stack([jnp.sqrt(jnp.mean(output * output)), jnp.sqrt(jnp.mean(attn * attn))])
    return (output.astype(jnp.bfloat16), grads[0].astype(jnp.bfloat16), grads[1], grads[2], grads[3], grads[4], grads[5], grads[6], grads[7], grads[8], grads[9], root_means)
```

```python
import functools

import jax
import jax.numpy as jnp
import numpy as np
from jax import lax
from jax.experimental import pallas as pl
from jax.experimental.pallas import tpu as pltpu
from jax.sharding import PartitionSpec as P

H = 16
HD = 80
EPSILON = 1e-06
LOWEST = -1e30
BF = jnp.bfloat16
F32 = jnp.float32
MIB = 1024 * 1024
FLOPS_A_US = 1.15e9

GROUP = 16
CHIPS = 8
RING = (0, 2, 4, 6, 7, 5, 3, 1)
ORDER = (
    ((0, 0), (0, 1))
    + tuple((off, core) for s in (1, 2, 3) for core in (0, 1) for off in (-s, s))
    + ((4, 0), (4, 1))
)
SOURCE = [
    [RING[(RING.index(h // 2) + off) % CHIPS] * 2 + ((h % 2) ^ core) for off, core in ORDER]
    for h in range(GROUP)
]
PLACE = [
    [((h % 2) ^ core) * CHIPS + (RING.index(h // 2) + off) % CHIPS for off, core in ORDER]
    for h in range(GROUP)
]

OWN_ENTRIES = (0, 2, 3, 6, 7, 10, 11, 14)
SIB_ENTRIES = (1, 4, 5, 8, 9, 12, 13, 15)

NN = (((1,), (0,)), ((), ()))
NT = (((1,), (1,)), ((), ()))
TN = (((0,), (0,)), ((), ()))


def dot(a, b, dims):
    return lax.dot_general(a, b, dims, preferred_element_type=F32)


def call(body, outs, ins, scratch=(), specs=None, out_specs=None, name=None, smem=0, after=(), grid=None, aliases=None, us=1.0, mib=24):
    given = len(ins)
    waits = len(after)

    def run(*refs):
        body(*refs[:given], *refs[given + waits :])

    if specs is None:
        specs = [pl.BlockSpec(memory_space=pltpu.VMEM)] * (given - smem)
    specs = list(specs) + [pl.BlockSpec(memory_space=pl.ANY)] * waits
    out_specs = out_specs or [pl.BlockSpec(memory_space=pltpu.VMEM)] * len(outs)
    if grid is None:
        how = dict(
            in_specs=[pl.BlockSpec(memory_space=pltpu.SMEM)] * smem + specs,
            out_specs=out_specs,
            scratch_shapes=list(scratch),
        )
    else:
        how = dict(
            grid_spec=pltpu.PrefetchScalarGridSpec(
                num_scalar_prefetch=smem,
                grid=grid,
                in_specs=specs,
                out_specs=out_specs,
                scratch_shapes=list(scratch),
            )
        )
    return pl.pallas_call(
        run,
        out_shape=[jax.ShapeDtypeStruct(shape, kind) for shape, kind in outs],
        compiler_params=pltpu.CompilerParams(vmem_limit_bytes=mib * MIB),
        cost_estimate=pl.CostEstimate(flops=int(us * FLOPS_A_US), bytes_accessed=1, transcendentals=0),
        input_output_aliases=aliases or {},
        name=name,
        **how,
    )(*ins, *after)


def start_copies(jobs, sems):
    copies = []
    for at, (source, target) in enumerate(jobs):
        copy = pltpu.make_async_copy(source, target, sems.at[at])
        copy.start()
        copies.append(copy)
    return copies


def slab_body(spot, q0, q1, k0, k1, v0, v1, gain_one, gain_two, scale, out, turned):
    start = spot[3] * HD
    off = pl.multiple_of(start - start // 128 * 128, 16)
    for w, (left, right) in enumerate(((q0, q1), (k0, k1), (v0, v1))):
        turned[:128] = left[...].astype(F32).T
        turned[128:] = right[...].astype(F32).T
        out[w * HD : w * HD + HD] = turned[pl.ds(off, HD)].astype(BF)
    width = out.shape[1]
    part = scale.shape[0]
    line = jnp.concatenate([line_of(scale), jnp.zeros((1, width - part), F32)], axis=1)
    tail = [line_of(gain_one), line_of(gain_two), line, jnp.zeros((13, width), F32)]
    out[3 * HD :] = jnp.concatenate(tail, axis=0).astype(BF)


def line_of(vector):
    return vector[...].astype(F32).reshape(1, vector.shape[0])


def setup_body(spot, slab, slab_x, weight, gains, scale_col, scale_row):
    width = slab.shape[1]
    f = spot[0]
    mine, theirs = slab[...], slab_x[...]
    left = jnp.where(f == 0, mine, theirs)
    right = jnp.where(f == 0, theirs, mine)
    weight[:, :width] = left[: 3 * HD]
    weight[:, width:] = right[: 3 * HD]
    left, right = left[3 * HD :].astype(F32), right[3 * HD :].astype(F32)
    gains[...] = jnp.concatenate([left[:8], right[:8]], axis=1)
    part = HD // 2
    row = jnp.concatenate([left[2:3, :part], right[2:3, :part], jnp.zeros((1, 128 - HD), F32)], axis=1)
    row = jnp.broadcast_to(row, (128, 128))
    scale_row[...] = row[:8]
    scale_col[...] = row.T[:HD, :1] * HD ** (-0.5)


def project_body(layout, spot, *refs):
    count, pieces, has_previous, jobs, slot = layout
    first = slot == 0
    xs, refs = refs[:count], refs[count:]
    (gains, weight, weight_sib, scale), refs = refs[:4], refs[4:]
    if has_previous:
        previous, refs = refs[0], refs[1:]
    moved, refs = refs[:jobs], refs[jobs:]
    refs = refs if first else refs[1:]
    (norm_out, q_out, kv_out, sib_out), refs = refs[:4], refs[4:]
    carried, (norm_vmem, sems, norm_sem) = refs[:-3], refs[-3:]
    copies = []
    for w, out in zip(moved, carried):
        quarter = out.shape[0]
        rows = pl.ds(pl.multiple_of(spot[1] * quarter, 16), quarter)
        copies.append((w.at[rows], out))
    copies = start_copies(copies, sems)
    x = jnp.concatenate([r[...] for r in xs], axis=0).astype(F32)
    inv = lax.rsqrt(jnp.mean(x * x, axis=-1, keepdims=True) + EPSILON)
    norm = (x * inv * gains[0:1]).astype(BF)
    norm_vmem[...] = norm.reshape(norm_vmem.shape)
    keep = pltpu.make_async_copy(norm_vmem, norm_out.at[pl.ds(slot, pieces)], norm_sem)
    keep.start()
    for which, table in enumerate((weight, weight_sib)):
        out = dot(table[...], norm, NT)
        q = (out[:HD] * scale[...]).astype(BF)
        kv = out[HD:].astype(BF)
        for j in range(pieces):
            lanes = slice(j * 128, (j + 1) * 128)
            if which == 0:
                q_out[j] = q[:, lanes]
                kv_out[j] = kv[:, lanes]
            else:
                sib_out[j, :HD] = q[:, lanes]
                sib_out[j, HD:] = kv[:, lanes]
    if has_previous:
        for j in range(previous.shape[0]):
            kv_out[pieces + j] = previous[j, HD:]
    for copy in copies:
        copy.wait()
    keep.wait()


def forward_body(layout, chunks, slots_q, slots_k, slots_out, full, total, qblock, *refs):
    count = layout["arrays"]
    arrays, refs = refs[:count], refs[count:]
    (pieces, q_t, k_t, k_rows, v_rows, att, lse), refs = refs[:7], refs[7:]
    block_q, block_kv, v_t, scores, block_out = refs
    for kind, which, index, row, entry, side in layout["blocks"]:
        for half in range(2):
            lanes = slice(half * 64, half * 64 + 64)
            if kind == "q":
                block_q[slots_q[entry, half]] = arrays[which][index, :HD, lanes]
            else:
                value = arrays[which][index, row : row + 2 * HD, lanes]
                block_kv[side, slots_k[entry, half]] = value
    rows = 2 * 256
    ones_row = jnp.where(lax.broadcasted_iota(jnp.int32, (16, rows), 0) == 0, 1.0, 0.0).astype(BF)

    @pl.loop(0, chunks)
    def _(c):
        tile = jnp.concatenate(
            [block_kv[side, 4 * c + m] for side in range(2) for m in range(4)], axis=1
        )
        k_t[c] = tile[:HD]
        k_rows[c] = tile[:HD].astype(F32).T.astype(BF)
        v_rows[c] = tile[HD:].astype(F32).T.astype(BF)
        v_t[c] = jnp.concatenate([tile[HD:], ones_row], axis=0)

    width = q_t.shape[2]
    per = width // 64

    @pl.loop(0, q_t.shape[0])
    def _(i):
        query = jnp.concatenate([block_q[per * i + m] for m in range(per)], axis=1)
        q_t[i] = query
        ids = qblock[i]

        def scan_max(masked, c, top):
            s = dot(k_rows[c], query, NN)
            if masked:
                s = jnp.where(block_of_row(width) + 4 * c <= ids, s, LOWEST)
            scores[c] = s
            return jnp.maximum(top, jnp.max(s.reshape(rows // 8, 8, width), axis=0))

        top = jnp.full((8, width), LOWEST, F32)
        top = lax.fori_loop(0, full[i], functools.partial(scan_max, False), top)
        top = lax.fori_loop(full[i], total[i], functools.partial(scan_max, True), top)
        top = jnp.max(top, axis=0, keepdims=True)

        def gather(c, acc):
            w = jnp.exp(scores[c] - top).astype(BF)
            return acc + dot(v_t[c], w, NN)

        acc = lax.fori_loop(0, total[i], gather, jnp.zeros((HD + 16, width), F32))
        sums = acc[HD : HD + 1]
        out = acc[:HD] / sums
        att[i] = out
        lse[i] = top + jnp.log(sums)
        low = out.astype(BF)
        for m in range(per):
            block_out[per * i + m] = low[:, m * 64 : m * 64 + 64]

    for c in range(GROUP):
        pieces[c] = jnp.concatenate(
            [block_out[slots_out[c, 0]], block_out[slots_out[c, 1]]], axis=1
        )


def block_of_row(width):
    return lax.broadcasted_iota(jnp.int32, (512, width), 0) % 256 // 64


def backward_body(first, last, low, slots_out, begin, clear, qblock, scale, *refs):
    (given, q_t, k_t, k_rows, v_rows, stat, lse), refs = refs[:7], refs[7:]
    if not first:
        dq_in, refs = refs[0], refs[1:]
    (dkv_own, dkv_other), refs = refs[:2], refs[2:]
    tiles, _, width = q_t.shape
    per = width // 64
    if first:
        (grad_t, delta_out, dq), refs = refs[:3], refs[3:]
        (blocks,) = refs
        for c in range(GROUP):
            for half in range(2):
                blocks[slots_out[c, half]] = given[c, :, half * 64 : half * 64 + 64]

        @pl.loop(0, tiles)
        def _(i):
            grad = jnp.concatenate([blocks[per * i + m] for m in range(per)], axis=1)
            grad_t[i] = grad
            delta_out[i] = jnp.sum(grad.astype(F32) * stat[i], axis=0, keepdims=True)
            dq[i] = jnp.zeros((HD, width), F32)

        delta = delta_out
    else:
        grad_t, delta = given, stat
        if last:
            (dq_pieces, scale_sum, dq, blocks) = refs
        else:
            (dq,) = refs
        dq[...] = dq_in[...]

    @pl.loop(0, dkv_own.shape[0])
    def _(at):
        c = low + at

        def step(masked, i, carry):
            d_k, d_v = carry
            query, grad = q_t[i], grad_t[i]
            prob = jnp.exp(dot(k_rows[c], query, NN) - lse[i])
            if masked:
                prob = jnp.where(block_of_row(width) + 4 * c <= qblock[i], prob, 0.0)
            d_score = (prob * (dot(v_rows[c], grad, NN) - delta[i])).astype(BF)
            dq[i] += dot(k_t[c], d_score, NN)
            return d_k + dot(query, d_score, NT), d_v + dot(grad, prob.astype(BF), NT)

        carry = (jnp.zeros((HD, 512), F32), jnp.zeros((HD, 512), F32))
        carry = lax.fori_loop(begin[c], clear[c], functools.partial(step, True), carry)
        d_k, d_v = lax.fori_loop(clear[c], tiles, functools.partial(step, False), carry)
        dkv_own[at, :HD] = d_k[:, :256]
        dkv_own[at, HD:] = d_v[:, :256]
        dkv_other[at, :HD] = d_k[:, 256:].astype(BF)
        dkv_other[at, HD:] = d_v[:, 256:].astype(BF)

    if last:
        total = jnp.zeros((HD, width), F32)
        for i in range(tiles):
            total = total + dq[i] * q_t[i].astype(F32)
            rounded = (dq[i] * scale[...]).astype(BF)
            for m in range(per):
                blocks[per * i + m] = rounded[:, m * 64 : m * 64 + 64]
        scale_sum[...] = total
        for c in range(GROUP):
            dq_pieces[c] = jnp.concatenate(
                [blocks[slots_out[c, 0]], blocks[slots_out[c, 1]]], axis=1
            )


def join_body(slots_kv, dq_pieces, *refs):
    parts, (pieces, blocks) = refs[:-2], refs[-2:]
    low = 0
    for own, received in zip(parts[: len(parts) // 2], parts[len(parts) // 2 :]):

        @pl.loop(0, own.shape[0])
        def _(at, low=low, own=own, received=received):
            tile = (own[at] + received[at].astype(F32)).astype(BF)
            for m in range(4):
                blocks[4 * (low + at) + m] = tile[:, m * 64 : m * 64 + 64]

        low += own.shape[0]

    for c in range(GROUP):
        pieces[c, :HD] = dq_pieces[c]
        pieces[c, HD:] = jnp.concatenate(
            [blocks[slots_kv[c, 0]], blocks[slots_kv[c, 1]]], axis=1
        )


def qkv_grad_body(source, spot, pieces, scale_sum, *refs):
    norms, (own, other, table) = refs[:-3], refs[-3:]
    total = jnp.zeros((3 * HD, table.shape[1]), F32)
    for norm, entries in zip(norms, (OWN_ENTRIES, SIB_ENTRIES)):
        for j, entry in enumerate(entries):
            total = total + dot(pieces[source[entry]], norm[j], NN)
    table[...] = total
    width = table.shape[1] // 2
    f = spot[0]
    own[: 3 * HD] = table[:, pl.ds(pl.multiple_of(f * width, 128), width)]
    other[: 3 * HD] = table[:, pl.ds(pl.multiple_of((1 - f) * width, 128), width)].astype(BF)
    column = jnp.broadcast_to(jnp.sum(scale_sum[...], axis=1, keepdims=True), (HD, 128))
    line = column.T[:1]
    high = line.astype(BF)
    low = (line - high.astype(F32)).astype(BF)
    own[3 * HD :] = jnp.zeros((16, width), F32)
    own[3 * HD : 3 * HD + 1, :HD] = line
    tail = jnp.concatenate([high.astype(F32), low.astype(F32), jnp.zeros((14, HD), F32)], axis=0)
    other[3 * HD :] = jnp.concatenate([tail, jnp.zeros((16, width - HD), F32)], axis=1).astype(BF)


def qkv_sum_body(own, received, slab, out):
    width = own.shape[1]
    total = own[: 3 * HD] + received[: 3 * HD].astype(F32)
    out[: 3 * HD] = total.astype(BF)
    gain = jnp.sum(total * slab[: 3 * HD].astype(F32), axis=0, keepdims=True)
    tail = received[3 * HD :].astype(F32)
    line = own[3 * HD : 3 * HD + 1] + tail[0:1] + tail[1:2]
    rows = []
    for value in (gain, line):
        high = value.astype(BF).astype(F32)
        rows += [high, value - high]
    out[3 * HD :] = jnp.concatenate(rows + [jnp.zeros((12, width), F32)], axis=0).astype(BF)


def pack_body(*refs):
    ins, out = refs[:-1], refs[-1]
    width = out.shape[1]
    row = 0
    for ref in ins:
        for at in range(0, ref.shape[1], width):
            out[row : row + ref.shape[0]] = ref[:, at : at + width]
            row += ref.shape[0]


def qkv_place_body(layout, source, spot, *refs):
    count, blocks = layout
    arrays, (gain, scale_row), refs = refs[:count], refs[count : count + 2], refs[count + 2 :]
    outs, (gain_out, scale_out, table) = refs[:3], refs[3:]
    width = gain.shape[0]
    tail = jnp.zeros((16, width), F32)
    for entry, parts in blocks:
        block = [arrays[which][row : row + size] for which, row, size in parts]
        block = jnp.concatenate(block, axis=0) if len(block) > 1 else block[0]
        head = pl.multiple_of(source[entry] * HD, 16)
        for w in range(3):
            table[w, pl.ds(head, HD)] = block[w * HD : w * HD + HD]
        tail = tail + block[3 * HD :].astype(F32)
    for w in range(3):
        for at in range(0, H * HD, 256):
            outs[w][:, at : at + 256] = table[w, at : at + 256].astype(F32).T
    gain_out[...] = ((tail[0:1] + tail[1:2]) / line_of(gain)).reshape(width)
    scale = (tail[2:3, :128] + tail[3:4, :128]) / scale_row[0:1]
    part = scale_out.shape[0]
    chosen = jnp.where(spot[0] == 0, scale[:, :part], scale[:, part : 2 * part])
    scale_out[...] = chosen.reshape(part)


def rows_body(
    spot,
    att_t,
    x_in,
    g_in,
    gain_in,
    *refs,
):
    weights = (refs[:5], refs[5:8], refs[8:11])
    refs = refs[11:]
    (stream_out, dy_out, datt_out), outs, sums_out = refs[:3], refs[3:7], refs[7]
    full = refs[8:11]
    turned, sems = refs[11:]
    f, k = spot[0], spot[1]
    half, quarter = weights[1][0].shape[0], weights[1][1].shape[0]
    copies = []
    for w in range(3):
        mine, *theirs = weights[w]
        jobs = [(mine, full[w].at[pl.ds(pl.multiple_of(f * half, 16), half)])]
        for at, piece in enumerate(theirs):
            core = k if at % 2 == 0 else 1 - k
            start = (1 - f) * half + core * quarter + (quarter - piece.shape[0]) * (at // 2)
            rows = pl.ds(pl.multiple_of(start, 16), piece.shape[0])
            jobs.append((piece, full[w].at[rows]))
        copies.append(start_copies(jobs, sems.at[w]))
    w_out, w_hid, w_ret = full
    x = x_in[...].astype(F32)
    gain = gain_in[1:2]
    for copy in copies[0]:
        copy.wait()
    attn = dot(att_t[...], w_out[...], TN)
    y1 = x + attn
    inv = lax.rsqrt(jnp.mean(y1 * y1, axis=-1, keepdims=True) + EPSILON)
    unit = y1 * inv
    norm = (unit * gain).astype(BF)
    for copy in copies[1]:
        copy.wait()
    h = dot(norm, w_hid[...], NN)
    sig = jax.nn.sigmoid(h)
    act = (h * sig).astype(BF)
    for copy in copies[2]:
        copy.wait()
    stream = y1 + dot(act, w_ret[...], NN)
    stream_out[...] = stream.astype(BF)
    squares = jnp.where(
        lax.broadcasted_iota(jnp.int32, (8, 128), 0) == 0,
        jnp.sum(stream * stream),
        jnp.sum(attn * attn),
    )
    sums_out[...] = squares
    g = g_in[...]
    d_act = dot(g, w_ret[...], NT)
    d_h = (d_act * sig * (1.0 + h * (1.0 - sig))).astype(BF)
    d_norm = dot(d_h, w_hid[...], NT)
    c2 = d_norm * gain
    dy = inv * (c2 - unit * jnp.mean(c2 * unit, axis=-1, keepdims=True)) + g.astype(F32)
    dy_out[...] = dy
    dy_b = dy.astype(BF)
    datt_out[...] = dot(w_out[...], dy_b, NT).astype(BF)
    turned[0] = att_t[...]
    turned[1] = norm.astype(F32).T.astype(BF)
    turned[2] = act.astype(F32).T.astype(BF)
    for ref, ff, kk in zip(outs, (f, f, 1 - f, 1 - f), (k, 1 - k, k, 1 - k)):
        at = pl.multiple_of(ff * half + kk * quarter, 16)
        for w in range(3):
            ref[w * quarter : (w + 1) * quarter] = turned[w, pl.ds(at, quarter)]
    rows = x.shape[0]
    for ref in outs[:3]:
        for w, right in enumerate((dy_b, d_h)):
            for c in range(right.shape[1] // 128):
                start = 3 * quarter + (w * (right.shape[1] // 128) + c) * rows
                ref[start : start + rows] = right[:, c * 128 : (c + 1) * 128]


def pooled_grad_body(own, sib, far, far_left, far_right, *refs):
    gs, out = refs[:4], refs[4]
    model = out.shape[2]
    columns = model // 128
    quarter = far_left.shape[0] // 3
    rows = 128
    totals = []
    for w in range(3):
        lefts, rights = [], []
        for at, (left, right) in enumerate(
            ((own, own), (sib, sib), (far, far), (far_left, far_right))
        ):
            lefts.append(left[w * quarter : (w + 1) * quarter])
            start = 3 * quarter + w * columns * rows
            if w == 2:
                rights.append(gs[at][...])
                continue
            rights.append(
                jnp.concatenate(
                    [right[start + c * rows : start + (c + 1) * rows] for c in range(columns)], axis=1
                )
            )
        left, right = jnp.concatenate(lefts, axis=1), jnp.concatenate(rights, axis=0)
        totals.append(dot(left, right, NN))
    for c in range(CHIPS):
        rows = [t[40 * c : 40 * c + 40] for t in totals] + [jnp.zeros((8, model), F32)]
        out[c] = jnp.concatenate(rows, axis=0).astype(BF)


def reduce_step_body(step, spot, up, down, *refs):
    received, (up_out, down_out) = refs[:-2], refs[-2:]
    model = up.shape[2]
    for side, (block, out) in enumerate(((up, up_out), (down, down_out))):
        near = slice(side * model // 2, (side + 1) * model // 2)
        if step == 0:
            out[...] = block[0, :, near]
            continue
        add = received[side][...].astype(F32)
        if step == 1:
            out[...] = block[0]
            out[:, near] = (block[0, :, near].astype(F32) + add).astype(BF)
        else:
            out[...] = (block[0].astype(F32) + add).astype(BF)


def reduce_end_body(spot, block, up, down, sums, sums_x, out):
    model = block.shape[2]
    total = block[0].astype(F32) + up[...].astype(F32) + down[...].astype(F32)
    pair = sums[...] + sums_x[...]
    high = pair.astype(BF).astype(F32)
    low = pair - high
    lane = lax.broadcasted_iota(jnp.int32, (8, 128), 1)
    row = lax.broadcasted_iota(jnp.int32, (8, 128), 0)
    first = jnp.where(row == 0, high[0:1], low[0:1])
    second = jnp.where(row == 0, high[1:2], low[1:2])
    tail = jnp.where(row < 2, jnp.where(lane == 0, first, jnp.where(lane == 1, second, 0.0)), 0.0)
    tail = jnp.concatenate([tail, jnp.zeros((8, model - 128), F32)], axis=1)
    out[...] = jnp.concatenate([total[:120], tail], axis=0).astype(BF)


def rows_place_body(layout, elements, place, *refs):
    count, blocks = layout
    arrays, (w_hidden, gain), refs = refs[:count], refs[count : count + 2], refs[count + 2 :]
    outs, (gain_out, means_out) = refs[:3], refs[3:]
    tail = jnp.zeros((8, 128), F32)
    for entry, parts in blocks:
        block = [arrays[which][row : row + 128] for which, row in parts]
        block = jnp.concatenate(block, axis=1) if len(block) > 1 else block[0]
        block = block.astype(F32)
        at = pl.multiple_of(place[entry] * 40, 8)
        for w in range(3):
            outs[w][pl.ds(at, 40)] = block[w * 40 : w * 40 + 40]
        tail = tail + block[120:, :128]
    means = jnp.sqrt((tail[0:1, :2] + tail[1:2, :2]) / elements)
    means_out[...] = means.reshape(2)
    half, model = w_hidden.shape
    total = jnp.zeros((half, 128), F32)
    for at in range(0, model, 128):
        total = total + outs[1][:, at : at + 128] * w_hidden[:, at : at + 128].astype(F32)
    line = jnp.sum(total.T, axis=0, keepdims=True) / line_of(gain)
    gain_out[...] = line.reshape(half)


def inputs_product_body(back, back_x, w_q, w_k, w_v, own, other, turned):
    for side, pieces in enumerate((back, back_x)):
        for h in range(H):
            for w in range(3):
                turned[w, h * HD : h * HD + HD, side * 128 : side * 128 + 128] = pieces[
                    h, w * HD : w * HD + HD
                ]
    total = dot(w_q[...], turned[0], NN) + dot(w_k[...], turned[1], NN)
    total = total + dot(w_v[...], turned[2], NN)
    own[...] = total[:, :128]
    other[...] = total[:, 128:].astype(BF)


def inputs_grad_body(spot, x_in, dy_in, gains, own, received, out):
    mine, theirs = own[...].T, received[...].astype(F32).T
    f = spot[0]
    left = jnp.where(f == 0, mine, theirs)
    right = jnp.where(f == 0, theirs, mine)
    x = x_in[...].astype(F32)
    inv = lax.rsqrt(jnp.mean(x * x, axis=-1, keepdims=True) + EPSILON)
    unit = x * inv
    c1 = jnp.concatenate([left, right], axis=1) * gains[0:1]
    dx = inv * (c1 - unit * jnp.mean(c1 * unit, axis=-1, keepdims=True)) + dy_in[...]
    out[...] = dx.astype(BF)


def per_device(
    ctx_count,
    stream_in,
    pairing,
    w_query,
    w_key,
    w_value,
    w_output,
    w_hidden,
    w_return,
    gain_attn,
    gain_mlp,
    query_scale,
    cotangent,
):
    sequences, dev_rows, model = stream_in.shape
    half = w_query.shape[0]
    quarter = half // 2
    groups = ctx_count // GROUP
    blocks = 2 * ctx_count
    chunks = blocks // 4
    ctx = lax.axis_index("ctx")
    f = lax.axis_index("fsdp")
    head = ctx % GROUP
    k = head % 2

    def ring(a, shift):
        pairs = [
            (
                g * GROUP + RING[i] * 2 + core,
                g * GROUP + RING[(i + shift) % CHIPS] * 2 + core,
            )
            for g in range(groups)
            for i in range(CHIPS)
            for core in range(2)
        ]
        return lax.ppermute(a, "ctx", pairs)

    def swap_core(a):
        return lax.ppermute(a, "ctx", [(c, c ^ 1) for c in range(ctx_count)])

    def swap_x(a):
        return lax.ppermute(a, "fsdp", [(0, 1), (1, 0)])

    def turn_groups(a, by):
        return lax.ppermute(
            a, "ctx", [(c, (c + by * GROUP) % ctx_count) for c in range(ctx_count)]
        )

    def sum_groups(a, kind):
        total = a
        for by in range(1, groups):
            total = total + turn_groups(a.astype(kind), by).astype(a.dtype)
        return total

    def exchange(a):
        which = (
            None
            if groups == 1
            else [[g * GROUP + h for h in range(GROUP)] for g in range(groups)]
        )
        return lax.all_to_all(a, "ctx", 0, 0, axis_index_groups=which, tiled=True)

    def swap_cores(arrays):
        swapped = []
        for a in arrays:
            swapped.append(swap_core(a))
        return swapped

    def ring_step(up, down):
        return ring(up, 1), ring(down, -1)

    def ring_gather(a, axis, cut, hold=lambda v: v):
        up = down = a
        found = [(a, swap_core(a))]
        for _ in range(3):
            up, down = ring(up, 1), ring(down, -1)
            found.append((up, down, swap_core(up), swap_core(down)))
        size = a.shape[axis]
        up = ring(hold(lax.slice_in_dim(up, 0, cut, axis=axis)), 1)
        down = ring(hold(lax.slice_in_dim(down, cut, size, axis=axis)), -1)
        found.append((up, down, swap_core(up), swap_core(down)))
        return found

    source = jnp.asarray(SOURCE, jnp.int32)[head]
    place = jnp.asarray(PLACE, jnp.int32)[head]
    chip = head // 2
    ring_at = jnp.where(chip % 2 == 0, chip // 2, CHIPS - 1 - chip // 2)
    spot = jnp.stack([f, k, ring_at, head]).astype(jnp.int32)
    group = ctx // GROUP

    def pairs_of(which):
        return lax.dynamic_slice_in_dim(pairing, which * GROUP, GROUP, 0)

    def slots_of(pairs):
        return jnp.stack([pairs, blocks - 1 - pairs], axis=1).astype(jnp.int32)

    my_pairs = pairs_of(group)
    slots_ctx = slots_of(my_pairs)
    slots_ring = slots_ctx[source]
    if groups == 1:
        ids = np.arange(2 * GROUP, dtype=np.int32)
        slots_q, slots_out = slots_ring, slots_ctx
        slots_k = slots_ring
    else:
        flat = slots_ctx.reshape(-1)
        rank = jnp.sum((flat[None, :] < flat[:, None]).astype(jnp.int32), axis=1)
        ids = jnp.sum(
            jnp.where(rank[None, :] == jnp.arange(2 * GROUP)[:, None], flat[None, :], 0), axis=1
        ).astype(jnp.int32)
        slots_out = rank.reshape(GROUP, 2).astype(jnp.int32)
        slots_q = slots_out[source]
        slots_k = jnp.concatenate(
            [slots_of(pairs_of((group - by) % groups))[source] for by in range(groups)], axis=0
        )
    tiles, width = (4, 512) if groups == 1 else (8, 256)
    by_tile = ids.reshape(tiles, width // 64)
    full = jnp.asarray((by_tile[:, 0] + 1) // 4, jnp.int32)
    total = jnp.asarray(by_tile[:, -1] // 4 + 1, jnp.int32)
    every = np.arange(chunks)[:, None]
    begin = (total[None, :] <= every).sum(axis=1).astype(jnp.int32)
    clear = (full[None, :] <= every).sum(axis=1).astype(jnp.int32)
    qblock = jnp.asarray(ids.repeat(64).reshape(tiles, 1, width), jnp.int32)
    if groups == 1:
        full, total, begin, clear = [
            jnp.asarray(a, jnp.int32)
            for a in (
                (by_tile[:, 0] + 1) // 4,
                by_tile[:, -1] // 4 + 1,
                (by_tile[None, :, -1] // 4 + 1 <= every).sum(axis=1),
                ((by_tile[None, :, 0] + 1) // 4 <= every).sum(axis=1),
            )
        ]

    any_spec = pl.BlockSpec(memory_space=pl.ANY)
    vmem_spec = pl.BlockSpec(memory_space=pltpu.VMEM)
    x = stream_in.reshape(dev_rows, model)
    g_rows = cotangent.reshape(dev_rows, model)
    last = model // 128 - 1

    def columns(more):
        def at(i, spot):
            return (0, jnp.minimum(spot[3] * HD // 128 + more, last))

        return pl.BlockSpec((half, 128), at)

    def whole(shape):
        return pl.BlockSpec(shape, lambda i, spot: (0,) * len(shape))

    part = query_scale.shape[0]
    def gates(arrays, after):
        return call(
            lambda *refs: None,
            [(a.shape, a.dtype) for a in arrays],
            arrays,
            specs=[any_spec] * len(arrays),
            out_specs=[any_spec] * len(arrays),
            after=after,
            aliases={at: at for at in range(len(arrays))},
            name="gate",
        mib=1,
        us=0.1,
        )

    def gate(a, after):
        return gates([a], after)[0]

    steps = [(x,), ring_step(x, x)]
    for step in range(2, 5):
        up, down = steps[-1]
        if step == 4:
            up, down = up[: dev_rows // 2], down[dev_rows // 2 :]
        steps.append(ring_step(up, down))
    early = quarter // 5 * 2
    out_xs = [swap_x(lax.dynamic_slice_in_dim(w_output, k * quarter, early, 0))]
    (slab,) = call(
        slab_body,
        [((3 * HD + 16, half), BF)],
        [
            spot,
            *[w for w in (w_query, w_key, w_value) for _ in range(2)],
            gain_attn,
            gain_mlp,
            query_scale,
        ],
        specs=[columns(0), columns(1)] * 3
        + [pl.BlockSpec((n,), lambda i, spot: (0,)) for n in (half, half, part)],
        out_specs=[whole((3 * HD + 16, half))],
        scratch=[pltpu.VMEM((256, half), F32)],
        smem=1,
        grid=(1,),
        name="slab",
        us=3,
        mib=60,
    )
    slab_x = swap_x(slab)
    late = lax.dynamic_slice_in_dim(w_output, k * quarter + early, quarter - early, 0)
    out_xs.append(swap_x(gate(late, [slab_x])))
    weight_t, gains, scale_col, scale_row = call(
        setup_body,
        [((3 * HD, model), BF), ((8, model), F32), ((HD, 1), F32), ((8, 128), F32)],
        [spot, slab, slab_x],
        smem=1,
        after=[*steps[2], *out_xs[:1]],
        name="setup",
        mib=6,
        us=2,
    )
    weight_sib = swap_core(weight_t)

    norms = None
    sibs, queries, keys, others = [], [], [], []
    norms = None
    slot = 0
    for step, arrays in enumerate(([x, *steps[1], *steps[2]], steps[3], steps[4])):
        count = sum(a.shape[0] for a in arrays) // dev_rows
        moved = (w_hidden, w_return) if step == 2 else ()
        previous = sibs[-1:]
        outs = [
            ((CHIPS, dev_rows, model), BF),
            ((count, HD, 128), BF),
            ((count + sum(p.shape[0] for p in previous), 2 * HD, 128), BF),
            ((count, 3 * HD, 128), BF),
        ]
        outs += [((quarter, model), BF)] * len(moved)
        ins = [spot, *arrays, gains, weight_t, weight_sib, scale_col, *previous, *moved]
        ins += [norms] if step else []
        norms, q_part, kv_part, sib_part, *moved_parts = call(
            functools.partial(
                project_body, (len(arrays), count, bool(previous), len(moved), slot)
            ),
            outs,
            ins,
            specs=[vmem_spec] * (len(arrays) + 4 + len(previous))
            + [any_spec] * (len(moved) + bool(step)),
            out_specs=[any_spec] + [vmem_spec] * (len(outs) - 1),
            scratch=[
                pltpu.VMEM((count, dev_rows, model), BF),
                pltpu.SemaphoreType.DMA((max(1, len(moved)),)),
                pltpu.SemaphoreType.DMA,
            ],
            smem=1,
            after=[(), out_xs[1:], others[:1]][step],
            aliases={len(ins) - 1: 0} if step else None,
            name="project",
            us=[3, 2, 2, 2][step],
            mib=16,
        )
        slot += count
        queries.append(q_part)
        keys.append(kv_part)
        sibs.append(swap_core(sib_part))
        others.append(swap_x(kv_part))
    hid_part, ret_part = moved_parts
    others.append(swap_x(sibs[-1]))
    norms_sib = swap_core(norms)
    parts = [w_output]
    for out_x in out_xs:
        out_x = gate(out_x, [norms])
        parts += [out_x, swap_core(out_x)]
    hid_x = swap_x(gate(hid_part, others))
    ret_x = swap_x(gate(ret_part, others))

    arrays = queries + sibs + keys + others
    n_steps = len(queries)
    places = []
    own_entries, sib_entries = list(OWN_ENTRIES), list(SIB_ENTRIES)
    at = 0
    for step in range(n_steps):
        count = queries[step].shape[0]
        for j in range(count):
            own, sib = own_entries[at + j], sib_entries[at + j]
            places.append(("q", step, j, 0, own, 0))
            places.append(("q", n_steps + step, j, 0, sib, 0))
            places.append(("kv", 2 * n_steps + step, j, 0, own, 0))
            places.append(("kv", 3 * n_steps + step, j, 0, own, 1))
            if step + 1 < n_steps:
                index = queries[step + 1].shape[0] + j
                places.append(("kv", 2 * n_steps + step + 1, index, 0, sib, 0))
                places.append(("kv", 3 * n_steps + step + 1, index, 0, sib, 1))
            else:
                places.append(("kv", n_steps + step, j, HD, sib, 0))
                places.append(("kv", 4 * n_steps, j, HD, sib, 1))
        at += count
    if groups > 1:
        mine = [*keys, sibs[-1][:, HD:]]
        theirs = [*others[:-1], others[-1][:, HD:]]
        order = []
        at = 0
        for step in range(n_steps + 1):
            count = queries[step].shape[0] if step < n_steps else 0
            order += own_entries[at : at + count]
            if step:
                before = queries[step - 1].shape[0]
                order += sib_entries[at - before : at]
            at += count
        for by in range(1, groups):
            for side, parts_of in enumerate((mine, theirs)):
                which = len(arrays)
                arrays.append(turn_groups(jnp.concatenate(parts_of, axis=0), by))
                for j in range(GROUP):
                    places.append(("kv", which, j, 0, by * GROUP + order[j], side))
    pieces, q_t, k_t, k_rows, v_rows, att, lse = call(
        functools.partial(forward_body, {"arrays": len(arrays), "blocks": places}, chunks),
        [
            ((GROUP, HD, 128), BF),
            ((tiles, HD, width), BF),
            ((chunks, HD, 512), BF),
            ((chunks, 512, HD), BF),
            ((chunks, 512, HD), BF),
            ((tiles, HD, width), F32),
            ((tiles, 1, width), F32),
        ],
        [slots_q, slots_k, slots_out, full, total, qblock, *arrays],
        scratch=[
            pltpu.VMEM((2 * GROUP, HD, 64), BF),
            pltpu.VMEM((2, blocks, 2 * HD, 64), BF),
            pltpu.VMEM((chunks, HD + 16, 512), BF),
            pltpu.VMEM((chunks, 512, width), F32),
            pltpu.VMEM((2 * GROUP, HD, 64), BF),
        ],
        smem=5,
        name="attention_forward",
        us=20,
        mib=36 if groups == 1 else 60,
    )
    att_t = exchange(pieces).reshape(model, dev_rows)
    for first, w, when in ((hid_x, w_hidden, pieces), (ret_x, w_return, att_t)):
        first = gate(first, [when])
        parts += [w, first, swap_core(first)]

    g_sib = swap_core(g_rows)
    g_x = swap_x(gate(g_rows, [pieces]))

    share_rows = 3 * quarter + 2 * (model // 128) * dev_rows
    stream, dy, datt_t, f_own, f_sib, f_x, f_xs, sums = call(
        rows_body,
        [
            ((dev_rows, model), BF),
            ((dev_rows, model), F32),
            ((model, dev_rows), BF),
            ((share_rows, 128), BF),
            ((share_rows, 128), BF),
            ((share_rows, 128), BF),
            ((3 * quarter, 128), BF),
            ((8, 128), F32),
        ],
        [spot, att_t, x, g_rows, gains, *parts],
        specs=[vmem_spec] * 4 + [any_spec] * 11,
        scratch=[pltpu.VMEM((model, model), BF)] * 3
        + [pltpu.VMEM((3, model, dev_rows), BF), pltpu.SemaphoreType.DMA((3, 5))],
        smem=1,
        name="row_part",
        mib=60,
        us=10,
    )
    datt_t, g_sib, g_x = gates([datt_t, g_sib, g_x], ())
    grads = exchange(datt_t.reshape(GROUP, HD, dev_rows))
    g_xs, sums_x = swap_core(g_x), swap_x(sums)

    from_x = swap_x(f_x)
    from_sib = swap_core(f_sib)
    forward = swap_core(f_xs)
    from_xs = swap_x(forward)

    def chunk_call(body, shifts, ins, outs, name, after):
        def at(shift):
            return pl.BlockSpec((1, 128, model), lambda i, spot: ((spot[2] + shift) % CHIPS, 0, 0))

        return call(
            body,
            outs,
            [spot, *([partial] * len(shifts)), *ins],
            specs=[at(s) for s in shifts] + [whole(a.shape) for a in ins],
            out_specs=[whole(shape) for shape, _ in outs],
            smem=1,
            grid=(1,),
            after=after,
            name=name,
            us=2.8,
            mib=8,
        )

    def reduce_step(step, received, after):
        shift = 4 - step
        up, down = chunk_call(
            functools.partial(reduce_step_body, step),
            (shift, CHIPS - shift),
            received,
            [((128, model if step else model // 2), BF)] * 2,
            "reduce_step",
            after,
        )
        return (ring(up, 1), ring(down, -1)), [up]

    low = chunks // 4

    def backward(first, size, outs, ins, scratch, after, us):
        return call(
            functools.partial(backward_body, first, not first, low if first else 0),
            [((size, 2 * HD, 256), F32), ((size, 2 * HD, 256), BF), *outs],
            [slots_out, begin, clear, qblock, scale_col, *ins],
            scratch=[*scratch, pltpu.VMEM((2 * GROUP, HD, 64), BF)],
            smem=3,
            after=after,
            name="attention_backward",
            us=us,
            mib=60,
        )

    state = [((tiles, HD, width), BF), ((tiles, 1, width), F32), ((tiles, HD, width), F32)]
    ins = [q_t, k_t, k_rows, v_rows]
    own_high, other_high, grad_t, delta, dq = backward(
        True, chunks - low, state, [grads, *ins, att, lse], [], [forward], 16
    )
    high_x = swap_x(other_high)
    from_x, from_sib, from_xs, g_xs, sums_x = gates(
        [from_x, from_sib, from_xs, g_xs, sums_x], [own_high]
    )
    back_xs = swap_core(from_x)
    (partial,) = call(
        pooled_grad_body,
        [((CHIPS, 128, model), BF)],
        [f_own, from_sib, from_x, from_xs, back_xs, g_rows, g_sib, g_x, g_xs],
        name="pooled_grads",
        us=2,
        mib=24,
    )
    received, done = reduce_step(0, (), ())
    own_low, other_low, dq_pieces, scale_sum = backward(
        False,
        low,
        [((GROUP, HD, 128), BF), ((HD, width), F32)],
        [grad_t, *ins, delta, lse, dq],
        [pltpu.VMEM((tiles, HD, width), F32)],
        done,
        10,
    )
    low_x = swap_x(other_low)
    owns, receiveds = [own_low, own_high], [low_x, high_x]

    received, done = reduce_step(1, received, [dq_pieces, high_x])
    if groups > 1:
        for at in range(2):
            owns[at] = sum_groups(owns[at] + receiveds[at].astype(F32), BF)
            receiveds[at] = jnp.zeros_like(receiveds[at])
    (d_pieces,) = call(
        join_body,
        [((GROUP, 3 * HD, 128), BF)],
        [slots_ctx, dq_pieces, *owns, *receiveds],
        scratch=[pltpu.VMEM((blocks, 2 * HD, 64), BF)],
        smem=1,
        after=received,
        name="join",
        us=2,
        mib=24 if groups == 1 else 60,
    )
    back = exchange(d_pieces)
    received, done = reduce_step(2, received, [d_pieces])
    own_share, other_share = call(
        qkv_grad_body,
        [((3 * HD + 16, half), F32), ((3 * HD + 16, half), BF)],
        [source, spot, d_pieces, scale_sum, norms, norms_sib],
        scratch=[pltpu.VMEM((3 * HD, model), F32)],
        smem=2,
        after=done,
        name="qkv_grads",
        us=4.7,
        mib=24,
    )
    share_x = swap_x(other_share)
    (share,) = call(
        qkv_sum_body,
        [((3 * HD + 16, half), BF)],
        [own_share, share_x, slab],
        name="qkv_sum",
        us=1,
        mib=8,
    )
    share = sum_groups(share.astype(F32), BF).astype(BF) if groups > 1 else share

    def handed(arrays, after=()):
        rows = sum(a.shape[0] * (a.shape[1] // half) for a in arrays)
        (packed,) = call(
            pack_body, [((rows, half), BF)], arrays, after=after, name="pack", us=1, mib=8
        )
        return swap_core(packed)

    q_now, q_sib = ring_step(share, share), swap_core(share)
    received, done = reduce_step(3, received, [share])
    back = gate(back, received)
    back_x = swap_x(back)
    (mine,) = chunk_call(
        reduce_end_body, (0,), (*received, sums, sums_x), [((128, model), BF)], "reduce_end", q_now
    )
    mine = sum_groups(mine.astype(F32), BF).astype(BF) if groups > 1 else mine
    sibs = [handed([*q_now, mine])]
    q_own, m_own = [share, *q_now], [mine]
    q_now, m_now = ring_step(*q_now), ring_step(mine, mine)
    product, product_other = call(
        inputs_product_body,
        [((half, dev_rows), F32), ((half, dev_rows), BF)],
        [back, back_x, w_query, w_key, w_value],
        scratch=[pltpu.VMEM((3, model, 2 * dev_rows), BF)],
        after=[mine],
        name="inputs_product",
        us=3,
        mib=24,
    )
    product_x = swap_x(product_other)
    for step in (2, 3, 4):
        waits = {2: [product], 3: [product_x], 4: ()}[step]
        sibs.append(handed([*q_now, *m_now], waits))
        q_own += q_now
        m_own += m_now
        if step == 2:
            q_now, m_now = ring_step(*q_now), ring_step(*m_now)
        elif step == 3:
            q_now, m_now = ring_step(q_now[0][:128], q_now[1][128:]), ring_step(*m_now)
            (d_in,) = call(
                inputs_grad_body,
                [((dev_rows, model), BF)],
                [spot, x, dy, gains, product, product_x],
                smem=1,
                after=sibs[-1:],
                name="inputs_grad",
                us=2,
                mib=16,
            )
        else:
            m_now = ring_step(m_now[0][:, : model // 2], m_now[1][:, model // 2 :])

    q_arrays = [*q_own, q_sib, *sibs]
    q_blocks = [(entry, [(at, 0, 256)]) for at, entry in enumerate(OWN_ENTRIES[:7])]
    q_blocks.append((OWN_ENTRIES[7], [(7, 0, 128), (8, 0, 128)]))
    q_blocks.append((SIB_ENTRIES[0], [(9, 0, 256)]))
    q_blocks += [
        (entry, [(10 + at // 2, at % 2 * 256, 256)]) for at, entry in enumerate(SIB_ENTRIES[1:])
    ]
    grad_query, grad_key, grad_value, gain_one_grad, scale_grad = call(
        functools.partial(qkv_place_body, (len(q_arrays), q_blocks)),
        [((half, model), F32)] * 3 + [((half,), F32), ((part,), F32)],
        [source, spot, *q_arrays, gain_attn, scale_row],
        scratch=[pltpu.VMEM((3, model, half), BF)],
        smem=2,
        after=[d_in],
        name="qkv_place",
        us=6,
        mib=40,
    )
    m_now = gates(m_now, [grad_query])
    m_own += m_now
    m_arrays = [*m_own, *sibs, *swap_cores(m_now)]
    m_blocks = [(entry, [(at, 0)]) for at, entry in enumerate(OWN_ENTRIES[:7])]
    m_blocks.append((OWN_ENTRIES[7], [(7, 0), (8, 0)]))
    first = len(m_own)
    starts = [(0, 512), (1, 512), (1, 768), (2, 512), (2, 768), (3, 256), (3, 512)]
    m_blocks += [
        (entry, [(first + at, row), (first + at, row + 128)])
        for entry, (at, row) in zip(SIB_ENTRIES, starts)
    ]
    m_blocks.append((SIB_ENTRIES[7], [(first + 4, 0), (first + 5, 0)]))
    elements = float(ctx_count * 2 * dev_rows * model)
    grad_output, grad_hidden, grad_return, gain_two_grad, root_means = call(
        functools.partial(rows_place_body, (len(m_arrays), m_blocks), elements),
        [((half, model), F32)] * 3 + [((half,), F32), ((2,), F32)],
        [place, *m_arrays, w_hidden, gain_mlp],
        smem=1,
        name="rows_place",
        us=5,
        mib=40,
    )
    return (
        stream.reshape(stream_in.shape),
        d_in.reshape(stream_in.shape),
        grad_query,
        grad_key,
        grad_value,
        grad_output,
        grad_hidden,
        grad_return,
        gain_one_grad,
        gain_two_grad,
        scale_grad,
        root_means,
    )


def solution(mesh):
    rows = P(None, ("ctx", "fsdp"), None)
    weight, vector = P("fsdp", None), P("fsdp")
    return jax.shard_map(
        functools.partial(per_device, mesh.shape["ctx"]),
        mesh=mesh,
        in_specs=(rows, P(), *([weight] * 6), *([vector] * 3), rows),
        out_specs=(rows, rows, *([weight] * 6), *([vector] * 3), P()),
        check_vma=False,
    )
```

```python
import functools

import jax
import jax.numpy as jnp
import numpy as np
from jax import lax
from jax.experimental import pallas as pl
from jax.experimental.pallas import tpu as pltpu
from jax.sharding import PartitionSpec as P

H = 16
HD = 80
EPSILON = 1e-06
LOWEST = -1e30
BF = jnp.bfloat16
F32 = jnp.float32
MIB = 1024 * 1024
FLOPS_A_US = 1.15e9

GROUP = 16
CHIPS = 8
RING = (0, 2, 4, 6, 7, 5, 3, 1)
ORDER = (
    ((0, 0), (0, 1))
    + tuple((off, core) for s in (1, 2, 3) for core in (0, 1) for off in (-s, s))
    + ((4, 0), (4, 1))
)
SOURCE = [
    [RING[(RING.index(h // 2) + off) % CHIPS] * 2 + ((h % 2) ^ core) for off, core in ORDER]
    for h in range(GROUP)
]
PLACE = [
    [((h % 2) ^ core) * CHIPS + (RING.index(h // 2) + off) % CHIPS for off, core in ORDER]
    for h in range(GROUP)
]

OWN_ENTRIES = (0, 2, 3, 6, 7, 10, 11, 14)
SIB_ENTRIES = (1, 4, 5, 8, 9, 12, 13, 15)

NN = (((1,), (0,)), ((), ()))
NT = (((1,), (1,)), ((), ()))
TN = (((0,), (0,)), ((), ()))


def dot(a, b, dims):
    return lax.dot_general(a, b, dims, preferred_element_type=F32)


def call(body, outs, ins, scratch=(), specs=None, out_specs=None, name=None, smem=0, after=(), grid=None, aliases=None, us=1.0, mib=24):
    given = len(ins)
    waits = len(after)

    def run(*refs):
        body(*refs[:given], *refs[given + waits :])

    if specs is None:
        specs = [pl.BlockSpec(memory_space=pltpu.VMEM)] * (given - smem)
    specs = list(specs) + [pl.BlockSpec(memory_space=pl.ANY)] * waits
    out_specs = out_specs or [pl.BlockSpec(memory_space=pltpu.VMEM)] * len(outs)
    if grid is None:
        how = dict(
            in_specs=[pl.BlockSpec(memory_space=pltpu.SMEM)] * smem + specs,
            out_specs=out_specs,
            scratch_shapes=list(scratch),
        )
    else:
        how = dict(
            grid_spec=pltpu.PrefetchScalarGridSpec(
                num_scalar_prefetch=smem,
                grid=grid,
                in_specs=specs,
                out_specs=out_specs,
                scratch_shapes=list(scratch),
            )
        )
    return pl.pallas_call(
        run,
        out_shape=[jax.ShapeDtypeStruct(shape, kind) for shape, kind in outs],
        compiler_params=pltpu.CompilerParams(vmem_limit_bytes=mib * MIB),
        cost_estimate=pl.CostEstimate(flops=int(us * FLOPS_A_US), bytes_accessed=1, transcendentals=0),
        input_output_aliases=aliases or {},
        name=name,
        **how,
    )(*ins, *after)


def start_copies(jobs, sems):
    copies = []
    for at, (source, target) in enumerate(jobs):
        copy = pltpu.make_async_copy(source, target, sems.at[at])
        copy.start()
        copies.append(copy)
    return copies


def slab_body(spot, q0, q1, k0, k1, v0, v1, gain_one, gain_two, scale, out, turned):
    start = spot[3] * HD
    off = pl.multiple_of(start - start // 128 * 128, 16)
    for w, (left, right) in enumerate(((q0, q1), (k0, k1), (v0, v1))):
        turned[:128] = left[...].astype(F32).T
        turned[128:] = right[...].astype(F32).T
        out[w * HD : w * HD + HD] = turned[pl.ds(off, HD)].astype(BF)
    width = out.shape[1]
    part = scale.shape[0]
    line = jnp.concatenate([line_of(scale), jnp.zeros((1, width - part), F32)], axis=1)
    tail = [line_of(gain_one), line_of(gain_two), line, jnp.zeros((13, width), F32)]
    out[3 * HD :] = jnp.concatenate(tail, axis=0).astype(BF)


def line_of(vector):
    return vector[...].astype(F32).reshape(1, vector.shape[0])


def setup_body(spot, slab, slab_x, weight, gains, scale_col, scale_row):
    width = slab.shape[1]
    f = spot[0]
    mine, theirs = slab[...], slab_x[...]
    left = jnp.where(f == 0, mine, theirs)
    right = jnp.where(f == 0, theirs, mine)
    weight[:, :width] = left[: 3 * HD]
    weight[:, width:] = right[: 3 * HD]
    left, right = left[3 * HD :].astype(F32), right[3 * HD :].astype(F32)
    gains[...] = jnp.concatenate([left[:8], right[:8]], axis=1)
    part = HD // 2
    row = jnp.concatenate([left[2:3, :part], right[2:3, :part], jnp.zeros((1, 128 - HD), F32)], axis=1)
    row = jnp.broadcast_to(row, (128, 128))
    scale_row[...] = row[:8]
    scale_col[...] = row.T[:HD, :1] * HD ** (-0.5)


def project_body(layout, spot, *refs):
    count, pieces, carried, slot = layout
    xs, refs = refs[:count], refs[count:]
    (gains, weight, weight_sib, scale), refs = refs[:4], refs[4:]
    moved, refs = refs[:carried], refs[carried:]
    refs = refs if slot == 0 else refs[1:]
    (norm_out, q_out, kv_out, near_out, far_out), refs = refs[:5], refs[5:]
    outs, (norm_vmem, sems, norm_sem) = refs[:-3], refs[-3:]
    copies = []
    for w, out in zip(moved, outs):
        size = out.shape[0]
        rows = pl.ds(pl.multiple_of(spot[1] * size, 16), size)
        copies.append((w.at[rows], out))
    copies = start_copies(copies, sems)
    x = jnp.concatenate([r[...] for r in xs], axis=0).astype(F32)
    inv = lax.rsqrt(jnp.mean(x * x, axis=-1, keepdims=True) + EPSILON)
    norm = (x * inv * gains[0:1]).astype(BF)
    norm_vmem[...] = norm.reshape(norm_vmem.shape)
    keep = pltpu.make_async_copy(norm_vmem, norm_out.at[pl.ds(slot, pieces)], norm_sem)
    keep.start()
    for table, other in ((weight, False), (weight_sib, True)):
        out = dot(table[...], norm, NT)
        q = (out[:HD] * scale[...]).astype(BF)
        kv = out[HD:].astype(BF)
        for j in range(pieces):
            lanes = slice(j * 128, (j + 1) * 128)
            if other:
                near_out[j, :HD] = q[:, lanes]
                near_out[j, HD:] = kv[:, lanes]
                far_out[j] = kv[:, lanes]
            else:
                q_out[j] = q[:, lanes]
                kv_out[j] = kv[:, lanes]
    for copy in copies:
        copy.wait()
    keep.wait()


def forward_body(layout, chunks, slots_q, slots_k, slots_out, full, total, qblock, *refs):
    count = layout["arrays"]
    arrays, refs = refs[:count], refs[count:]
    (pieces, q_t, k_t, k_rows, v_rows, att, lse), refs = refs[:7], refs[7:]
    block_q, block_kv, v_t, scores, block_out = refs
    for kind, which, index, entry, side in layout["blocks"]:
        for half in range(2):
            lanes = slice(half * 64, half * 64 + 64)
            if kind == "q":
                block_q[slots_q[entry, half]] = arrays[which][index, :HD, lanes]
            else:
                value = arrays[which][index, :, lanes]
                block_kv[side, slots_k[entry, half]] = value[value.shape[0] - 2 * HD :]
    rows = 2 * 256
    ones_row = jnp.where(lax.broadcasted_iota(jnp.int32, (16, rows), 0) == 0, 1.0, 0.0).astype(BF)

    @pl.loop(0, chunks)
    def _(c):
        tile = jnp.concatenate(
            [block_kv[side, 4 * c + m] for side in range(2) for m in range(4)], axis=1
        )
        k_t[c] = tile[:HD]
        k_rows[c] = tile[:HD].astype(F32).T.astype(BF)
        v_rows[c] = tile[HD:].astype(F32).T.astype(BF)
        v_t[c] = jnp.concatenate([tile[HD:], ones_row], axis=0)

    width = q_t.shape[2]
    per = width // 64

    @pl.loop(0, q_t.shape[0])
    def _(i):
        query = jnp.concatenate([block_q[per * i + m] for m in range(per)], axis=1)
        q_t[i] = query
        ids = qblock[i]

        def scan_max(masked, c, top):
            s = dot(k_rows[c], query, NN)
            if masked:
                s = jnp.where(block_of_row(width) + 4 * c <= ids, s, LOWEST)
            scores[c] = s
            return jnp.maximum(top, jnp.max(s.reshape(rows // 8, 8, width), axis=0))

        top = jnp.full((8, width), LOWEST, F32)
        top = lax.fori_loop(0, full[i], functools.partial(scan_max, False), top)
        top = lax.fori_loop(full[i], total[i], functools.partial(scan_max, True), top)
        top = jnp.max(top, axis=0, keepdims=True)

        def gather(c, acc):
            w = jnp.exp(scores[c] - top).astype(BF)
            return acc + dot(v_t[c], w, NN)

        acc = lax.fori_loop(0, total[i], gather, jnp.zeros((HD + 16, width), F32))
        sums = acc[HD : HD + 1]
        out = acc[:HD] / sums
        att[i] = out
        lse[i] = top + jnp.log(sums)
        low = out.astype(BF)
        for m in range(per):
            block_out[per * i + m] = low[:, m * 64 : m * 64 + 64]

    for c in range(GROUP):
        pieces[c] = jnp.concatenate(
            [block_out[slots_out[c, 0]], block_out[slots_out[c, 1]]], axis=1
        )


def block_of_row(width):
    return lax.broadcasted_iota(jnp.int32, (512, width), 0) % 256 // 64


def backward_body(first, last, low, slots_out, begin, clear, qblock, scale, *refs):
    (given, q_t, stat, lse), refs = refs[:4], refs[4:]
    if not first:
        dq_in, refs = refs[0], refs[1:]
    sources, (dkv_own, dkv_other), refs = refs[:3], refs[3:5], refs[5:]
    (k_t, k_rows, v_rows, sems), refs = refs[-4:], refs[:-4]
    size = dkv_own.shape[0]
    copies = start_copies(
        [(a.at[pl.ds(low, size)], o) for a, o in zip(sources, (k_t, k_rows, v_rows))], sems
    )
    tiles, _, width = q_t.shape
    per = width // 64
    if first:
        (grad_t, delta_out, dq), refs = refs[:3], refs[3:]
        (blocks,) = refs
        for c in range(GROUP):
            for half in range(2):
                blocks[slots_out[c, half]] = given[c, :, half * 64 : half * 64 + 64]

        @pl.loop(0, tiles)
        def _(i):
            grad = jnp.concatenate([blocks[per * i + m] for m in range(per)], axis=1)
            grad_t[i] = grad
            delta_out[i] = jnp.sum(grad.astype(F32) * stat[i], axis=0, keepdims=True)
            dq[i] = jnp.zeros((HD, width), F32)

        delta = delta_out
    else:
        grad_t, delta = given, stat
        if last:
            (dq_pieces, scale_sum, dq, blocks) = refs
        else:
            (dq,) = refs
        dq[...] = dq_in[...]

    for copy in copies:
        copy.wait()

    @pl.loop(0, size)
    def _(at):
        c = low + at

        def step(masked, i, carry):
            d_k, d_v = carry
            query, grad = q_t[i], grad_t[i]
            prob = jnp.exp(dot(k_rows[at], query, NN) - lse[i])
            if masked:
                prob = jnp.where(block_of_row(width) + 4 * c <= qblock[i], prob, 0.0)
            d_score = (prob * (dot(v_rows[at], grad, NN) - delta[i])).astype(BF)
            dq[i] += dot(k_t[at], d_score, NN)
            return d_k + dot(query, d_score, NT), d_v + dot(grad, prob.astype(BF), NT)

        carry = (jnp.zeros((HD, 512), F32), jnp.zeros((HD, 512), F32))
        carry = lax.fori_loop(begin[c], clear[c], functools.partial(step, True), carry)
        d_k, d_v = lax.fori_loop(clear[c], tiles, functools.partial(step, False), carry)
        dkv_own[at, :HD] = d_k[:, :256]
        dkv_own[at, HD:] = d_v[:, :256]
        dkv_other[at, :HD] = d_k[:, 256:].astype(BF)
        dkv_other[at, HD:] = d_v[:, 256:].astype(BF)

    if last:
        total = jnp.zeros((HD, width), F32)
        for i in range(tiles):
            total = total + dq[i] * q_t[i].astype(F32)
            rounded = (dq[i] * scale[...]).astype(BF)
            for m in range(per):
                blocks[per * i + m] = rounded[:, m * 64 : m * 64 + 64]
        scale_sum[...] = total
        for c in range(GROUP):
            dq_pieces[c] = jnp.concatenate(
                [blocks[slots_out[c, 0]], blocks[slots_out[c, 1]]], axis=1
            )


def join_body(slots_kv, spot, dq_pieces, *refs):
    parts, (pieces, other, blocks) = refs[:-3], refs[-3:]
    low = 0
    for own, received in zip(parts[: len(parts) // 2], parts[len(parts) // 2 :]):

        @pl.loop(0, own.shape[0])
        def _(at, low=low, own=own, received=received):
            tile = (own[at] + received[at].astype(F32)).astype(BF)
            for m in range(4):
                blocks[4 * (low + at) + m] = tile[:, m * 64 : m * 64 + 64]

        low += own.shape[0]

    for p in range(CHIPS):
        for core in range(2):
            c = RING[p] * 2 + core
            pieces[2 * p + core, :HD] = dq_pieces[c]
            pieces[2 * p + core, HD:] = jnp.concatenate(
                [blocks[slots_kv[c, 0]], blocks[slots_kv[c, 1]]], axis=1
            )
    sign = 1 - 2 * spot[1]
    for j in range(5):
        pos = lax.rem(spot[2] + CHIPS - sign * j, CHIPS)
        for core in range(2):
            other[2 * j + core] = pieces[2 * pos + core]


def products_body(spot, pieces, near, weight, weight_sib, out):
    sign = 1 - 2 * spot[1]
    for j in range(5):
        pos = lax.rem(spot[2] + CHIPS + sign * j, CHIPS)
        for core in range(2):
            total = dot(pieces[2 * pos + core], weight[...], TN)
            total = total + dot(near[2 * j + core], weight_sib[...], TN)
            out[j, core * 128 : core * 128 + 128] = total.astype(BF)


def qkv_grad_body(place, spot, pieces, scale_sum, *refs):
    norms, (own, other, table) = refs[:-3], refs[-3:]
    total = jnp.zeros((3 * HD, table.shape[1]), F32)
    for norm, entries in zip(norms, (OWN_ENTRIES, SIB_ENTRIES)):
        for j, entry in enumerate(entries):
            at = 2 * lax.rem(place[entry], CHIPS) + place[entry] // CHIPS
            total = total + dot(pieces[at], norm[j], NN)
    table[...] = total
    width = table.shape[1] // 2
    f = spot[0]
    own[: 3 * HD] = table[:, pl.ds(pl.multiple_of(f * width, 128), width)]
    other[: 3 * HD] = table[:, pl.ds(pl.multiple_of((1 - f) * width, 128), width)].astype(BF)
    column = jnp.broadcast_to(jnp.sum(scale_sum[...], axis=1, keepdims=True), (HD, 128))
    line = column.T[:1]
    high = line.astype(BF)
    low = (line - high.astype(F32)).astype(BF)
    own[3 * HD :] = jnp.zeros((16, width), F32)
    own[3 * HD : 3 * HD + 1, :HD] = line
    tail = jnp.concatenate([high.astype(F32), low.astype(F32), jnp.zeros((14, HD), F32)], axis=0)
    other[3 * HD :] = jnp.concatenate([tail, jnp.zeros((16, width - HD), F32)], axis=1).astype(BF)


def qkv_sum_body(own, received, slab, out):
    width = own.shape[1]
    total = own[: 3 * HD] + received[: 3 * HD].astype(F32)
    out[: 3 * HD] = total.astype(BF)
    gain = jnp.sum(total * slab[: 3 * HD].astype(F32), axis=0, keepdims=True)
    tail = received[3 * HD :].astype(F32)
    line = own[3 * HD : 3 * HD + 1] + tail[0:1] + tail[1:2]
    rows = []
    for value in (gain, line):
        high = value.astype(BF).astype(F32)
        rows += [high, value - high]
    out[3 * HD :] = jnp.concatenate(rows + [jnp.zeros((12, width), F32)], axis=0).astype(BF)


def chip_pack_body(spot, own, near, out):
    rows = own.shape[0]
    out[pl.ds(pl.multiple_of(spot[1] * rows, 16), rows)] = own[...]
    out[pl.ds(pl.multiple_of((1 - spot[1]) * rows, 16), rows)] = near[...]


def ring_positions(spot):
    sign = 1 - 2 * spot[1]
    offsets = [0] + [-sign * s for s in (1, 2, 3)] + [sign * s for s in (1, 2, 3)] + [4]
    return [lax.rem(spot[2] + CHIPS + off, CHIPS) for off in offsets]


def qkv_place_body(spot, *refs):
    arrays, (gain, scale_row), refs = refs[:9], refs[9:11], refs[11:]
    outs, (gain_out, scale_out, table) = refs[:3], refs[3:]
    width = gain.shape[0]
    size = 3 * HD + 16
    tail = jnp.zeros((16, width), F32)
    positions = ring_positions(spot)
    blocks = [(arrays[at], c * size, positions[at], c) for at in range(7) for c in range(2)]
    blocks += [(arrays[7], 0, positions[7], spot[1]), (arrays[8], 0, positions[7], 1 - spot[1])]
    for ref, row, pos, core in blocks:
        chip = jnp.where(pos < 4, 2 * pos, 15 - 2 * pos)
        head = pl.multiple_of((2 * chip + core) * HD, 16)
        for w in range(3):
            table[w, pl.ds(head, HD)] = ref[row + w * HD : row + w * HD + HD]
        tail = tail + ref[row + 3 * HD : row + size].astype(F32)
    for w in range(3):
        for at in range(0, H * HD, 256):
            outs[w][:, at : at + 256] = table[w, at : at + 256].astype(F32).T
    gain_out[...] = ((tail[0:1] + tail[1:2]) / line_of(gain)).reshape(width)
    scale = (tail[2:3, :128] + tail[3:4, :128]) / scale_row[0:1]
    part = scale_out.shape[0]
    chosen = jnp.where(spot[0] == 0, scale[:, :part], scale[:, part : 2 * part])
    scale_out[...] = chosen.reshape(part)


def rows_body(
    spot,
    att_t,
    x_in,
    g_in,
    gain_in,
    *refs,
):
    weights = (refs[:5], refs[5:8], refs[8:11])
    refs = refs[11:]
    (stream_out, dy_out, datt_out), outs = refs[:3], refs[3:7]
    full = refs[7:10]
    turned, sems = refs[10:]
    f, k = spot[0], spot[1]
    half = weights[0][0].shape[0]
    quarter = half // 2
    early = weights[0][1].shape[0]
    places = [
        [k * quarter, (1 - k) * quarter, k * quarter + early, (1 - k) * quarter + early],
        *[[k * quarter, (1 - k) * quarter]] * 2,
    ]
    copies = []
    for w in range(3):
        mine, *theirs = weights[w]
        jobs = [(mine, full[w].at[pl.ds(pl.multiple_of(f * half, 16), half)])]
        for piece, start in zip(theirs, places[w]):
            rows = pl.ds(pl.multiple_of((1 - f) * half + start, 16), piece.shape[0])
            jobs.append((piece, full[w].at[rows]))
        copies.append(start_copies(jobs, sems.at[w]))
    w_out, w_hid, w_ret = full
    x = x_in[...].astype(F32)
    gain = gain_in[1:2]
    for copy in copies[0]:
        copy.wait()
    attn = dot(att_t[...], w_out[...], TN)
    y1 = x + attn
    inv = lax.rsqrt(jnp.mean(y1 * y1, axis=-1, keepdims=True) + EPSILON)
    unit = y1 * inv
    norm = (unit * gain).astype(BF)
    for copy in copies[1]:
        copy.wait()
    h = dot(norm, w_hid[...], NN)
    sig = jax.nn.sigmoid(h)
    act = (h * sig).astype(BF)
    for copy in copies[2]:
        copy.wait()
    stream = y1 + dot(act, w_ret[...], NN)
    stream_out[...] = stream.astype(BF)
    squares = jnp.where(
        lax.broadcasted_iota(jnp.int32, (8, 128), 0) == 0,
        jnp.sum(stream * stream),
        jnp.sum(attn * attn),
    )
    g = g_in[...]
    d_act = dot(g, w_ret[...], NT)
    d_h = (d_act * sig * (1.0 + h * (1.0 - sig))).astype(BF)
    d_norm = dot(d_h, w_hid[...], NT)
    c2 = d_norm * gain
    dy = inv * (c2 - unit * jnp.mean(c2 * unit, axis=-1, keepdims=True)) + g.astype(F32)
    dy_out[...] = dy
    dy_b = dy.astype(BF)
    datt_out[...] = dot(w_out[...], dy_b, NT).astype(BF)
    turned[0] = att_t[...]
    turned[1] = norm.astype(F32).T.astype(BF)
    turned[2] = act.astype(F32).T.astype(BF)
    rows = x.shape[0]
    columns = x.shape[1] // 128
    chunk = half // CHIPS
    sign = 1 - 2 * k
    for ref, part, way in zip(outs, (f, f, 1 - f, 1 - f), (sign, -sign, sign, -sign)):
        for j in range(5):
            pos = lax.rem(spot[2] + CHIPS + way * j, CHIPS)
            at = pl.multiple_of(part * half + pos * chunk, 16)
            for w in range(3):
                start = (w * 5 + j) * chunk
                ref[start : start + chunk] = turned[w, pl.ds(at, chunk)]
    line = sums_line(squares)
    tail = jnp.concatenate([sums_tail(line, 128), jnp.zeros((8, 128), F32)], axis=0).astype(BF)
    for ref in outs[:3]:
        start = 15 * chunk
        for right in (dy_b, d_h):
            for c in range(columns):
                ref[start : start + rows] = right[:, c * 128 : (c + 1) * 128]
                start += rows
        ref[start : start + 16] = tail


def sums_tail(line, width):
    high = line.astype(BF).astype(F32)
    row = lax.broadcasted_iota(jnp.int32, (8, 128), 0)
    tail = jnp.where(row == 0, high, jnp.where(row == 1, line - high, 0.0))
    return tail if width == 128 else jnp.concatenate([tail, jnp.zeros((8, width - 128), F32)], axis=1)


def sums_line(sums):
    lane = lax.broadcasted_iota(jnp.int32, (1, 128), 1)
    return jnp.where(lane == 0, sums[0:1], jnp.where(lane == 1, sums[1:2], 0.0))


def pooled_grad_body(own, sib, far, far_left, far_right, *refs):
    gs, out = refs[:4], refs[4]
    model = out.shape[2]
    columns = model // 128
    group = far_left.shape[0] // 3
    chunk = group // 5
    rows = 128
    totals = []
    for w in range(3):
        lefts, rights = [], []
        for at, (left, right) in enumerate(
            ((own, own), (sib, sib), (far, far), (far_left, far_right))
        ):
            lefts.append(left[w * group : (w + 1) * group])
            start = 3 * group + w * columns * rows
            if w == 2:
                rights.append(gs[at][...])
                continue
            rights.append(
                jnp.concatenate(
                    [right[start + c * rows : start + (c + 1) * rows] for c in range(columns)], axis=1
                )
            )
        left, right = jnp.concatenate(lefts, axis=1), jnp.concatenate(rights, axis=0)
        totals.append(dot(left, right, NN))
    line = jnp.zeros((1, 128), F32)
    for ref in (own, sib, far, far_right):
        tail = ref[ref.shape[0] - 16 :].astype(F32)
        line = line + tail[0:1] + tail[1:2]
    for j in range(5):
        parts = [t[chunk * j : chunk * (j + 1)] for t in totals]
        tail = jnp.zeros((16, model), F32)
        if j == 0:
            tail = jnp.concatenate([sums_tail(line, model), tail[:8]], axis=0)
        out[j] = jnp.concatenate([*parts, tail], axis=0).astype(BF)


def reduce_step_body(step, spot, block, *refs):
    received, out = refs[:-1], refs[-1]
    half = block.shape[2] // 2
    near = pl.ds(pl.multiple_of(spot[1] * half, 128), half)
    if step == 0:
        out[...] = block[0, :, near]
    elif step == 1:
        out[...] = block[0]
        out[:, near] = (block[0, :, near].astype(F32) + received[0][...].astype(F32)).astype(BF)
    else:
        out[...] = (block[0].astype(F32) + received[0][...].astype(F32)).astype(BF)


def reduce_end_body(spot, block, mine, near, out):
    out[...] = (block[0].astype(F32) + mine[...].astype(F32) + near[...].astype(F32)).astype(BF)


def rows_place_body(elements, spot, *refs):
    arrays, (w_hidden, gain), refs = refs[:9], refs[9:11], refs[11:]
    outs, (gain_out, means_out) = refs[:3], refs[3:]
    chunk = outs[0].shape[0] // CHIPS
    tail = jnp.zeros((8, 128), F32)
    positions = ring_positions(spot)
    for at in range(9):
        block = arrays[at][...].astype(F32)
        rows = pl.ds(pl.multiple_of(positions[min(at, 7)] * chunk, 16), chunk)
        core = spot[1] if at == 7 else 1 - spot[1]
        width = block.shape[1]
        for w in range(3):
            part = block[w * chunk : (w + 1) * chunk]
            if at < 7:
                outs[w][rows] = part
            else:
                outs[w][rows, pl.ds(pl.multiple_of(core * width, 128), width)] = part
        if at < 7:
            tail = tail + block[3 * chunk : 3 * chunk + 8, :128]
        else:
            tail = tail + jnp.where(core == 0, block[3 * chunk : 3 * chunk + 8, :128], 0.0)
    means = jnp.sqrt((tail[0:1, :2] + tail[1:2, :2]) / elements)
    means_out[...] = means.reshape(2)
    half, model = w_hidden.shape
    total = jnp.zeros((half, 128), F32)
    for at in range(0, model, 128):
        total = total + outs[1][:, at : at + 128] * w_hidden[:, at : at + 128].astype(F32)
    line = jnp.sum(total.T, axis=0, keepdims=True) / line_of(gain)
    gain_out[...] = line.reshape(half)


def inputs_grad_body(spot, block, mine, near, x_in, dy_in, gains, out):
    size = out.shape[0]
    rows = pl.ds(pl.multiple_of(spot[1] * size, 16), size)
    d_norm = block[0, rows].astype(F32) + mine[rows].astype(F32) + near[rows].astype(F32)
    x = x_in[...].astype(F32)
    inv = lax.rsqrt(jnp.mean(x * x, axis=-1, keepdims=True) + EPSILON)
    unit = x * inv
    c1 = d_norm * gains[0:1]
    dx = inv * (c1 - unit * jnp.mean(c1 * unit, axis=-1, keepdims=True)) + dy_in[...]
    out[...] = dx.astype(BF)


def per_device(
    ctx_count,
    stream_in,
    pairing,
    w_query,
    w_key,
    w_value,
    w_output,
    w_hidden,
    w_return,
    gain_attn,
    gain_mlp,
    query_scale,
    cotangent,
):
    sequences, dev_rows, model = stream_in.shape
    half = w_query.shape[0]
    quarter = half // 2
    groups = ctx_count // GROUP
    blocks = 2 * ctx_count
    chunks = blocks // 4
    ctx = lax.axis_index("ctx")
    f = lax.axis_index("fsdp")
    head = ctx % GROUP
    k = head % 2

    def ring(a, shift):
        pairs = [
            (
                g * GROUP + RING[i] * 2 + core,
                g * GROUP + RING[(i + shift) % CHIPS] * 2 + core,
            )
            for g in range(groups)
            for i in range(CHIPS)
            for core in range(2)
        ]
        return lax.ppermute(a, "ctx", pairs)

    def ring_by_core(a):
        pairs = [
            (
                g * GROUP + RING[i] * 2 + core,
                g * GROUP + RING[(i + 1 - 2 * core) % CHIPS] * 2 + core,
            )
            for g in range(groups)
            for i in range(CHIPS)
            for core in range(2)
        ]
        return lax.ppermute(a, "ctx", pairs)

    def swap_core(a):
        return lax.ppermute(a, "ctx", [(c, c ^ 1) for c in range(ctx_count)])

    def swap_far(a):
        pairs = [
            (2 * c + side, 2 * (c ^ 1) + 1 - side) for c in range(ctx_count) for side in range(2)
        ]
        return lax.ppermute(a, ("ctx", "fsdp"), pairs)

    def swap_x(a):
        return lax.ppermute(a, "fsdp", [(0, 1), (1, 0)])

    def turn_groups(a, by):
        return lax.ppermute(
            a, "ctx", [(c, (c + by * GROUP) % ctx_count) for c in range(ctx_count)]
        )

    def sum_groups(a, kind):
        total = a
        for by in range(1, groups):
            total = total + turn_groups(a.astype(kind), by).astype(a.dtype)
        return total

    def exchange(a):
        which = (
            None
            if groups == 1
            else [[g * GROUP + h for h in range(GROUP)] for g in range(groups)]
        )
        return lax.all_to_all(a, "ctx", 0, 0, axis_index_groups=which, tiled=True)

    def swap_cores(arrays):
        swapped = []
        for a in arrays:
            swapped.append(swap_core(a))
        return swapped

    def ring_step(up, down):
        return ring(up, 1), ring(down, -1)

    source = jnp.asarray(SOURCE, jnp.int32)[head]
    place = jnp.asarray(PLACE, jnp.int32)[head]
    chip = head // 2
    ring_at = jnp.where(chip % 2 == 0, chip // 2, CHIPS - 1 - chip // 2)
    spot = jnp.stack([f, k, ring_at, head]).astype(jnp.int32)
    group = ctx // GROUP

    def pairs_of(which):
        return lax.dynamic_slice_in_dim(pairing, which * GROUP, GROUP, 0)

    def slots_of(pairs):
        return jnp.stack([pairs, blocks - 1 - pairs], axis=1).astype(jnp.int32)

    my_pairs = pairs_of(group)
    slots_ctx = slots_of(my_pairs)
    slots_ring = slots_ctx[source]
    if groups == 1:
        ids = np.arange(2 * GROUP, dtype=np.int32)
        slots_q, slots_out = slots_ring, slots_ctx
        slots_k = slots_ring
    else:
        flat = slots_ctx.reshape(-1)
        rank = jnp.sum((flat[None, :] < flat[:, None]).astype(jnp.int32), axis=1)
        ids = jnp.sum(
            jnp.where(rank[None, :] == jnp.arange(2 * GROUP)[:, None], flat[None, :], 0), axis=1
        ).astype(jnp.int32)
        slots_out = rank.reshape(GROUP, 2).astype(jnp.int32)
        slots_q = slots_out[source]
        slots_k = jnp.concatenate(
            [slots_of(pairs_of((group - by) % groups))[source] for by in range(groups)], axis=0
        )
    tiles, width = (4, 512) if groups == 1 else (8, 256)
    by_tile = ids.reshape(tiles, width // 64)
    full = jnp.asarray((by_tile[:, 0] + 1) // 4, jnp.int32)
    total = jnp.asarray(by_tile[:, -1] // 4 + 1, jnp.int32)
    every = np.arange(chunks)[:, None]
    begin = (total[None, :] <= every).sum(axis=1).astype(jnp.int32)
    clear = (full[None, :] <= every).sum(axis=1).astype(jnp.int32)
    qblock = jnp.asarray(ids.repeat(64).reshape(tiles, 1, width), jnp.int32)
    if groups == 1:
        full, total, begin, clear = [
            jnp.asarray(a, jnp.int32)
            for a in (
                (by_tile[:, 0] + 1) // 4,
                by_tile[:, -1] // 4 + 1,
                (by_tile[None, :, -1] // 4 + 1 <= every).sum(axis=1),
                ((by_tile[None, :, 0] + 1) // 4 <= every).sum(axis=1),
            )
        ]

    any_spec = pl.BlockSpec(memory_space=pl.ANY)
    vmem_spec = pl.BlockSpec(memory_space=pltpu.VMEM)
    x = stream_in.reshape(dev_rows, model)
    g_rows = cotangent.reshape(dev_rows, model)
    last = model // 128 - 1

    def columns(more):
        def at(i, spot):
            return (0, jnp.minimum(spot[3] * HD // 128 + more, last))

        return pl.BlockSpec((half, 128), at)

    def whole(shape):
        return pl.BlockSpec(shape, lambda i, spot: (0,) * len(shape))

    part = query_scale.shape[0]
    def gates(arrays, after):
        return call(
            lambda *refs: None,
            [(a.shape, a.dtype) for a in arrays],
            arrays,
            specs=[any_spec] * len(arrays),
            out_specs=[any_spec] * len(arrays),
            after=after,
            aliases={at: at for at in range(len(arrays))},
            name="gate",
        mib=1,
        us=0.1,
        )

    def gate(a, after):
        return gates([a], after)[0]

    steps = [(x,), ring_step(x, x)]
    for _ in range(2):
        steps.append(ring_step(*steps[-1]))
    early = quarter // 5 * 2
    out_xs = [swap_x(lax.dynamic_slice_in_dim(w_output, k * quarter, early, 0))]
    (slab,) = call(
        slab_body,
        [((3 * HD + 16, half), BF)],
        [
            spot,
            *[w for w in (w_query, w_key, w_value) for _ in range(2)],
            gain_attn,
            gain_mlp,
            query_scale,
        ],
        specs=[columns(0), columns(1)] * 3
        + [pl.BlockSpec((n,), lambda i, spot: (0,)) for n in (half, half, part)],
        out_specs=[whole((3 * HD + 16, half))],
        scratch=[pltpu.VMEM((256, half), F32)],
        smem=1,
        grid=(1,),
        name="slab",
        us=3,
        mib=60,
    )
    slab_x = swap_x(slab)
    late = lax.dynamic_slice_in_dim(w_output, k * quarter + early, quarter - early, 0)
    out_xs.append(swap_x(gate(late, [slab_x])))
    weight_t, gains, scale_col, scale_row = call(
        setup_body,
        [((3 * HD, model), BF), ((8, model), F32), ((HD, 1), F32), ((8, 128), F32)],
        [spot, slab, slab_x],
        smem=1,
        after=[*steps[2], *out_xs[:1]],
        name="setup",
        mib=6,
        us=2,
    )
    weight_sib = swap_core(weight_t)

    norms = None
    queries, keys, far_keys, near = [], [], [], []
    norms = None
    slot = 0
    for step in range(2):
        if step:
            up, down = gates(steps[3], queries)
            arrays = [up, down, *ring_step(up[: dev_rows // 2], down[dev_rows // 2 :])]
        else:
            arrays = [x, *steps[1], *steps[2]]
        count = sum(a.shape[0] for a in arrays) // dev_rows
        moved = (w_hidden, w_return) if step else ()
        outs = [((CHIPS, dev_rows, model), BF)]
        outs += [((count, HD, 128), BF), ((count, 2 * HD, 128), BF)]
        outs += [((count, 3 * HD, 128), BF), ((count, 2 * HD, 128), BF)]
        outs += [((quarter, model), BF)] * len(moved)
        ins = [spot, *arrays, gains, weight_t, weight_sib, scale_col, *moved]
        ins += [norms] if step else []
        norms, q_part, kv_part, near_part, far_part, *moved_parts = call(
            functools.partial(project_body, (len(arrays), count, len(moved), slot)),
            outs,
            ins,
            specs=[vmem_spec] * (len(arrays) + 4) + [any_spec] * (len(moved) + bool(step)),
            out_specs=[any_spec] + [vmem_spec] * (len(outs) - 1),
            scratch=[
                pltpu.VMEM((count, dev_rows, model), BF),
                pltpu.SemaphoreType.DMA((max(1, len(moved)),)),
                pltpu.SemaphoreType.DMA,
            ],
            smem=1,
            after=[(), out_xs[1:]][step],
            aliases={len(ins) - 1: 0} if step else None,
            name="project",
            us=[3, 3][step],
            mib=60,
        )
        slot += count
        queries.append(q_part)
        keys.append(kv_part)
        far_keys += [swap_x(kv_part), swap_far(far_part)]
        near.append(swap_core(near_part))
    hid_part, ret_part = moved_parts
    norms_sib = swap_core(norms)
    parts = [w_output]
    for out_x in out_xs:
        out_x = gate(out_x, [norms])
        parts += [out_x, swap_core(out_x)]
    hid_x = swap_x(gate(hid_part, far_keys))
    ret_x = swap_x(gate(ret_part, far_keys))

    arrays, places = [], []
    at = 0
    for step, q_part in enumerate(queries):
        mine, theirs = (q_part, keys[step], far_keys[2 * step]), (near[step], far_keys[2 * step + 1])
        count = q_part.shape[0]
        for entries, blocks_of in ((OWN_ENTRIES, mine), (SIB_ENTRIES, theirs)):
            for j in range(count):
                entry = entries[at + j]
                last = len(arrays) + len(blocks_of) - 1
                places.append(("q", len(arrays), j, entry, 0))
                places.append(("kv", last - 1, j, entry, 0))
                places.append(("kv", last, j, entry, 1))
            arrays += blocks_of
        at += count
    if groups > 1:
        order = OWN_ENTRIES + SIB_ENTRIES
        mine = jnp.concatenate([*keys, *[a[:, HD:] for a in near]], axis=0)
        theirs = jnp.concatenate([*far_keys[::2], *far_keys[1::2]], axis=0)
        for by in range(1, groups):
            for side, a in enumerate((mine, theirs)):
                places += [
                    ("kv", len(arrays), j, by * GROUP + order[j], side) for j in range(GROUP)
                ]
                arrays.append(turn_groups(a, by))
    pieces, q_t, k_t, k_rows, v_rows, att, lse = call(
        functools.partial(forward_body, {"arrays": len(arrays), "blocks": places}, chunks),
        [
            ((GROUP, HD, 128), BF),
            ((tiles, HD, width), BF),
            ((chunks, HD, 512), BF),
            ((chunks, 512, HD), BF),
            ((chunks, 512, HD), BF),
            ((tiles, HD, width), F32),
            ((tiles, 1, width), F32),
        ],
        [slots_q, slots_k, slots_out, full, total, qblock, *arrays],
        scratch=[
            pltpu.VMEM((2 * GROUP, HD, 64), BF),
            pltpu.VMEM((2, blocks, 2 * HD, 64), BF),
            pltpu.VMEM((chunks, HD + 16, 512), BF),
            pltpu.VMEM((chunks, 512, width), F32),
            pltpu.VMEM((2 * GROUP, HD, 64), BF),
        ],
        smem=5,
        name="attention_forward",
        us=20,
        mib=36 if groups == 1 else 60,
    )
    att_t = exchange(pieces).reshape(model, dev_rows)
    hid_x, ret_x = gates([hid_x, ret_x], [att_t])
    for w, first in ((w_hidden, hid_x), (w_return, ret_x)):
        parts += [w, first, swap_core(first)]

    g_sib, g_x = swap_core(g_rows), swap_x(gate(g_rows, [pieces]))

    left_rows = 15 * (half // CHIPS)
    share_rows = left_rows + 2 * (model // 128) * dev_rows + 16
    stream, dy, datt_t, f_own, f_sib, f_x, f_xs = call(
        rows_body,
        [
            ((dev_rows, model), BF),
            ((dev_rows, model), F32),
            ((model, dev_rows), BF),
            ((share_rows, 128), BF),
            ((share_rows, 128), BF),
            ((share_rows, 128), BF),
            ((left_rows, 128), BF),
        ],
        [spot, att_t, x, g_rows, gains, *parts],
        specs=[vmem_spec] * 4 + [any_spec] * 11,
        scratch=[pltpu.VMEM((model, model), BF)] * 3
        + [pltpu.VMEM((3, model, dev_rows), BF), pltpu.SemaphoreType.DMA((3, 5))],
        smem=1,
        name="row_part",
        mib=60,
        us=10,
    )
    datt_t, g_x = gates([datt_t, g_x], ())
    grads = exchange(datt_t.reshape(GROUP, HD, dev_rows))
    g_xs = swap_core(g_x)

    from_x = swap_x(f_x)
    forward = swap_core(f_xs)
    from_sib, from_xs = swap_core(f_sib), swap_x(forward)

    def chunk_call(table, body, chunk, ins, outs, name, after):
        return call(
            body,
            outs,
            [spot, table, *ins],
            specs=[pl.BlockSpec((1, 256, model), lambda i, spot: (chunk, 0, 0))]
            + [whole(a.shape) for a in ins],
            out_specs=[whole(shape) for shape, _ in outs],
            smem=1,
            grid=(1,),
            after=after,
            name=name,
            us=2,
            mib=16,
        )

    def reduce_step(table, step, received, after):
        outs = chunk_call(
            table,
            functools.partial(reduce_step_body, step),
            4 - step,
            received,
            [((256, model if step else model // 2), BF)],
            "reduce_step",
            after,
        )
        return [ring_by_core(outs[0])], outs

    cuts = (chunks, chunks // 8, 0)
    state = [((tiles, HD, width), BF), ((tiles, 1, width), F32), ((tiles, HD, width), F32)]
    owns, receiveds = [], []
    handed = [grads, att]
    dq, done = [], [forward]
    for at in range(2):
        low, size = cuts[at + 1], cuts[at] - cuts[at + 1]
        given, stat = handed
        outs = [((size, 2 * HD, 256), F32), ((size, 2 * HD, 256), BF)]
        outs += [((GROUP, HD, 128), BF), ((HD, width), F32)] if at else state
        own, other, *more = call(
            functools.partial(backward_body, at == 0, at == 1, low),
            outs,
            [slots_out, begin, clear, qblock, scale_col]
            + [given, q_t, stat, lse, *dq, k_t, k_rows, v_rows],
            specs=[vmem_spec] * (6 + len(dq)) + [any_spec] * 3,
            scratch=[pltpu.VMEM((tiles, HD, width), F32)] * at
            + [
                pltpu.VMEM((2 * GROUP, HD, 64), BF),
                pltpu.VMEM((size, HD, 512), BF),
                pltpu.VMEM((size, 512, HD), BF),
                pltpu.VMEM((size, 512, HD), BF),
                pltpu.SemaphoreType.DMA((3,)),
            ],
            smem=3,
            after=done,
            name="attention_backward",
            us=[20, 7][at],
            mib=60,
        )
        owns.insert(0, own)
        receiveds.insert(0, swap_x(other))
        if not at:
            *handed, dq_now = more
            dq, done = [dq_now], []
            from_x, from_sib, from_xs, g_xs, norms_sib = gates(
                [from_x, from_sib, from_xs, g_xs, norms_sib], [own]
            )
            back_xs = swap_core(from_x)
    dq_pieces, scale_sum = more
    (partial,) = call(
        pooled_grad_body,
        [((5, 256, model), BF)],
        [f_own, from_sib, from_x, from_xs, back_xs, g_rows, g_sib, g_x, g_xs],
        after=[dq_pieces],
        name="pooled_grads",
        us=3,
        mib=24,
    )
    received, done = reduce_step(partial, 0, (), ())
    if groups > 1:
        for at in range(2):
            owns[at] = sum_groups(owns[at] + receiveds[at].astype(F32), BF)
            receiveds[at] = jnp.zeros_like(receiveds[at])
    d_pieces, d_other = call(
        join_body,
        [((GROUP, 3 * HD, 128), BF), ((10, 3 * HD, 128), BF)],
        [slots_ctx, spot, dq_pieces, *owns, *receiveds],
        scratch=[pltpu.VMEM((blocks, 2 * HD, 64), BF)],
        smem=2,
        after=done,
        name="join",
        us=2,
        mib=24 if groups == 1 else 60,
    )
    d_near = swap_core(d_other)
    own_share, other_share = call(
        qkv_grad_body,
        [((3 * HD + 16, half), F32), ((3 * HD + 16, half), BF)],
        [place, spot, d_pieces, scale_sum, norms, norms_sib],
        scratch=[pltpu.VMEM((3 * HD, model), F32)],
        smem=2,
        name="qkv_grads",
        us=4.7,
        mib=24,
    )
    share_x = swap_x(other_share)
    received, done = reduce_step(partial, 1, received, [own_share])

    (table,) = call(
        products_body,
        [((5, 256, model), BF)],
        [spot, d_pieces, d_near, weight_t, weight_sib],
        smem=1,
        after=done,
        name="products",
        us=4,
        mib=24,
    )
    first, done = reduce_step(table, 0, (), ())
    (share,) = call(
        qkv_sum_body,
        [((3 * HD + 16, half), BF)],
        [own_share, share_x, slab],
        after=done,
        name="qkv_sum",
        us=1,
        mib=8,
    )
    share = sum_groups(share.astype(F32), BF).astype(BF) if groups > 1 else share
    share_near = swap_core(share)
    received, done = reduce_step(partial, 2, received, [share, *first])
    first, done = reduce_step(table, 1, first, done)
    (chip_share,) = call(
        chip_pack_body,
        [((2 * (3 * HD + 16), half), BF)],
        [spot, share, share_near],
        smem=1,
        after=done,
        name="chip_pack",
        us=1,
        mib=8,
    )
    q_steps = [chip_share, ring_by_core(chip_share)]
    received, done = reduce_step(partial, 3, received, [chip_share])
    received_near = swap_core(received[0])
    first, done = reduce_step(table, 2, first, [*done, q_steps[1]])
    (mine,) = chunk_call(
        partial,
        reduce_end_body,
        0,
        (*received, received_near),
        [((256, model), BF)],
        "reduce_end",
        done,
    )
    mine = sum_groups(mine.astype(F32), BF).astype(BF) if groups > 1 else mine
    m_steps = [mine, ring_by_core(mine)]
    q_steps.append(ring_by_core(q_steps[-1]))
    first, done = reduce_step(table, 3, first, [mine, q_steps[2]])
    m_steps.append(ring_by_core(m_steps[-1]))
    q_steps.append(ring_by_core(q_steps[-1]))
    m_steps.append(ring_by_core(m_steps[-1]))
    first_near = swap_core(first[0])
    (d_in,) = chunk_call(
        table,
        inputs_grad_body,
        0,
        (*first, first_near, x, dy, gains),
        [((dev_rows, model), BF)],
        "inputs_grad",
        [m_steps[2], q_steps[3]],
    )

    def last_step(a, axis):
        size = a.shape[axis] // 2
        return ring_by_core(lax.dynamic_slice_in_dim(a, k * size, size, axis))

    q_last, m_last = last_step(q_steps[-1], 0), last_step(m_steps[-1], 1)
    q_near = [swap_core(a) for a in q_steps[1:]]
    m_near = [swap_core(a) for a in m_steps[1:]]
    grad_query, grad_key, grad_value, gain_one_grad, scale_grad = call(
        qkv_place_body,
        [((half, model), F32)] * 3 + [((half,), F32), ((part,), F32)],
        [spot, *q_steps, *q_near, q_last, swap_core(q_last), gain_attn, scale_row],
        scratch=[pltpu.VMEM((3, model, half), BF)],
        smem=1,
        after=[d_in],
        name="qkv_place",
        us=6,
        mib=40,
    )
    (m_last,) = gates([m_last], [grad_query])
    elements = float(ctx_count * 2 * dev_rows * model)
    grad_output, grad_hidden, grad_return, gain_two_grad, root_means = call(
        functools.partial(rows_place_body, elements),
        [((half, model), F32)] * 3 + [((half,), F32), ((2,), F32)],
        [spot, *m_steps, *m_near, m_last, swap_core(m_last), w_hidden, gain_mlp],
        smem=1,
        name="rows_place",
        us=5,
        mib=40,
    )
    return (
        stream.reshape(stream_in.shape),
        d_in.reshape(stream_in.shape),
        grad_query,
        grad_key,
        grad_value,
        grad_output,
        grad_hidden,
        grad_return,
        gain_one_grad,
        gain_two_grad,
        scale_grad,
        root_means,
    )


def solution(mesh):
    rows = P(None, ("ctx", "fsdp"), None)
    weight, vector = P("fsdp", None), P("fsdp")
    return jax.shard_map(
        functools.partial(per_device, mesh.shape["ctx"]),
        mesh=mesh,
        in_specs=(rows, P(), *([weight] * 6), *([vector] * 3), rows),
        out_specs=(rows, rows, *([weight] * 6), *([vector] * 3), P()),
        check_vma=False,
    )
```

```python
import functools

import jax
import jax.numpy as jnp
import numpy as np
from jax import lax
from jax.experimental import pallas as pl
from jax.experimental.pallas import tpu as pltpu
from jax.sharding import PartitionSpec as P

H = 16
HD = 80
EPSILON = 1e-06
LOWEST = -1e30
BF = jnp.bfloat16
F32 = jnp.float32
MIB = 1024 * 1024
FLOPS_A_US = 1.15e9

GROUP = 16
CHIPS = 8
RING = (0, 2, 4, 6, 7, 5, 3, 1)
ORDER = (
    ((0, 0), (0, 1))
    + tuple((off, core) for s in (1, 2, 3) for core in (0, 1) for off in (-s, s))
    + ((4, 0), (4, 1))
)
SOURCE = [
    [RING[(RING.index(h // 2) + off) % CHIPS] * 2 + ((h % 2) ^ core) for off, core in ORDER]
    for h in range(GROUP)
]
PLACE = [
    [((h % 2) ^ core) * CHIPS + (RING.index(h // 2) + off) % CHIPS for off, core in ORDER]
    for h in range(GROUP)
]

OWN_ENTRIES = (0, 2, 3, 6, 7, 10, 11, 14)
SIB_ENTRIES = (1, 4, 5, 8, 9, 12, 13, 15)

NN = (((1,), (0,)), ((), ()))
NT = (((1,), (1,)), ((), ()))
TN = (((0,), (0,)), ((), ()))


def dot(a, b, dims):
    return lax.dot_general(a, b, dims, preferred_element_type=F32)


def call(body, outs, ins, scratch=(), specs=None, out_specs=None, name=None, smem=0, after=(), grid=None, aliases=None, us=1.0, mib=24):
    given = len(ins)
    waits = len(after)

    def run(*refs):
        body(*refs[:given], *refs[given + waits :])

    if specs is None:
        specs = [pl.BlockSpec(memory_space=pltpu.VMEM)] * (given - smem)
    specs = list(specs) + [pl.BlockSpec(memory_space=pl.ANY)] * waits
    out_specs = out_specs or [pl.BlockSpec(memory_space=pltpu.VMEM)] * len(outs)
    if grid is None:
        how = dict(
            in_specs=[pl.BlockSpec(memory_space=pltpu.SMEM)] * smem + specs,
            out_specs=out_specs,
            scratch_shapes=list(scratch),
        )
    else:
        how = dict(
            grid_spec=pltpu.PrefetchScalarGridSpec(
                num_scalar_prefetch=smem,
                grid=grid,
                in_specs=specs,
                out_specs=out_specs,
                scratch_shapes=list(scratch),
            )
        )
    return pl.pallas_call(
        run,
        out_shape=[jax.ShapeDtypeStruct(shape, kind) for shape, kind in outs],
        compiler_params=pltpu.CompilerParams(vmem_limit_bytes=mib * MIB),
        cost_estimate=pl.CostEstimate(flops=int(us * FLOPS_A_US), bytes_accessed=1, transcendentals=0),
        input_output_aliases=aliases or {},
        name=name,
        **how,
    )(*ins, *after)


def start_copies(jobs, sems):
    copies = []
    for at, (source, target) in enumerate(jobs):
        copy = pltpu.make_async_copy(source, target, sems.at[at])
        copy.start()
        copies.append(copy)
    return copies


def slab_body(spot, q0, q1, k0, k1, v0, v1, gain_one, gain_two, scale, out, turned):
    start = spot[3] * HD
    off = pl.multiple_of(start - start // 128 * 128, 16)
    for w, (left, right) in enumerate(((q0, q1), (k0, k1), (v0, v1))):
        turned[:128] = left[...].astype(F32).T
        turned[128:] = right[...].astype(F32).T
        out[w * HD : w * HD + HD] = turned[pl.ds(off, HD)].astype(BF)
    width = out.shape[1]
    part = scale.shape[0]
    line = jnp.concatenate([line_of(scale), jnp.zeros((1, width - part), F32)], axis=1)
    tail = [line_of(gain_one), line_of(gain_two), line, jnp.zeros((13, width), F32)]
    out[3 * HD :] = jnp.concatenate(tail, axis=0).astype(BF)


def line_of(vector):
    return vector[...].astype(F32).reshape(1, vector.shape[0])


def setup_body(spot, slab, slab_x, weight, gains, scale_col, scale_row):
    width = slab.shape[1]
    f = spot[0]
    mine, theirs = slab[...], slab_x[...]
    left = jnp.where(f == 0, mine, theirs)
    right = jnp.where(f == 0, theirs, mine)
    weight[:, :width] = left[: 3 * HD]
    weight[:, width:] = right[: 3 * HD]
    left, right = left[3 * HD :].astype(F32), right[3 * HD :].astype(F32)
    gains[...] = jnp.concatenate([left[:8], right[:8]], axis=1)
    part = HD // 2
    row = jnp.concatenate([left[2:3, :part], right[2:3, :part], jnp.zeros((1, 128 - HD), F32)], axis=1)
    row = jnp.broadcast_to(row, (128, 128))
    scale_row[...] = row[:8]
    scale_col[...] = row.T[:HD, :1] * HD ** (-0.5)


def project_body(layout, spot, *refs):
    count, pieces, carried, slot = layout
    xs, refs = refs[:count], refs[count:]
    (gains, weight, weight_sib, scale), refs = refs[:4], refs[4:]
    moved, refs = refs[:carried], refs[carried:]
    refs = refs if slot == 0 else refs[1:]
    (norm_out, q_out, kv_out, near_out, far_out), refs = refs[:5], refs[5:]
    outs, (norm_vmem, sems, norm_sem) = refs[:-3], refs[-3:]
    copies = []
    for w, out in zip(moved, outs):
        size = out.shape[0]
        rows = pl.ds(pl.multiple_of(spot[1] * size, 16), size)
        copies.append((w.at[rows], out))
    copies = start_copies(copies, sems)
    x = jnp.concatenate([r[...] for r in xs], axis=0).astype(F32)
    inv = lax.rsqrt(jnp.mean(x * x, axis=-1, keepdims=True) + EPSILON)
    norm = (x * inv * gains[0:1]).astype(BF)
    norm_vmem[...] = norm.reshape(norm_vmem.shape)
    keep = pltpu.make_async_copy(norm_vmem, norm_out.at[pl.ds(slot, pieces)], norm_sem)
    keep.start()
    for table, other in ((weight, False), (weight_sib, True)):
        out = dot(table[...], norm, NT)
        q = (out[:HD] * scale[...]).astype(BF)
        kv = out[HD:].astype(BF)
        for j in range(pieces):
            lanes = slice(j * 128, (j + 1) * 128)
            if other:
                near_out[j, :HD] = q[:, lanes]
                near_out[j, HD:] = kv[:, lanes]
                far_out[j] = kv[:, lanes]
            else:
                q_out[j] = q[:, lanes]
                kv_out[j] = kv[:, lanes]
    for copy in copies:
        copy.wait()
    keep.wait()


def forward_body(layout, chunks, slots_q, slots_k, slots_out, full, total, qblock, *refs):
    count = layout["arrays"]
    arrays, refs = refs[:count], refs[count:]
    (pieces, q_t, k_t, k_rows, v_rows, att, lse), refs = refs[:7], refs[7:]
    block_q, block_kv, v_t, scores, block_out = refs
    for kind, which, index, entry, side in layout["blocks"]:
        for half in range(2):
            lanes = slice(half * 64, half * 64 + 64)
            if kind == "q":
                block_q[slots_q[entry, half]] = arrays[which][index, :HD, lanes]
            else:
                value = arrays[which][index, :, lanes]
                block_kv[side, slots_k[entry, half]] = value[value.shape[0] - 2 * HD :]
    rows = 2 * 256
    ones_row = jnp.where(lax.broadcasted_iota(jnp.int32, (16, rows), 0) == 0, 1.0, 0.0).astype(BF)

    @pl.loop(0, chunks)
    def _(c):
        tile = jnp.concatenate(
            [block_kv[side, 4 * c + m] for side in range(2) for m in range(4)], axis=1
        )
        k_t[c] = tile[:HD]
        k_rows[c] = tile[:HD].astype(F32).T.astype(BF)
        v_rows[c] = tile[HD:].astype(F32).T.astype(BF)
        v_t[c] = jnp.concatenate([tile[HD:], ones_row], axis=0)

    width = q_t.shape[2]
    per = width // 64

    @pl.loop(0, q_t.shape[0])
    def _(i):
        query = jnp.concatenate([block_q[per * i + m] for m in range(per)], axis=1)
        q_t[i] = query
        ids = qblock[i]

        def scan_max(masked, c, top):
            s = dot(k_rows[c], query, NN)
            if masked:
                s = jnp.where(block_of_row(width) + 4 * c <= ids, s, LOWEST)
            scores[c] = s
            return jnp.maximum(top, jnp.max(s.reshape(rows // 8, 8, width), axis=0))

        top = jnp.full((8, width), LOWEST, F32)
        top = lax.fori_loop(0, full[i], functools.partial(scan_max, False), top)
        top = lax.fori_loop(full[i], total[i], functools.partial(scan_max, True), top)
        top = jnp.max(top, axis=0, keepdims=True)

        def gather(c, acc):
            w = jnp.exp(scores[c] - top).astype(BF)
            return acc + dot(v_t[c], w, NN)

        acc = lax.fori_loop(0, total[i], gather, jnp.zeros((HD + 16, width), F32))
        sums = acc[HD : HD + 1]
        out = acc[:HD] / sums
        att[i] = out
        lse[i] = top + jnp.log(sums)
        low = out.astype(BF)
        for m in range(per):
            block_out[per * i + m] = low[:, m * 64 : m * 64 + 64]

    for c in range(GROUP):
        pieces[c] = jnp.concatenate(
            [block_out[slots_out[c, 0]], block_out[slots_out[c, 1]]], axis=1
        )


def block_of_row(width):
    return lax.broadcasted_iota(jnp.int32, (512, width), 0) % 256 // 64


def backward_body(
    slots_out,
    begin,
    clear,
    qblock,
    scale,
    grads,
    q_t,
    att,
    lse,
    k_t_in,
    k_rows_in,
    v_rows_in,
    dkv_own,
    dkv_other,
    dq_pieces,
    scale_sum,
    grad_t,
    delta,
    dq,
    blocks,
    k_t,
    k_rows,
    v_rows,
    sems,
):
    copies = start_copies([(k_t_in, k_t), (k_rows_in, k_rows), (v_rows_in, v_rows)], sems)
    tiles, _, width = q_t.shape
    per = width // 64
    for c in range(GROUP):
        for half in range(2):
            blocks[slots_out[c, half]] = grads[c, :, half * 64 : half * 64 + 64]

    @pl.loop(0, tiles)
    def _(i):
        grad = jnp.concatenate([blocks[per * i + m] for m in range(per)], axis=1)
        grad_t[i] = grad
        delta[i] = jnp.sum(grad.astype(F32) * att[i], axis=0, keepdims=True)
        dq[i] = jnp.zeros((HD, width), F32)

    for copy in copies:
        copy.wait()

    @pl.loop(0, k_t.shape[0])
    def _(c):
        def step(masked, i, carry):
            d_k, d_v = carry
            query, grad = q_t[i], grad_t[i]
            prob = jnp.exp(dot(k_rows[c], query, NN) - lse[i])
            if masked:
                prob = jnp.where(block_of_row(width) + 4 * c <= qblock[i], prob, 0.0)
            d_score = (prob * (dot(v_rows[c], grad, NN) - delta[i])).astype(BF)
            dq[i] += dot(k_t[c], d_score, NN)
            return d_k + dot(query, d_score, NT), d_v + dot(grad, prob.astype(BF), NT)

        carry = (jnp.zeros((HD, 512), F32), jnp.zeros((HD, 512), F32))
        carry = lax.fori_loop(begin[c], clear[c], functools.partial(step, True), carry)
        d_k, d_v = lax.fori_loop(clear[c], tiles, functools.partial(step, False), carry)
        dkv_own[c, :HD] = d_k[:, :256]
        dkv_own[c, HD:] = d_v[:, :256]
        dkv_other[c, :HD] = d_k[:, 256:].astype(BF)
        dkv_other[c, HD:] = d_v[:, 256:].astype(BF)

    total = jnp.zeros((HD, width), F32)
    for i in range(tiles):
        total = total + dq[i] * q_t[i].astype(F32)
        rounded = (dq[i] * scale[...]).astype(BF)
        for m in range(per):
            blocks[per * i + m] = rounded[:, m * 64 : m * 64 + 64]
    scale_sum[...] = total
    for c in range(GROUP):
        dq_pieces[c] = jnp.concatenate(
            [blocks[slots_out[c, 0]], blocks[slots_out[c, 1]]], axis=1
        )


def join_body(slots_kv, spot, dq_pieces, own, received, pieces, other, blocks):
    @pl.loop(0, own.shape[0])
    def _(c):
        tile = (own[c] + received[c].astype(F32)).astype(BF)
        for m in range(4):
            blocks[4 * c + m] = tile[:, m * 64 : m * 64 + 64]

    for p in range(CHIPS):
        for core in range(2):
            c = RING[p] * 2 + core
            pieces[2 * p + core, :HD] = dq_pieces[c]
            pieces[2 * p + core, HD:] = jnp.concatenate(
                [blocks[slots_kv[c, 0]], blocks[slots_kv[c, 1]]], axis=1
            )
    sign = 1 - 2 * spot[1]
    for j in range(5):
        pos = lax.rem(spot[2] + CHIPS - sign * j, CHIPS)
        for core in range(2):
            other[2 * j + core] = pieces[2 * pos + core]


def products_body(spot, pieces, near, weight, weight_sib, out):
    sign = 1 - 2 * spot[1]
    for j in range(5):
        pos = lax.rem(spot[2] + CHIPS + sign * j, CHIPS)
        for core in range(2):
            total = dot(pieces[2 * pos + core], weight[...], TN)
            total = total + dot(near[2 * j + core], weight_sib[...], TN)
            out[j, core * 128 : core * 128 + 128] = total.astype(BF)


def qkv_grad_body(place, spot, pieces, scale_sum, *refs):
    norms, (own, other, table) = refs[:-3], refs[-3:]
    total = jnp.zeros((3 * HD, table.shape[1]), F32)
    for norm, entries in zip(norms, (OWN_ENTRIES, SIB_ENTRIES)):
        for j, entry in enumerate(entries):
            at = 2 * lax.rem(place[entry], CHIPS) + place[entry] // CHIPS
            total = total + dot(pieces[at], norm[j], NN)
    table[...] = total
    width = table.shape[1] // 2
    f = spot[0]
    own[: 3 * HD] = table[:, pl.ds(pl.multiple_of(f * width, 128), width)]
    other[: 3 * HD] = table[:, pl.ds(pl.multiple_of((1 - f) * width, 128), width)].astype(BF)
    column = jnp.broadcast_to(jnp.sum(scale_sum[...], axis=1, keepdims=True), (HD, 128))
    line = column.T[:1]
    high = line.astype(BF)
    low = (line - high.astype(F32)).astype(BF)
    own[3 * HD :] = jnp.zeros((16, width), F32)
    own[3 * HD : 3 * HD + 1, :HD] = line
    tail = jnp.concatenate([high.astype(F32), low.astype(F32), jnp.zeros((14, HD), F32)], axis=0)
    other[3 * HD :] = jnp.concatenate([tail, jnp.zeros((16, width - HD), F32)], axis=1).astype(BF)


def qkv_sum_body(own, received, slab, out):
    width = own.shape[1]
    total = own[: 3 * HD] + received[: 3 * HD].astype(F32)
    out[: 3 * HD] = total.astype(BF)
    gain = jnp.sum(total * slab[: 3 * HD].astype(F32), axis=0, keepdims=True)
    tail = received[3 * HD :].astype(F32)
    line = own[3 * HD : 3 * HD + 1] + tail[0:1] + tail[1:2]
    rows = []
    for value in (gain, line):
        high = value.astype(BF).astype(F32)
        rows += [high, value - high]
    out[3 * HD :] = jnp.concatenate(rows + [jnp.zeros((12, width), F32)], axis=0).astype(BF)


def chip_pack_body(spot, own, near, out):
    rows = own.shape[0]
    out[pl.ds(pl.multiple_of(spot[1] * rows, 16), rows)] = own[...]
    out[pl.ds(pl.multiple_of((1 - spot[1]) * rows, 16), rows)] = near[...]


def ring_positions(spot):
    sign = 1 - 2 * spot[1]
    offsets = [0] + [-sign * s for s in (1, 2, 3)] + [sign * s for s in (1, 2, 3)] + [4]
    return [lax.rem(spot[2] + CHIPS + off, CHIPS) for off in offsets]


def qkv_place_body(spot, *refs):
    arrays, (gain, scale_row), refs = refs[:9], refs[9:11], refs[11:]
    outs, (gain_out, scale_out, table) = refs[:3], refs[3:]
    width = gain.shape[0]
    size = 3 * HD + 16
    tail = jnp.zeros((16, width), F32)
    positions = ring_positions(spot)
    blocks = [(arrays[at], c * size, positions[at], c) for at in range(7) for c in range(2)]
    blocks += [(arrays[7], 0, positions[7], spot[1]), (arrays[8], 0, positions[7], 1 - spot[1])]
    for ref, row, pos, core in blocks:
        chip = jnp.where(pos < 4, 2 * pos, 15 - 2 * pos)
        head = pl.multiple_of((2 * chip + core) * HD, 16)
        for w in range(3):
            table[w, pl.ds(head, HD)] = ref[row + w * HD : row + w * HD + HD]
        tail = tail + ref[row + 3 * HD : row + size].astype(F32)
    for w in range(3):
        for at in range(0, H * HD, 256):
            outs[w][:, at : at + 256] = table[w, at : at + 256].astype(F32).T
    gain_out[...] = ((tail[0:1] + tail[1:2]) / line_of(gain)).reshape(width)
    scale = (tail[2:3, :128] + tail[3:4, :128]) / scale_row[0:1]
    part = scale_out.shape[0]
    chosen = jnp.where(spot[0] == 0, scale[:, :part], scale[:, part : 2 * part])
    scale_out[...] = chosen.reshape(part)


def rows_body(
    spot,
    att_t,
    x_in,
    g_in,
    gain_in,
    *refs,
):
    weights = (refs[:5], refs[5:8], refs[8:11])
    refs = refs[11:]
    (stream_out, dy_out, datt_out), outs = refs[:3], refs[3:7]
    full = refs[7:10]
    turned, sems = refs[10:]
    f, k = spot[0], spot[1]
    half = weights[0][0].shape[0]
    quarter = half // 2
    early = weights[0][1].shape[0]
    places = [
        [k * quarter, (1 - k) * quarter, k * quarter + early, (1 - k) * quarter + early],
        *[[k * quarter, (1 - k) * quarter]] * 2,
    ]
    copies = []
    for w in range(3):
        mine, *theirs = weights[w]
        jobs = [(mine, full[w].at[pl.ds(pl.multiple_of(f * half, 16), half)])]
        for piece, start in zip(theirs, places[w]):
            rows = pl.ds(pl.multiple_of((1 - f) * half + start, 16), piece.shape[0])
            jobs.append((piece, full[w].at[rows]))
        copies.append(start_copies(jobs, sems.at[w]))
    w_out, w_hid, w_ret = full
    x = x_in[...].astype(F32)
    gain = gain_in[1:2]
    for copy in copies[0]:
        copy.wait()
    attn = dot(att_t[...], w_out[...], TN)
    y1 = x + attn
    inv = lax.rsqrt(jnp.mean(y1 * y1, axis=-1, keepdims=True) + EPSILON)
    unit = y1 * inv
    norm = (unit * gain).astype(BF)
    for copy in copies[1]:
        copy.wait()
    h = dot(norm, w_hid[...], NN)
    sig = jax.nn.sigmoid(h)
    act = (h * sig).astype(BF)
    for copy in copies[2]:
        copy.wait()
    stream = y1 + dot(act, w_ret[...], NN)
    stream_out[...] = stream.astype(BF)
    squares = jnp.where(
        lax.broadcasted_iota(jnp.int32, (8, 128), 0) == 0,
        jnp.sum(stream * stream),
        jnp.sum(attn * attn),
    )
    g = g_in[...]
    d_act = dot(g, w_ret[...], NT)
    d_h = (d_act * sig * (1.0 + h * (1.0 - sig))).astype(BF)
    d_norm = dot(d_h, w_hid[...], NT)
    c2 = d_norm * gain
    dy = inv * (c2 - unit * jnp.mean(c2 * unit, axis=-1, keepdims=True)) + g.astype(F32)
    dy_out[...] = dy
    dy_b = dy.astype(BF)
    datt_out[...] = dot(w_out[...], dy_b, NT).astype(BF)
    turned[0] = att_t[...]
    turned[1] = norm.astype(F32).T.astype(BF)
    turned[2] = act.astype(F32).T.astype(BF)
    rows = x.shape[0]
    columns = x.shape[1] // 128
    chunk = half // CHIPS
    sign = 1 - 2 * k
    for ref, part, way in zip(outs, (f, f, 1 - f, 1 - f), (sign, -sign, sign, -sign)):
        for j in range(5):
            pos = lax.rem(spot[2] + CHIPS + way * j, CHIPS)
            at = pl.multiple_of(part * half + pos * chunk, 16)
            for w in range(3):
                start = (w * 5 + j) * chunk
                ref[start : start + chunk] = turned[w, pl.ds(at, chunk)]
    line = sums_line(squares)
    tail = jnp.concatenate([sums_tail(line, 128), jnp.zeros((8, 128), F32)], axis=0).astype(BF)
    for ref in outs[:3]:
        start = 15 * chunk
        for right in (dy_b, d_h):
            for c in range(columns):
                ref[start : start + rows] = right[:, c * 128 : (c + 1) * 128]
                start += rows
        ref[start : start + 16] = tail


def sums_tail(line, width):
    high = line.astype(BF).astype(F32)
    row = lax.broadcasted_iota(jnp.int32, (8, 128), 0)
    tail = jnp.where(row == 0, high, jnp.where(row == 1, line - high, 0.0))
    return tail if width == 128 else jnp.concatenate([tail, jnp.zeros((8, width - 128), F32)], axis=1)


def sums_line(sums):
    lane = lax.broadcasted_iota(jnp.int32, (1, 128), 1)
    return jnp.where(lane == 0, sums[0:1], jnp.where(lane == 1, sums[1:2], 0.0))


def pooled_grad_body(own, sib, far, far_left, far_right, *refs):
    gs, out = refs[:4], refs[4]
    model = out.shape[2]
    columns = model // 128
    group = far_left.shape[0] // 3
    chunk = group // 5
    rows = 128
    totals = []
    for w in range(3):
        lefts, rights = [], []
        for at, (left, right) in enumerate(
            ((own, own), (sib, sib), (far, far), (far_left, far_right))
        ):
            lefts.append(left[w * group : (w + 1) * group])
            start = 3 * group + w * columns * rows
            if w == 2:
                rights.append(gs[at][...])
                continue
            rights.append(
                jnp.concatenate(
                    [right[start + c * rows : start + (c + 1) * rows] for c in range(columns)], axis=1
                )
            )
        left, right = jnp.concatenate(lefts, axis=1), jnp.concatenate(rights, axis=0)
        totals.append(dot(left, right, NN))
    line = jnp.zeros((1, 128), F32)
    for ref in (own, sib, far, far_right):
        tail = ref[ref.shape[0] - 16 :].astype(F32)
        line = line + tail[0:1] + tail[1:2]
    for j in range(5):
        parts = [t[chunk * j : chunk * (j + 1)] for t in totals]
        tail = jnp.zeros((16, model), F32)
        if j == 0:
            tail = jnp.concatenate([sums_tail(line, model), tail[:8]], axis=0)
        out[j] = jnp.concatenate([*parts, tail], axis=0).astype(BF)


def reduce_step_body(step, spot, block, *refs):
    received, out = refs[:-1], refs[-1]
    half = block.shape[2] // 2
    near = pl.ds(pl.multiple_of(spot[1] * half, 128), half)
    if step == 0:
        out[...] = block[0, :, near]
    elif step == 1:
        out[...] = block[0]
        out[:, near] = (block[0, :, near].astype(F32) + received[0][...].astype(F32)).astype(BF)
    else:
        out[...] = (block[0].astype(F32) + received[0][...].astype(F32)).astype(BF)


def reduce_end_body(spot, block, mine, near, out):
    out[...] = (block[0].astype(F32) + mine[...].astype(F32) + near[...].astype(F32)).astype(BF)


def rows_place_body(first, elements, spot, *refs):
    use = (0, 1, 2, 4, 5) if first else (3, 6, 7, 8)
    arrays, refs = refs[: len(use)], refs[len(use) :]
    if first:
        w_hidden, *outs, sums_out, tail_out, staged, sems = refs
    else:
        (w_hidden, gain, sums_in, tail_in), refs = refs[:4], refs[4:]
        outs, (gain_out, means_out, staged, sums, sems) = refs[3:6], refs[6:]
        sums[...] = sums_in[...]
        sums_out = sums
    rows = staged.shape[2]
    half, model = w_hidden.shape
    if first:
        sums_out[...] = jnp.zeros_like(sums_out)
    tail = jnp.zeros((8, 128), F32)
    positions = ring_positions(spot)
    copies = []
    for at, ref in zip(use, arrays):
        block = ref[...].astype(F32)
        place = pl.ds(pl.multiple_of(positions[min(at, 7)] * rows, 16), rows)
        core = spot[1] if at == 7 else 1 - spot[1]
        width = block.shape[1]
        lanes = pl.ds(pl.multiple_of(core * width, 128), width) if at >= 7 else pl.ds(0, width)
        slot = at % 4 if first else min(use.index(at), 2)
        stage = {0: 0, 1: 1, 2: 2, 4: 3, 5: 4}[at] if first else slot
        for w in range(3):
            staged[stage, w, :, lanes] = block[w * rows : (w + 1) * rows]
        total = jnp.zeros((rows, 128), F32)
        weight = w_hidden[place, lanes].astype(F32)
        for c in range(0, width, 128):
            total = total + block[rows : 2 * rows, c : c + 128] * weight[:, c : c + 128]
        sums_out[place] = sums_out[place] + total
        extra = block[3 * rows : 3 * rows + 8, :128]
        tail = tail + (extra if at < 7 else jnp.where(core == 0, extra, 0.0))
        if at != 7:
            for w in range(3):
                copy = pltpu.make_async_copy(staged.at[stage, w], outs[w].at[place], sems.at[stage, w])
                copy.start()
                copies.append(copy)
    if first:
        tail_out[...] = tail
    else:
        tail = tail + tail_in[...]
        means_out[...] = jnp.sqrt((tail[0:1, :2] + tail[1:2, :2]) / elements).reshape(2)
        line = jnp.sum(sums[...].T, axis=0, keepdims=True) / line_of(gain)
        gain_out[...] = line.reshape(half)
    for copy in copies:
        copy.wait()


def inputs_grad_body(spot, block, mine, near, x_in, dy_in, gains, out):
    size = out.shape[0]
    rows = pl.ds(pl.multiple_of(spot[1] * size, 16), size)
    d_norm = block[0, rows].astype(F32) + mine[rows].astype(F32) + near[rows].astype(F32)
    x = x_in[...].astype(F32)
    inv = lax.rsqrt(jnp.mean(x * x, axis=-1, keepdims=True) + EPSILON)
    unit = x * inv
    c1 = d_norm * gains[0:1]
    dx = inv * (c1 - unit * jnp.mean(c1 * unit, axis=-1, keepdims=True)) + dy_in[...]
    out[...] = dx.astype(BF)


def per_device(
    ctx_count,
    stream_in,
    pairing,
    w_query,
    w_key,
    w_value,
    w_output,
    w_hidden,
    w_return,
    gain_attn,
    gain_mlp,
    query_scale,
    cotangent,
):
    sequences, dev_rows, model = stream_in.shape
    half = w_query.shape[0]
    quarter = half // 2
    groups = ctx_count // GROUP
    blocks = 2 * ctx_count
    chunks = blocks // 4
    ctx = lax.axis_index("ctx")
    f = lax.axis_index("fsdp")
    head = ctx % GROUP
    k = head % 2

    def ring(a, shift):
        pairs = [
            (
                g * GROUP + RING[i] * 2 + core,
                g * GROUP + RING[(i + shift) % CHIPS] * 2 + core,
            )
            for g in range(groups)
            for i in range(CHIPS)
            for core in range(2)
        ]
        return lax.ppermute(a, "ctx", pairs)

    def ring_by_core(a):
        pairs = [
            (
                g * GROUP + RING[i] * 2 + core,
                g * GROUP + RING[(i + 1 - 2 * core) % CHIPS] * 2 + core,
            )
            for g in range(groups)
            for i in range(CHIPS)
            for core in range(2)
        ]
        return lax.ppermute(a, "ctx", pairs)

    def swap_core(a):
        return lax.ppermute(a, "ctx", [(c, c ^ 1) for c in range(ctx_count)])

    def swap_far(a):
        pairs = [
            (2 * c + side, 2 * (c ^ 1) + 1 - side) for c in range(ctx_count) for side in range(2)
        ]
        return lax.ppermute(a, ("ctx", "fsdp"), pairs)

    def swap_x(a):
        return lax.ppermute(a, "fsdp", [(0, 1), (1, 0)])

    def turn_groups(a, by):
        return lax.ppermute(
            a, "ctx", [(c, (c + by * GROUP) % ctx_count) for c in range(ctx_count)]
        )

    def sum_groups(a, kind):
        total = a
        for by in range(1, groups):
            total = total + turn_groups(a.astype(kind), by).astype(a.dtype)
        return total

    def exchange(a):
        which = (
            None
            if groups == 1
            else [[g * GROUP + h for h in range(GROUP)] for g in range(groups)]
        )
        return lax.all_to_all(a, "ctx", 0, 0, axis_index_groups=which, tiled=True)

    def swap_cores(arrays):
        swapped = []
        for a in arrays:
            swapped.append(swap_core(a))
        return swapped

    def ring_step(up, down):
        return ring(up, 1), ring(down, -1)

    source = jnp.asarray(SOURCE, jnp.int32)[head]
    place = jnp.asarray(PLACE, jnp.int32)[head]
    chip = head // 2
    ring_at = jnp.where(chip % 2 == 0, chip // 2, CHIPS - 1 - chip // 2)
    spot = jnp.stack([f, k, ring_at, head]).astype(jnp.int32)
    group = ctx // GROUP

    def pairs_of(which):
        return lax.dynamic_slice_in_dim(pairing, which * GROUP, GROUP, 0)

    def slots_of(pairs):
        return jnp.stack([pairs, blocks - 1 - pairs], axis=1).astype(jnp.int32)

    my_pairs = pairs_of(group)
    slots_ctx = slots_of(my_pairs)
    slots_ring = slots_ctx[source]
    if groups == 1:
        ids = np.arange(2 * GROUP, dtype=np.int32)
        slots_q, slots_out = slots_ring, slots_ctx
        slots_k = slots_ring
    else:
        flat = slots_ctx.reshape(-1)
        rank = jnp.sum((flat[None, :] < flat[:, None]).astype(jnp.int32), axis=1)
        ids = jnp.sum(
            jnp.where(rank[None, :] == jnp.arange(2 * GROUP)[:, None], flat[None, :], 0), axis=1
        ).astype(jnp.int32)
        slots_out = rank.reshape(GROUP, 2).astype(jnp.int32)
        slots_q = slots_out[source]
        slots_k = jnp.concatenate(
            [slots_of(pairs_of((group - by) % groups))[source] for by in range(groups)], axis=0
        )
    tiles, width = (4, 512) if groups == 1 else (8, 256)
    by_tile = ids.reshape(tiles, width // 64)
    full = jnp.asarray((by_tile[:, 0] + 1) // 4, jnp.int32)
    total = jnp.asarray(by_tile[:, -1] // 4 + 1, jnp.int32)
    every = np.arange(chunks)[:, None]
    begin = (total[None, :] <= every).sum(axis=1).astype(jnp.int32)
    clear = (full[None, :] <= every).sum(axis=1).astype(jnp.int32)
    qblock = jnp.asarray(ids.repeat(64).reshape(tiles, 1, width), jnp.int32)
    if groups == 1:
        full, total, begin, clear = [
            jnp.asarray(a, jnp.int32)
            for a in (
                (by_tile[:, 0] + 1) // 4,
                by_tile[:, -1] // 4 + 1,
                (by_tile[None, :, -1] // 4 + 1 <= every).sum(axis=1),
                ((by_tile[None, :, 0] + 1) // 4 <= every).sum(axis=1),
            )
        ]

    any_spec = pl.BlockSpec(memory_space=pl.ANY)
    vmem_spec = pl.BlockSpec(memory_space=pltpu.VMEM)
    x = stream_in.reshape(dev_rows, model)
    g_rows = cotangent.reshape(dev_rows, model)
    last = model // 128 - 1

    def columns(more):
        def at(i, spot):
            return (0, jnp.minimum(spot[3] * HD // 128 + more, last))

        return pl.BlockSpec((half, 128), at)

    def whole(shape):
        return pl.BlockSpec(shape, lambda i, spot: (0,) * len(shape))

    part = query_scale.shape[0]
    def gates(arrays, after):
        return call(
            lambda *refs: None,
            [(a.shape, a.dtype) for a in arrays],
            arrays,
            specs=[any_spec] * len(arrays),
            out_specs=[any_spec] * len(arrays),
            after=after,
            aliases={at: at for at in range(len(arrays))},
            name="gate",
        mib=1,
        us=0.1,
        )

    def gate(a, after):
        return gates([a], after)[0]

    steps = [(x,), ring_step(x, x)]
    for _ in range(2):
        steps.append(ring_step(*steps[-1]))
    early = quarter // 5 * 2
    out_xs = [swap_x(lax.dynamic_slice_in_dim(w_output, k * quarter, early, 0))]
    (slab,) = call(
        slab_body,
        [((3 * HD + 16, half), BF)],
        [
            spot,
            *[w for w in (w_query, w_key, w_value) for _ in range(2)],
            gain_attn,
            gain_mlp,
            query_scale,
        ],
        specs=[columns(0), columns(1)] * 3
        + [pl.BlockSpec((n,), lambda i, spot: (0,)) for n in (half, half, part)],
        out_specs=[whole((3 * HD + 16, half))],
        scratch=[pltpu.VMEM((256, half), F32)],
        smem=1,
        grid=(1,),
        name="slab",
        us=3,
        mib=60,
    )
    slab_x = swap_x(slab)
    late = lax.dynamic_slice_in_dim(w_output, k * quarter + early, quarter - early, 0)
    out_xs.append(swap_x(gate(late, [slab_x])))
    weight_t, gains, scale_col, scale_row = call(
        setup_body,
        [((3 * HD, model), BF), ((8, model), F32), ((HD, 1), F32), ((8, 128), F32)],
        [spot, slab, slab_x],
        smem=1,
        after=[*steps[2], *out_xs[:1]],
        name="setup",
        mib=6,
        us=2,
    )
    weight_sib = swap_core(weight_t)

    norms = None
    queries, keys, far_keys, near = [], [], [], []
    norms = None
    slot = 0
    for step in range(2):
        if step:
            up, down = gates(steps[3], queries)
            arrays = [up, down, *ring_step(up[: dev_rows // 2], down[dev_rows // 2 :])]
        else:
            arrays = [x, *steps[1], *steps[2]]
        count = sum(a.shape[0] for a in arrays) // dev_rows
        moved = (w_hidden, w_return) if step else ()
        outs = [((CHIPS, dev_rows, model), BF)]
        outs += [((count, HD, 128), BF), ((count, 2 * HD, 128), BF)]
        outs += [((count, 3 * HD, 128), BF), ((count, 2 * HD, 128), BF)]
        outs += [((quarter, model), BF)] * len(moved)
        ins = [spot, *arrays, gains, weight_t, weight_sib, scale_col, *moved]
        ins += [norms] if step else []
        norms, q_part, kv_part, near_part, far_part, *moved_parts = call(
            functools.partial(project_body, (len(arrays), count, len(moved), slot)),
            outs,
            ins,
            specs=[vmem_spec] * (len(arrays) + 4) + [any_spec] * (len(moved) + bool(step)),
            out_specs=[any_spec] + [vmem_spec] * (len(outs) - 1),
            scratch=[
                pltpu.VMEM((count, dev_rows, model), BF),
                pltpu.SemaphoreType.DMA((max(1, len(moved)),)),
                pltpu.SemaphoreType.DMA,
            ],
            smem=1,
            after=[(), out_xs[1:]][step],
            aliases={len(ins) - 1: 0} if step else None,
            name="project",
            us=[3, 3][step],
            mib=60,
        )
        slot += count
        queries.append(q_part)
        keys.append(kv_part)
        far_keys += [swap_x(kv_part), swap_far(far_part)]
        near.append(swap_core(near_part))
    hid_part, ret_part = moved_parts
    norms_sib = swap_core(norms)
    parts = [w_output]
    for out_x in out_xs:
        out_x = gate(out_x, [norms])
        parts += [out_x, swap_core(out_x)]
    hid_x = swap_x(gate(hid_part, far_keys))
    ret_x = swap_x(gate(ret_part, far_keys))

    arrays, places = [], []
    at = 0
    for step, q_part in enumerate(queries):
        mine, theirs = (q_part, keys[step], far_keys[2 * step]), (near[step], far_keys[2 * step + 1])
        count = q_part.shape[0]
        for entries, blocks_of in ((OWN_ENTRIES, mine), (SIB_ENTRIES, theirs)):
            for j in range(count):
                entry = entries[at + j]
                last = len(arrays) + len(blocks_of) - 1
                places.append(("q", len(arrays), j, entry, 0))
                places.append(("kv", last - 1, j, entry, 0))
                places.append(("kv", last, j, entry, 1))
            arrays += blocks_of
        at += count
    if groups > 1:
        order = OWN_ENTRIES + SIB_ENTRIES
        mine = jnp.concatenate([*keys, *[a[:, HD:] for a in near]], axis=0)
        theirs = jnp.concatenate([*far_keys[::2], *far_keys[1::2]], axis=0)
        for by in range(1, groups):
            for side, a in enumerate((mine, theirs)):
                places += [
                    ("kv", len(arrays), j, by * GROUP + order[j], side) for j in range(GROUP)
                ]
                arrays.append(turn_groups(a, by))
    pieces, q_t, k_t, k_rows, v_rows, att, lse = call(
        functools.partial(forward_body, {"arrays": len(arrays), "blocks": places}, chunks),
        [
            ((GROUP, HD, 128), BF),
            ((tiles, HD, width), BF),
            ((chunks, HD, 512), BF),
            ((chunks, 512, HD), BF),
            ((chunks, 512, HD), BF),
            ((tiles, HD, width), F32),
            ((tiles, 1, width), F32),
        ],
        [slots_q, slots_k, slots_out, full, total, qblock, *arrays],
        scratch=[
            pltpu.VMEM((2 * GROUP, HD, 64), BF),
            pltpu.VMEM((2, blocks, 2 * HD, 64), BF),
            pltpu.VMEM((chunks, HD + 16, 512), BF),
            pltpu.VMEM((chunks, 512, width), F32),
            pltpu.VMEM((2 * GROUP, HD, 64), BF),
        ],
        smem=5,
        name="attention_forward",
        us=20,
        mib=60,
    )
    (pieces,) = gates([pieces], [parts[2], parts[4]])
    att_t = exchange(pieces).reshape(model, dev_rows)
    hid_x, ret_x = gates([hid_x, ret_x], [att_t])
    for w, first in ((w_hidden, hid_x), (w_return, ret_x)):
        parts += [w, first, swap_core(first)]

    g_sib, g_x = swap_core(g_rows), swap_x(gate(g_rows, [pieces]))

    left_rows = 15 * (half // CHIPS)
    share_rows = left_rows + 2 * (model // 128) * dev_rows + 16
    stream, dy, datt_t, f_own, f_sib, f_x, f_xs = call(
        rows_body,
        [
            ((dev_rows, model), BF),
            ((dev_rows, model), F32),
            ((model, dev_rows), BF),
            ((share_rows, 128), BF),
            ((share_rows, 128), BF),
            ((share_rows, 128), BF),
            ((left_rows, 128), BF),
        ],
        [spot, att_t, x, g_rows, gains, *parts],
        specs=[vmem_spec] * 4 + [any_spec] * 11,
        scratch=[pltpu.VMEM((model, model), BF)] * 3
        + [pltpu.VMEM((3, model, dev_rows), BF), pltpu.SemaphoreType.DMA((3, 5))],
        smem=1,
        name="row_part",
        mib=60,
        us=10,
    )
    datt_t, g_x = gates([datt_t, g_x], ())
    grads = exchange(datt_t.reshape(GROUP, HD, dev_rows))
    g_xs = swap_core(g_x)

    from_x = swap_x(f_x)
    forward = swap_core(f_xs)
    from_sib, from_xs = swap_core(f_sib), swap_x(forward)

    def chunk_call(table, body, chunk, ins, outs, name, after):
        return call(
            body,
            outs,
            [spot, table, *ins],
            specs=[pl.BlockSpec((1, 256, model), lambda i, spot: (chunk, 0, 0))]
            + [whole(a.shape) for a in ins],
            out_specs=[whole(shape) for shape, _ in outs],
            smem=1,
            grid=(1,),
            after=after,
            name=name,
            us=2,
            mib=16,
        )

    def reduce_step(table, step, received, after):
        outs = chunk_call(
            table,
            functools.partial(reduce_step_body, step),
            4 - step,
            received,
            [((256, model if step else model // 2), BF)],
            "reduce_step",
            after,
        )
        return [ring_by_core(outs[0])], outs

    own, other, dq_pieces, scale_sum = call(
        backward_body,
        [
            ((chunks, 2 * HD, 256), F32),
            ((chunks, 2 * HD, 256), BF),
            ((GROUP, HD, 128), BF),
            ((HD, width), F32),
        ],
        [slots_out, begin, clear, qblock, scale_col, grads, q_t, att, lse, k_t, k_rows, v_rows],
        specs=[vmem_spec] * 6 + [any_spec] * 3,
        scratch=[
            pltpu.VMEM((tiles, HD, width), BF),
            pltpu.VMEM((tiles, 1, width), F32),
            pltpu.VMEM((tiles, HD, width), F32),
            pltpu.VMEM((2 * GROUP, HD, 64), BF),
            pltpu.VMEM((chunks, HD, 512), BF),
            pltpu.VMEM((chunks, 512, HD), BF),
            pltpu.VMEM((chunks, 512, HD), BF),
            pltpu.SemaphoreType.DMA((3,)),
        ],
        smem=3,
        after=[forward],
        name="attention_backward",
        us=25,
        mib=60,
    )
    other_x = swap_x(other)
    from_x, from_sib, from_xs, g_xs, norms_sib = gates(
        [from_x, from_sib, from_xs, g_xs, norms_sib], [own]
    )
    (partial,) = call(
        pooled_grad_body,
        [((5, 256, model), BF)],
        [f_own, from_sib, from_x, from_xs, swap_core(from_x), g_rows, g_sib, g_x, g_xs],
        name="pooled_grads",
        us=3,
        mib=24,
    )
    received, done = reduce_step(partial, 0, (), ())
    if groups > 1:
        own = sum_groups(own + other_x.astype(F32), BF)
        other_x = jnp.zeros_like(other_x)
    received, done = reduce_step(partial, 1, received, ())
    d_pieces, d_other = call(
        join_body,
        [((GROUP, 3 * HD, 128), BF), ((10, 3 * HD, 128), BF)],
        [slots_ctx, spot, dq_pieces, own, other_x],
        scratch=[pltpu.VMEM((blocks, 2 * HD, 64), BF)],
        smem=2,
        after=done,
        name="join",
        us=2,
        mib=24 if groups == 1 else 60,
    )
    d_near = swap_core(d_other)
    own_share, other_share = call(
        qkv_grad_body,
        [((3 * HD + 16, half), F32), ((3 * HD + 16, half), BF)],
        [place, spot, d_pieces, scale_sum, norms, norms_sib],
        scratch=[pltpu.VMEM((3 * HD, model), F32)],
        smem=2,
        name="qkv_grads",
        us=4.7,
        mib=24,
    )
    share_x = swap_x(other_share)
    received, done = reduce_step(partial, 2, received, [own_share])

    (table,) = call(
        products_body,
        [((5, 256, model), BF)],
        [spot, d_pieces, d_near, weight_t, weight_sib],
        smem=1,
        after=done,
        name="products",
        us=4,
        mib=24,
    )
    first, done = reduce_step(table, 0, (), ())
    (share,) = call(
        qkv_sum_body,
        [((3 * HD + 16, half), BF)],
        [own_share, share_x, slab],
        after=done,
        name="qkv_sum",
        us=1,
        mib=8,
    )
    share = sum_groups(share.astype(F32), BF).astype(BF) if groups > 1 else share
    share_near = swap_core(share)
    received, done = reduce_step(partial, 3, received, [share])
    received_near = swap_core(received[0])
    (chip_share,) = call(
        chip_pack_body,
        [((2 * (3 * HD + 16), half), BF)],
        [spot, share, share_near],
        smem=1,
        after=done,
        name="chip_pack",
        us=1,
        mib=8,
    )
    q_steps = [chip_share, ring_by_core(chip_share)]
    first, done = reduce_step(table, 1, first, [chip_share])
    (mine,) = chunk_call(
        partial,
        reduce_end_body,
        0,
        (*received, received_near),
        [((256, model), BF)],
        "reduce_end",
        [chip_share],
    )
    first, done = reduce_step(table, 2, first, [mine, q_steps[1]])
    mine = sum_groups(mine.astype(F32), BF).astype(BF) if groups > 1 else mine
    m_steps = [mine, ring_by_core(mine)]
    q_steps.append(ring_by_core(q_steps[-1]))
    first, done = reduce_step(table, 3, first, [*done, q_steps[2]])
    m_steps.append(ring_by_core(m_steps[-1]))
    q_steps.append(ring_by_core(q_steps[-1]))
    m_steps.append(ring_by_core(m_steps[-1]))
    first_near = swap_core(first[0])
    (d_in,) = chunk_call(
        table,
        inputs_grad_body,
        0,
        (*first, first_near, x, dy, gains),
        [((dev_rows, model), BF)],
        "inputs_grad",
        [m_steps[2], q_steps[3]],
    )
    q_near = [swap_core(a) for a in q_steps[1:3]]
    m_near = [swap_core(a) for a in m_steps[1:3]]
    elements = float(ctx_count * 2 * dev_rows * model)
    chunk = half // CHIPS
    grads_shape = [((half, model), F32)] * 3
    *rows_grads, gain_sums, tails = call(
        functools.partial(rows_place_body, True, elements),
        [*grads_shape, ((half, 128), F32), ((8, 128), F32)],
        [spot, *m_steps[:3], *m_near, w_hidden],
        out_specs=[any_spec] * 3 + [vmem_spec] * 2,
        scratch=[pltpu.VMEM((5, 3, chunk, model), F32), pltpu.SemaphoreType.DMA((5, 3))],
        smem=1,
        after=q_near,
        name="rows_place",
        us=4,
        mib=40,
    )

    def last_step(a, axis):
        size = a.shape[axis] // 2
        return ring_by_core(lax.dynamic_slice_in_dim(a, k * size, size, axis))

    q_last = last_step(q_steps[-1], 0)
    (m_held,) = gates([m_steps[-1]], [d_in, tails])
    m_last = last_step(m_held, 1)
    q_near += [swap_core(a) for a in q_steps[3:]]
    m_near += [swap_core(m_held)]
    grad_query, grad_key, grad_value, gain_one_grad, scale_grad = call(
        qkv_place_body,
        [((half, model), F32)] * 3 + [((half,), F32), ((part,), F32)],
        [spot, *q_steps, *q_near, q_last, swap_core(q_last), gain_attn, scale_row],
        scratch=[pltpu.VMEM((3, model, half), BF)],
        smem=1,
        name="qkv_place",
        us=6,
        mib=40,
    )
    (m_last,) = gates([m_last], [grad_query])
    ins = [spot, m_held, m_near[2], m_last, swap_core(m_last), w_hidden, gain_mlp, gain_sums, tails]
    grad_output, grad_hidden, grad_return, gain_two_grad, root_means = call(
        functools.partial(rows_place_body, False, elements),
        [*grads_shape, ((half,), F32), ((2,), F32)],
        [*ins, *rows_grads],
        specs=[vmem_spec] * (len(ins) - 1) + [any_spec] * 3,
        out_specs=[any_spec] * 3 + [vmem_spec] * 2,
        scratch=[
            pltpu.VMEM((3, 3, chunk, model), F32),
            pltpu.VMEM((half, 128), F32),
            pltpu.SemaphoreType.DMA((3, 3)),
        ],
        smem=1,
        aliases={len(ins) + at: at for at in range(3)},
        name="rows_place",
        us=3,
        mib=40,
    )
    return (
        stream.reshape(stream_in.shape),
        d_in.reshape(stream_in.shape),
        grad_query,
        grad_key,
        grad_value,
        grad_output,
        grad_hidden,
        grad_return,
        gain_one_grad,
        gain_two_grad,
        scale_grad,
        root_means,
    )


def solution(mesh):
    rows = P(None, ("ctx", "fsdp"), None)
    weight, vector = P("fsdp", None), P("fsdp")
    return jax.shard_map(
        functools.partial(per_device, mesh.shape["ctx"]),
        mesh=mesh,
        in_specs=(rows, P(), *([weight] * 6), *([vector] * 3), rows),
        out_specs=(rows, rows, *([weight] * 6), *([vector] * 3), P()),
        check_vma=False,
    )
```

```python
import functools

import jax
import jax.numpy as jnp
import numpy as np
from jax import lax
from jax.experimental import pallas as pl
from jax.experimental.pallas import tpu as pltpu
from jax.sharding import PartitionSpec as P

H = 16
HD = 80
EPSILON = 1e-06
LOWEST = -1e30
BF = jnp.bfloat16
F32 = jnp.float32
MIB = 1024 * 1024
FLOPS_A_US = 1.15e9

GROUP = 16
CHIPS = 8
RING = (0, 2, 4, 6, 7, 5, 3, 1)
ORDER = (
    ((0, 0), (0, 1))
    + tuple((off, core) for s in (1, 2, 3) for core in (0, 1) for off in (-s, s))
    + ((4, 0), (4, 1))
)
SOURCE = [
    [RING[(RING.index(h // 2) + off) % CHIPS] * 2 + ((h % 2) ^ core) for off, core in ORDER]
    for h in range(GROUP)
]
PLACE = [
    [((h % 2) ^ core) * CHIPS + (RING.index(h // 2) + off) % CHIPS for off, core in ORDER]
    for h in range(GROUP)
]

OWN_ENTRIES = (0, 2, 3, 6, 7, 10, 11, 14)
SIB_ENTRIES = (1, 4, 5, 8, 9, 12, 13, 15)

NN = (((1,), (0,)), ((), ()))
NT = (((1,), (1,)), ((), ()))
TN = (((0,), (0,)), ((), ()))


def dot(a, b, dims):
    return lax.dot_general(a, b, dims, preferred_element_type=F32)


def call(body, outs, ins, scratch=(), specs=None, out_specs=None, name=None, smem=0, after=(), grid=None, aliases=None, us=1.0, mib=24):
    given = len(ins)
    waits = len(after)

    def run(*refs):
        body(*refs[:given], *refs[given + waits :])

    if specs is None:
        specs = [pl.BlockSpec(memory_space=pltpu.VMEM)] * (given - smem)
    specs = list(specs) + [pl.BlockSpec(memory_space=pl.ANY)] * waits
    out_specs = out_specs or [pl.BlockSpec(memory_space=pltpu.VMEM)] * len(outs)
    if grid is None:
        how = dict(
            in_specs=[pl.BlockSpec(memory_space=pltpu.SMEM)] * smem + specs,
            out_specs=out_specs,
            scratch_shapes=list(scratch),
        )
    else:
        how = dict(
            grid_spec=pltpu.PrefetchScalarGridSpec(
                num_scalar_prefetch=smem,
                grid=grid,
                in_specs=specs,
                out_specs=out_specs,
                scratch_shapes=list(scratch),
            )
        )
    return pl.pallas_call(
        run,
        out_shape=[jax.ShapeDtypeStruct(shape, kind) for shape, kind in outs],
        compiler_params=pltpu.CompilerParams(vmem_limit_bytes=mib * MIB),
        cost_estimate=pl.CostEstimate(flops=int(us * FLOPS_A_US), bytes_accessed=1, transcendentals=0),
        input_output_aliases=aliases or {},
        name=name,
        **how,
    )(*ins, *after)


def start_copies(jobs, sems):
    copies = []
    for at, (source, target) in enumerate(jobs):
        copy = pltpu.make_async_copy(source, target, sems.at[at])
        copy.start()
        copies.append(copy)
    return copies


def slab_body(spot, q0, q1, k0, k1, v0, v1, gain_one, gain_two, scale, out, turned):
    start = spot[3] * HD
    off = pl.multiple_of(start - start // 128 * 128, 16)
    for w, (left, right) in enumerate(((q0, q1), (k0, k1), (v0, v1))):
        turned[:128] = left[...].astype(F32).T
        turned[128:] = right[...].astype(F32).T
        out[w * HD : w * HD + HD] = turned[pl.ds(off, HD)].astype(BF)
    width = out.shape[1]
    part = scale.shape[0]
    line = jnp.concatenate([line_of(scale), jnp.zeros((1, width - part), F32)], axis=1)
    tail = [line_of(gain_one), line_of(gain_two), line, jnp.zeros((13, width), F32)]
    out[3 * HD :] = jnp.concatenate(tail, axis=0).astype(BF)


def line_of(vector):
    return vector[...].astype(F32).reshape(1, vector.shape[0])


def setup_body(spot, slab, slab_x, weight, gains, scale_col, scale_row):
    width = slab.shape[1]
    f = spot[0]
    mine, theirs = slab[...], slab_x[...]
    left = jnp.where(f == 0, mine, theirs)
    right = jnp.where(f == 0, theirs, mine)
    weight[:, :width] = left[: 3 * HD]
    weight[:, width:] = right[: 3 * HD]
    left, right = left[3 * HD :].astype(F32), right[3 * HD :].astype(F32)
    gains[...] = jnp.concatenate([left[:8], right[:8]], axis=1)
    part = HD // 2
    row = jnp.concatenate([left[2:3, :part], right[2:3, :part], jnp.zeros((1, 128 - HD), F32)], axis=1)
    row = jnp.broadcast_to(row, (128, 128))
    scale_row[...] = row[:8]
    scale_col[...] = row.T[:HD, :1] * HD ** (-0.5)


def project_body(layout, spot, *refs):
    count, pieces, carried, slot = layout
    xs, refs = refs[:count], refs[count:]
    (gains, weight, weight_sib, scale), refs = refs[:4], refs[4:]
    moved, refs = refs[:carried], refs[carried:]
    refs = refs if slot == 0 else refs[1:]
    (norm_out, q_out, kv_out, near_out, far_out), refs = refs[:5], refs[5:]
    outs, (norm_vmem, sems, norm_sem) = refs[:-3], refs[-3:]
    copies = []
    for w, out in zip(moved, outs):
        size = out.shape[0]
        rows = pl.ds(pl.multiple_of(spot[1] * size, 16), size)
        copies.append((w.at[rows], out))
    copies = start_copies(copies, sems)
    x = jnp.concatenate([r[...] for r in xs], axis=0).astype(F32)
    inv = lax.rsqrt(jnp.mean(x * x, axis=-1, keepdims=True) + EPSILON)
    norm = (x * inv * gains[0:1]).astype(BF)
    norm_vmem[...] = norm.reshape(norm_vmem.shape)
    keep = pltpu.make_async_copy(norm_vmem, norm_out.at[pl.ds(slot, pieces)], norm_sem)
    keep.start()
    for table, other in ((weight, False), (weight_sib, True)):
        out = dot(table[...], norm, NT)
        q = (out[:HD] * scale[...]).astype(BF)
        kv = out[HD:].astype(BF)
        for j in range(pieces):
            lanes = slice(j * 128, (j + 1) * 128)
            if other:
                near_out[j, :HD] = q[:, lanes]
                near_out[j, HD:] = kv[:, lanes]
                far_out[j] = kv[:, lanes]
            else:
                q_out[j] = q[:, lanes]
                kv_out[j] = kv[:, lanes]
    for copy in copies:
        copy.wait()
    keep.wait()


def forward_body(layout, chunks, slots_q, slots_k, slots_out, full, total, qblock, *refs):
    count = layout["arrays"]
    arrays, refs = refs[:count], refs[count:]
    (pieces, q_t, k_t, k_rows, v_rows, att, lse), refs = refs[:7], refs[7:]
    block_q, block_kv, v_t, scores, block_out = refs
    for kind, which, index, entry, side in layout["blocks"]:
        for half in range(2):
            lanes = slice(half * 64, half * 64 + 64)
            if kind == "q":
                block_q[slots_q[entry, half]] = arrays[which][index, :HD, lanes]
            else:
                value = arrays[which][index, :, lanes]
                block_kv[side, slots_k[entry, half]] = value[value.shape[0] - 2 * HD :]
    rows = 2 * 256
    ones_row = jnp.where(lax.broadcasted_iota(jnp.int32, (16, rows), 0) == 0, 1.0, 0.0).astype(BF)

    @pl.loop(0, chunks)
    def _(c):
        tile = jnp.concatenate(
            [block_kv[side, 4 * c + m] for side in range(2) for m in range(4)], axis=1
        )
        k_t[c] = tile[:HD]
        k_rows[c] = tile[:HD].astype(F32).T.astype(BF)
        v_rows[c] = tile[HD:].astype(F32).T.astype(BF)
        v_t[c] = jnp.concatenate([tile[HD:], ones_row], axis=0)

    width = q_t.shape[2]
    per = width // 64

    @pl.loop(0, q_t.shape[0])
    def _(i):
        query = jnp.concatenate([block_q[per * i + m] for m in range(per)], axis=1)
        q_t[i] = query
        ids = qblock[i]

        def scan_max(masked, c, top):
            s = dot(k_rows[c], query, NN)
            if masked:
                s = jnp.where(block_of_row(width) + 4 * c <= ids, s, LOWEST)
            scores[c] = s
            return jnp.maximum(top, jnp.max(s.reshape(rows // 8, 8, width), axis=0))

        top = jnp.full((8, width), LOWEST, F32)
        top = lax.fori_loop(0, full[i], functools.partial(scan_max, False), top)
        top = lax.fori_loop(full[i], total[i], functools.partial(scan_max, True), top)
        top = jnp.max(top, axis=0, keepdims=True)

        def gather(c, acc):
            w = jnp.exp(scores[c] - top).astype(BF)
            return acc + dot(v_t[c], w, NN)

        acc = lax.fori_loop(0, total[i], gather, jnp.zeros((HD + 16, width), F32))
        sums = acc[HD : HD + 1]
        out = acc[:HD] / sums
        att[i] = out
        lse[i] = top + jnp.log(sums)
        low = out.astype(BF)
        for m in range(per):
            block_out[per * i + m] = low[:, m * 64 : m * 64 + 64]

    for c in range(GROUP):
        pieces[c] = jnp.concatenate(
            [block_out[slots_out[c, 0]], block_out[slots_out[c, 1]]], axis=1
        )


def block_of_row(width):
    return lax.broadcasted_iota(jnp.int32, (512, width), 0) % 256 // 64


def backward_body(
    slots_out,
    begin,
    clear,
    qblock,
    scale,
    grads,
    q_t,
    att,
    lse,
    k_t_in,
    k_rows_in,
    v_rows_in,
    dkv_own,
    dkv_other,
    dq_pieces,
    scale_sum,
    grad_t,
    delta,
    dq,
    blocks,
    k_t,
    k_rows,
    v_rows,
    sems,
):
    copies = start_copies([(k_t_in, k_t), (k_rows_in, k_rows), (v_rows_in, v_rows)], sems)
    tiles, _, width = q_t.shape
    per = width // 64
    for c in range(GROUP):
        for half in range(2):
            blocks[slots_out[c, half]] = grads[c, :, half * 64 : half * 64 + 64]

    @pl.loop(0, tiles)
    def _(i):
        grad = jnp.concatenate([blocks[per * i + m] for m in range(per)], axis=1)
        grad_t[i] = grad
        delta[i] = jnp.sum(grad.astype(F32) * att[i], axis=0, keepdims=True)
        dq[i] = jnp.zeros((HD, width), F32)

    for copy in copies:
        copy.wait()

    @pl.loop(0, k_t.shape[0])
    def _(c):
        def step(masked, i, carry):
            d_k, d_v = carry
            query, grad = q_t[i], grad_t[i]
            prob = jnp.exp(dot(k_rows[c], query, NN) - lse[i])
            if masked:
                prob = jnp.where(block_of_row(width) + 4 * c <= qblock[i], prob, 0.0)
            d_score = (prob * (dot(v_rows[c], grad, NN) - delta[i])).astype(BF)
            dq[i] += dot(k_t[c], d_score, NN)
            return d_k + dot(query, d_score, NT), d_v + dot(grad, prob.astype(BF), NT)

        carry = (jnp.zeros((HD, 512), F32), jnp.zeros((HD, 512), F32))
        carry = lax.fori_loop(begin[c], clear[c], functools.partial(step, True), carry)
        d_k, d_v = lax.fori_loop(clear[c], tiles, functools.partial(step, False), carry)
        dkv_own[c, :HD] = d_k[:, :256]
        dkv_own[c, HD:] = d_v[:, :256]
        dkv_other[c, :HD] = d_k[:, 256:].astype(BF)
        dkv_other[c, HD:] = d_v[:, 256:].astype(BF)

    total = jnp.zeros((HD, width), F32)
    for i in range(tiles):
        total = total + dq[i] * q_t[i].astype(F32)
        rounded = (dq[i] * scale[...]).astype(BF)
        for m in range(per):
            blocks[per * i + m] = rounded[:, m * 64 : m * 64 + 64]
    scale_sum[...] = total
    for c in range(GROUP):
        dq_pieces[c] = jnp.concatenate(
            [blocks[slots_out[c, 0]], blocks[slots_out[c, 1]]], axis=1
        )


def join_body(slots_kv, spot, dq_pieces, own, received, pieces, other, blocks):
    @pl.loop(0, own.shape[0])
    def _(c):
        tile = (own[c] + received[c].astype(F32)).astype(BF)
        for m in range(4):
            blocks[4 * c + m] = tile[:, m * 64 : m * 64 + 64]

    for p in range(CHIPS):
        for core in range(2):
            c = RING[p] * 2 + core
            pieces[2 * p + core, :HD] = dq_pieces[c]
            pieces[2 * p + core, HD:] = jnp.concatenate(
                [blocks[slots_kv[c, 0]], blocks[slots_kv[c, 1]]], axis=1
            )
    sign = 1 - 2 * spot[1]
    for j in range(5):
        pos = lax.rem(spot[2] + CHIPS - sign * j, CHIPS)
        for core in range(2):
            other[2 * j + core] = pieces[2 * pos + core]


def products_body(spot, pieces, near, weight, weight_sib, out):
    sign = 1 - 2 * spot[1]
    for j in range(5):
        pos = lax.rem(spot[2] + CHIPS + sign * j, CHIPS)
        for core in range(2):
            total = dot(pieces[2 * pos + core], weight[...], TN)
            total = total + dot(near[2 * j + core], weight_sib[...], TN)
            out[j, core * 128 : core * 128 + 128] = total.astype(BF)


def qkv_grad_body(place, spot, pieces, scale_sum, *refs):
    norms, (own, other, table) = refs[:-3], refs[-3:]
    total = jnp.zeros((3 * HD, table.shape[1]), F32)
    for norm, entries in zip(norms, (OWN_ENTRIES, SIB_ENTRIES)):
        for j, entry in enumerate(entries):
            at = 2 * lax.rem(place[entry], CHIPS) + place[entry] // CHIPS
            total = total + dot(pieces[at], norm[j], NN)
    table[...] = total
    width = table.shape[1] // 2
    f = spot[0]
    own[: 3 * HD] = table[:, pl.ds(pl.multiple_of(f * width, 128), width)]
    other[: 3 * HD] = table[:, pl.ds(pl.multiple_of((1 - f) * width, 128), width)].astype(BF)
    column = jnp.broadcast_to(jnp.sum(scale_sum[...], axis=1, keepdims=True), (HD, 128))
    line = column.T[:1]
    high = line.astype(BF)
    low = (line - high.astype(F32)).astype(BF)
    own[3 * HD :] = jnp.zeros((16, width), F32)
    own[3 * HD : 3 * HD + 1, :HD] = line
    tail = jnp.concatenate([high.astype(F32), low.astype(F32), jnp.zeros((14, HD), F32)], axis=0)
    other[3 * HD :] = jnp.concatenate([tail, jnp.zeros((16, width - HD), F32)], axis=1).astype(BF)


def qkv_sum_body(own, received, slab, out):
    width = own.shape[1]
    total = own[: 3 * HD] + received[: 3 * HD].astype(F32)
    out[: 3 * HD] = total.astype(BF)
    gain = jnp.sum(total * slab[: 3 * HD].astype(F32), axis=0, keepdims=True)
    tail = received[3 * HD :].astype(F32)
    line = own[3 * HD : 3 * HD + 1] + tail[0:1] + tail[1:2]
    rows = []
    for value in (gain, line):
        high = value.astype(BF).astype(F32)
        rows += [high, value - high]
    out[3 * HD :] = jnp.concatenate(rows + [jnp.zeros((12, width), F32)], axis=0).astype(BF)


def chip_pack_body(spot, own, near, out):
    rows = own.shape[0]
    out[pl.ds(pl.multiple_of(spot[1] * rows, 16), rows)] = own[...]
    out[pl.ds(pl.multiple_of((1 - spot[1]) * rows, 16), rows)] = near[...]


def ring_positions(spot):
    sign = 1 - 2 * spot[1]
    offsets = [0] + [-sign * s for s in (1, 2, 3)] + [sign * s for s in (1, 2, 3)] + [4]
    return [lax.rem(spot[2] + CHIPS + off, CHIPS) for off in offsets]


def qkv_place_body(spot, *refs):
    arrays, (gain, scale_row), refs = refs[:9], refs[9:11], refs[11:]
    outs, (gain_out, scale_out, table) = refs[:3], refs[3:]
    width = gain.shape[0]
    size = 3 * HD + 16
    tail = jnp.zeros((16, width), F32)
    positions = ring_positions(spot)
    blocks = [(arrays[at], c * size, positions[at], c) for at in range(7) for c in range(2)]
    blocks += [(arrays[7], 0, positions[7], spot[1]), (arrays[8], 0, positions[7], 1 - spot[1])]
    for ref, row, pos, core in blocks:
        chip = jnp.where(pos < 4, 2 * pos, 15 - 2 * pos)
        head = pl.multiple_of((2 * chip + core) * HD, 16)
        for w in range(3):
            table[w, pl.ds(head, HD)] = ref[row + w * HD : row + w * HD + HD]
        tail = tail + ref[row + 3 * HD : row + size].astype(F32)
    for w in range(3):
        for at in range(0, H * HD, 256):
            outs[w][:, at : at + 256] = table[w, at : at + 256].astype(F32).T
    gain_out[...] = ((tail[0:1] + tail[1:2]) / line_of(gain)).reshape(width)
    scale = (tail[2:3, :128] + tail[3:4, :128]) / scale_row[0:1]
    part = scale_out.shape[0]
    chosen = jnp.where(spot[0] == 0, scale[:, :part], scale[:, part : 2 * part])
    scale_out[...] = chosen.reshape(part)


def rows_body(
    spot,
    att_t,
    x_in,
    g_in,
    gain_in,
    *refs,
):
    weights = (refs[:5], refs[5:8], refs[8:11])
    refs = refs[11:]
    (stream_out, dy_out, datt_out), outs = refs[:3], refs[3:7]
    full = refs[7:10]
    turned, sems = refs[10:]
    f, k = spot[0], spot[1]
    half = weights[0][0].shape[0]
    quarter = half // 2
    early = weights[0][1].shape[0]
    places = [
        [k * quarter, (1 - k) * quarter, k * quarter + early, (1 - k) * quarter + early],
        *[[k * quarter, (1 - k) * quarter]] * 2,
    ]
    copies = []
    for w in range(3):
        mine, *theirs = weights[w]
        jobs = [(mine, full[w].at[pl.ds(pl.multiple_of(f * half, 16), half)])]
        for piece, start in zip(theirs, places[w]):
            rows = pl.ds(pl.multiple_of((1 - f) * half + start, 16), piece.shape[0])
            jobs.append((piece, full[w].at[rows]))
        copies.append(start_copies(jobs, sems.at[w]))
    w_out, w_hid, w_ret = full
    x = x_in[...].astype(F32)
    gain = gain_in[1:2]
    for copy in copies[0]:
        copy.wait()
    attn = dot(att_t[...], w_out[...], TN)
    y1 = x + attn
    inv = lax.rsqrt(jnp.mean(y1 * y1, axis=-1, keepdims=True) + EPSILON)
    unit = y1 * inv
    norm = (unit * gain).astype(BF)
    for copy in copies[1]:
        copy.wait()
    h = dot(norm, w_hid[...], NN)
    sig = jax.nn.sigmoid(h)
    act = (h * sig).astype(BF)
    for copy in copies[2]:
        copy.wait()
    stream = y1 + dot(act, w_ret[...], NN)
    stream_out[...] = stream.astype(BF)
    squares = jnp.where(
        lax.broadcasted_iota(jnp.int32, (8, 128), 0) == 0,
        jnp.sum(stream * stream),
        jnp.sum(attn * attn),
    )
    g = g_in[...]
    d_act = dot(g, w_ret[...], NT)
    d_h = (d_act * sig * (1.0 + h * (1.0 - sig))).astype(BF)
    d_norm = dot(d_h, w_hid[...], NT)
    c2 = d_norm * gain
    dy = inv * (c2 - unit * jnp.mean(c2 * unit, axis=-1, keepdims=True)) + g.astype(F32)
    dy_out[...] = dy
    dy_b = dy.astype(BF)
    datt_out[...] = dot(w_out[...], dy_b, NT).astype(BF)
    turned[0] = att_t[...]
    turned[1] = norm.astype(F32).T.astype(BF)
    turned[2] = act.astype(F32).T.astype(BF)
    rows = x.shape[0]
    columns = x.shape[1] // 128
    chunk = half // CHIPS
    sign = 1 - 2 * k
    for ref, part, way in zip(outs, (f, f, 1 - f, 1 - f), (sign, -sign, sign, -sign)):
        for j in range(5):
            pos = lax.rem(spot[2] + CHIPS + way * j, CHIPS)
            at = pl.multiple_of(part * half + pos * chunk, 16)
            for w in range(3):
                start = (w * 5 + j) * chunk
                ref[start : start + chunk] = turned[w, pl.ds(at, chunk)]
    line = sums_line(squares)
    tail = jnp.concatenate([sums_tail(line, 128), jnp.zeros((8, 128), F32)], axis=0).astype(BF)
    for ref in outs[:3]:
        start = 15 * chunk
        for right in (dy_b, d_h):
            for c in range(columns):
                ref[start : start + rows] = right[:, c * 128 : (c + 1) * 128]
                start += rows
        ref[start : start + 16] = tail


def sums_tail(line, width):
    high = line.astype(BF).astype(F32)
    row = lax.broadcasted_iota(jnp.int32, (8, 128), 0)
    tail = jnp.where(row == 0, high, jnp.where(row == 1, line - high, 0.0))
    return tail if width == 128 else jnp.concatenate([tail, jnp.zeros((8, width - 128), F32)], axis=1)


def sums_line(sums):
    lane = lax.broadcasted_iota(jnp.int32, (1, 128), 1)
    return jnp.where(lane == 0, sums[0:1], jnp.where(lane == 1, sums[1:2], 0.0))


def pooled_grad_body(own, sib, far, far_left, far_right, *refs):
    gs, out = refs[:4], refs[4]
    model = out.shape[2]
    columns = model // 128
    group = far_left.shape[0] // 3
    chunk = group // 5
    rows = 128
    totals = []
    for w in range(3):
        lefts, rights = [], []
        for at, (left, right) in enumerate(
            ((own, own), (sib, sib), (far, far), (far_left, far_right))
        ):
            lefts.append(left[w * group : (w + 1) * group])
            start = 3 * group + w * columns * rows
            if w == 2:
                rights.append(gs[at][...])
                continue
            rights.append(
                jnp.concatenate(
                    [right[start + c * rows : start + (c + 1) * rows] for c in range(columns)], axis=1
                )
            )
        left, right = jnp.concatenate(lefts, axis=1), jnp.concatenate(rights, axis=0)
        totals.append(dot(left, right, NN))
    line = jnp.zeros((1, 128), F32)
    for ref in (own, sib, far, far_right):
        tail = ref[ref.shape[0] - 16 :].astype(F32)
        line = line + tail[0:1] + tail[1:2]
    for j in range(5):
        parts = [t[chunk * j : chunk * (j + 1)] for t in totals]
        tail = jnp.zeros((16, model), F32)
        if j == 0:
            tail = jnp.concatenate([sums_tail(line, model), tail[:8]], axis=0)
        out[j] = jnp.concatenate([*parts, tail], axis=0).astype(BF)


def reduce_step_body(step, spot, block, *refs):
    received, out = refs[:-1], refs[-1]
    half = block.shape[2] // 2
    near = pl.ds(pl.multiple_of(spot[1] * half, 128), half)
    if step == 0:
        out[...] = block[0, :, near]
    elif step == 1:
        out[...] = block[0]
        out[:, near] = (block[0, :, near].astype(F32) + received[0][...].astype(F32)).astype(BF)
    else:
        out[...] = (block[0].astype(F32) + received[0][...].astype(F32)).astype(BF)


def reduce_end_body(spot, block, mine, near, out):
    out[...] = (block[0].astype(F32) + mine[...].astype(F32) + near[...].astype(F32)).astype(BF)


def rows_place_body(first, elements, spot, *refs):
    use = (0, 1, 2, 4, 5) if first else (3, 6, 7, 8)
    arrays, refs = refs[: len(use)], refs[len(use) :]
    if first:
        w_hidden, *outs, sums_out, tail_out, staged, sems = refs
    else:
        (w_hidden, gain, sums_in, tail_in), refs = refs[:4], refs[4:]
        outs, (gain_out, means_out, staged, sums, sems) = refs[3:6], refs[6:]
        sums[...] = sums_in[...]
        sums_out = sums
    rows = staged.shape[2]
    half, model = w_hidden.shape
    if first:
        sums_out[...] = jnp.zeros_like(sums_out)
    tail = jnp.zeros((8, 128), F32)
    positions = ring_positions(spot)
    copies = []
    for at, ref in zip(use, arrays):
        block = ref[...].astype(F32)
        place = pl.ds(pl.multiple_of(positions[min(at, 7)] * rows, 16), rows)
        core = spot[1] if at == 7 else 1 - spot[1]
        width = block.shape[1]
        lanes = pl.ds(pl.multiple_of(core * width, 128), width) if at >= 7 else pl.ds(0, width)
        slot = at % 4 if first else min(use.index(at), 2)
        stage = {0: 0, 1: 1, 2: 2, 4: 3, 5: 4}[at] if first else slot
        for w in range(3):
            staged[stage, w, :, lanes] = block[w * rows : (w + 1) * rows]
        total = jnp.zeros((rows, 128), F32)
        weight = w_hidden[place, lanes].astype(F32)
        for c in range(0, width, 128):
            total = total + block[rows : 2 * rows, c : c + 128] * weight[:, c : c + 128]
        sums_out[place] = sums_out[place] + total
        extra = block[3 * rows : 3 * rows + 8, :128]
        tail = tail + (extra if at < 7 else jnp.where(core == 0, extra, 0.0))
        if at != 7:
            for w in range(3):
                copy = pltpu.make_async_copy(staged.at[stage, w], outs[w].at[place], sems.at[stage, w])
                copy.start()
                copies.append(copy)
    if first:
        tail_out[...] = tail
    else:
        tail = tail + tail_in[...]
        means_out[...] = jnp.sqrt((tail[0:1, :2] + tail[1:2, :2]) / elements).reshape(2)
        line = jnp.sum(sums[...].T, axis=0, keepdims=True) / line_of(gain)
        gain_out[...] = line.reshape(half)
    for copy in copies:
        copy.wait()


def inputs_grad_body(spot, block, mine, near, x_in, dy_in, gains, out):
    size = out.shape[0]
    rows = pl.ds(pl.multiple_of(spot[1] * size, 16), size)
    d_norm = block[0, rows].astype(F32) + mine[rows].astype(F32) + near[rows].astype(F32)
    x = x_in[...].astype(F32)
    inv = lax.rsqrt(jnp.mean(x * x, axis=-1, keepdims=True) + EPSILON)
    unit = x * inv
    c1 = d_norm * gains[0:1]
    dx = inv * (c1 - unit * jnp.mean(c1 * unit, axis=-1, keepdims=True)) + dy_in[...]
    out[...] = dx.astype(BF)


def per_device(
    ctx_count,
    stream_in,
    pairing,
    w_query,
    w_key,
    w_value,
    w_output,
    w_hidden,
    w_return,
    gain_attn,
    gain_mlp,
    query_scale,
    cotangent,
):
    sequences, dev_rows, model = stream_in.shape
    half = w_query.shape[0]
    quarter = half // 2
    groups = ctx_count // GROUP
    blocks = 2 * ctx_count
    chunks = blocks // 4
    ctx = lax.axis_index("ctx")
    f = lax.axis_index("fsdp")
    head = ctx % GROUP
    k = head % 2

    def ring(a, shift):
        pairs = [
            (
                g * GROUP + RING[i] * 2 + core,
                g * GROUP + RING[(i + shift) % CHIPS] * 2 + core,
            )
            for g in range(groups)
            for i in range(CHIPS)
            for core in range(2)
        ]
        return lax.ppermute(a, "ctx", pairs)

    def ring_by_core(a):
        pairs = [
            (
                g * GROUP + RING[i] * 2 + core,
                g * GROUP + RING[(i + 1 - 2 * core) % CHIPS] * 2 + core,
            )
            for g in range(groups)
            for i in range(CHIPS)
            for core in range(2)
        ]
        return lax.ppermute(a, "ctx", pairs)

    def swap_core(a):
        return lax.ppermute(a, "ctx", [(c, c ^ 1) for c in range(ctx_count)])

    def swap_far(a):
        pairs = [
            (2 * c + side, 2 * (c ^ 1) + 1 - side) for c in range(ctx_count) for side in range(2)
        ]
        return lax.ppermute(a, ("ctx", "fsdp"), pairs)

    def swap_x(a):
        return lax.ppermute(a, "fsdp", [(0, 1), (1, 0)])

    def turn_groups(a, by):
        return lax.ppermute(
            a, "ctx", [(c, (c + by * GROUP) % ctx_count) for c in range(ctx_count)]
        )

    def sum_groups(a, kind):
        total = a
        for by in range(1, groups):
            total = total + turn_groups(a.astype(kind), by).astype(a.dtype)
        return total

    def exchange(a):
        which = (
            None
            if groups == 1
            else [[g * GROUP + h for h in range(GROUP)] for g in range(groups)]
        )
        return lax.all_to_all(a, "ctx", 0, 0, axis_index_groups=which, tiled=True)

    def swap_cores(arrays):
        swapped = []
        for a in arrays:
            swapped.append(swap_core(a))
        return swapped

    def ring_step(up, down):
        return ring(up, 1), ring(down, -1)

    source = jnp.asarray(SOURCE, jnp.int32)[head]
    place = jnp.asarray(PLACE, jnp.int32)[head]
    chip = head // 2
    ring_at = jnp.where(chip % 2 == 0, chip // 2, CHIPS - 1 - chip // 2)
    spot = jnp.stack([f, k, ring_at, head]).astype(jnp.int32)
    group = ctx // GROUP

    def pairs_of(which):
        return lax.dynamic_slice_in_dim(pairing, which * GROUP, GROUP, 0)

    def slots_of(pairs):
        return jnp.stack([pairs, blocks - 1 - pairs], axis=1).astype(jnp.int32)

    my_pairs = pairs_of(group)
    slots_ctx = slots_of(my_pairs)
    slots_ring = slots_ctx[source]
    if groups == 1:
        ids = np.arange(2 * GROUP, dtype=np.int32)
        slots_q, slots_out = slots_ring, slots_ctx
        slots_k = slots_ring
    else:
        flat = slots_ctx.reshape(-1)
        rank = jnp.sum((flat[None, :] < flat[:, None]).astype(jnp.int32), axis=1)
        ids = jnp.sum(
            jnp.where(rank[None, :] == jnp.arange(2 * GROUP)[:, None], flat[None, :], 0), axis=1
        ).astype(jnp.int32)
        slots_out = rank.reshape(GROUP, 2).astype(jnp.int32)
        slots_q = slots_out[source]
        slots_k = jnp.concatenate(
            [slots_of(pairs_of((group - by) % groups))[source] for by in range(groups)], axis=0
        )
    tiles, width = (4, 512) if groups == 1 else (8, 256)
    by_tile = ids.reshape(tiles, width // 64)
    full = jnp.asarray((by_tile[:, 0] + 1) // 4, jnp.int32)
    total = jnp.asarray(by_tile[:, -1] // 4 + 1, jnp.int32)
    every = np.arange(chunks)[:, None]
    begin = (total[None, :] <= every).sum(axis=1).astype(jnp.int32)
    clear = (full[None, :] <= every).sum(axis=1).astype(jnp.int32)
    qblock = jnp.asarray(ids.repeat(64).reshape(tiles, 1, width), jnp.int32)
    if groups == 1:
        full, total, begin, clear = [
            jnp.asarray(a, jnp.int32)
            for a in (
                (by_tile[:, 0] + 1) // 4,
                by_tile[:, -1] // 4 + 1,
                (by_tile[None, :, -1] // 4 + 1 <= every).sum(axis=1),
                ((by_tile[None, :, 0] + 1) // 4 <= every).sum(axis=1),
            )
        ]

    any_spec = pl.BlockSpec(memory_space=pl.ANY)
    vmem_spec = pl.BlockSpec(memory_space=pltpu.VMEM)
    x = stream_in.reshape(dev_rows, model)
    g_rows = cotangent.reshape(dev_rows, model)
    last = model // 128 - 1

    def columns(more):
        def at(i, spot):
            return (0, jnp.minimum(spot[3] * HD // 128 + more, last))

        return pl.BlockSpec((half, 128), at)

    def whole(shape):
        return pl.BlockSpec(shape, lambda i, spot: (0,) * len(shape))

    part = query_scale.shape[0]
    def gates(arrays, after):
        return call(
            lambda *refs: None,
            [(a.shape, a.dtype) for a in arrays],
            arrays,
            specs=[any_spec] * len(arrays),
            out_specs=[any_spec] * len(arrays),
            after=after,
            aliases={at: at for at in range(len(arrays))},
            name="gate",
        mib=1,
        us=0.1,
        )

    def gate(a, after):
        return gates([a], after)[0]

    steps = [(x,), ring_step(x, x)]
    for _ in range(2):
        steps.append(ring_step(*steps[-1]))
    early = quarter // 5 * 2
    out_xs = [swap_x(lax.dynamic_slice_in_dim(w_output, k * quarter, early, 0))]
    (slab,) = call(
        slab_body,
        [((3 * HD + 16, half), BF)],
        [
            spot,
            *[w for w in (w_query, w_key, w_value) for _ in range(2)],
            gain_attn,
            gain_mlp,
            query_scale,
        ],
        specs=[columns(0), columns(1)] * 3
        + [pl.BlockSpec((n,), lambda i, spot: (0,)) for n in (half, half, part)],
        out_specs=[whole((3 * HD + 16, half))],
        scratch=[pltpu.VMEM((256, half), F32)],
        smem=1,
        grid=(1,),
        name="slab",
        us=3,
        mib=60,
    )
    slab_x = swap_x(slab)
    late = lax.dynamic_slice_in_dim(w_output, k * quarter + early, quarter - early, 0)
    out_xs.append(swap_x(gate(late, [slab_x])))
    weight_t, gains, scale_col, scale_row = call(
        setup_body,
        [((3 * HD, model), BF), ((8, model), F32), ((HD, 1), F32), ((8, 128), F32)],
        [spot, slab, slab_x],
        smem=1,
        after=[*steps[2], *out_xs[:1]],
        name="setup",
        mib=6,
        us=2,
    )
    weight_sib = swap_core(weight_t)

    norms = None
    queries, keys, far_keys, near = [], [], [], []
    norms = None
    slot = 0
    for step in range(2):
        if step:
            up, down = gates(steps[3], queries)
            arrays = [up, down, *ring_step(up[: dev_rows // 2], down[dev_rows // 2 :])]
        else:
            arrays = [x, *steps[1], *steps[2]]
        count = sum(a.shape[0] for a in arrays) // dev_rows
        moved = (w_hidden, w_return) if step else ()
        outs = [((CHIPS, dev_rows, model), BF)]
        outs += [((count, HD, 128), BF), ((count, 2 * HD, 128), BF)]
        outs += [((count, 3 * HD, 128), BF), ((count, 2 * HD, 128), BF)]
        outs += [((quarter, model), BF)] * len(moved)
        ins = [spot, *arrays, gains, weight_t, weight_sib, scale_col, *moved]
        ins += [norms] if step else []
        norms, q_part, kv_part, near_part, far_part, *moved_parts = call(
            functools.partial(project_body, (len(arrays), count, len(moved), slot)),
            outs,
            ins,
            specs=[vmem_spec] * (len(arrays) + 4) + [any_spec] * (len(moved) + bool(step)),
            out_specs=[any_spec] + [vmem_spec] * (len(outs) - 1),
            scratch=[
                pltpu.VMEM((count, dev_rows, model), BF),
                pltpu.SemaphoreType.DMA((max(1, len(moved)),)),
                pltpu.SemaphoreType.DMA,
            ],
            smem=1,
            after=[(), out_xs[1:]][step],
            aliases={len(ins) - 1: 0} if step else None,
            name="project",
            us=[3, 3][step],
            mib=60,
        )
        slot += count
        queries.append(q_part)
        keys.append(kv_part)
        far_keys += [swap_x(kv_part), swap_far(far_part)]
        near.append(swap_core(near_part))
    hid_part, ret_part = moved_parts
    norms_sib = swap_core(norms)
    parts = [w_output]
    for out_x in out_xs:
        out_x = gate(out_x, [norms])
        parts += [out_x, swap_core(out_x)]
    hid_x = swap_x(gate(hid_part, far_keys))
    ret_x = swap_x(gate(ret_part, far_keys))

    arrays, places = [], []
    at = 0
    for step, q_part in enumerate(queries):
        mine, theirs = (q_part, keys[step], far_keys[2 * step]), (near[step], far_keys[2 * step + 1])
        count = q_part.shape[0]
        for entries, blocks_of in ((OWN_ENTRIES, mine), (SIB_ENTRIES, theirs)):
            for j in range(count):
                entry = entries[at + j]
                last = len(arrays) + len(blocks_of) - 1
                places.append(("q", len(arrays), j, entry, 0))
                places.append(("kv", last - 1, j, entry, 0))
                places.append(("kv", last, j, entry, 1))
            arrays += blocks_of
        at += count
    if groups > 1:
        order = OWN_ENTRIES + SIB_ENTRIES
        mine = jnp.concatenate([*keys, *[a[:, HD:] for a in near]], axis=0)
        theirs = jnp.concatenate([*far_keys[::2], *far_keys[1::2]], axis=0)
        for by in range(1, groups):
            for side, a in enumerate((mine, theirs)):
                places += [
                    ("kv", len(arrays), j, by * GROUP + order[j], side) for j in range(GROUP)
                ]
                arrays.append(turn_groups(a, by))
    pieces, q_t, k_t, k_rows, v_rows, att, lse = call(
        functools.partial(forward_body, {"arrays": len(arrays), "blocks": places}, chunks),
        [
            ((GROUP, HD, 128), BF),
            ((tiles, HD, width), BF),
            ((chunks, HD, 512), BF),
            ((chunks, 512, HD), BF),
            ((chunks, 512, HD), BF),
            ((tiles, HD, width), F32),
            ((tiles, 1, width), F32),
        ],
        [slots_q, slots_k, slots_out, full, total, qblock, *arrays],
        scratch=[
            pltpu.VMEM((2 * GROUP, HD, 64), BF),
            pltpu.VMEM((2, blocks, 2 * HD, 64), BF),
            pltpu.VMEM((chunks, HD + 16, 512), BF),
            pltpu.VMEM((chunks, 512, width), F32),
            pltpu.VMEM((2 * GROUP, HD, 64), BF),
        ],
        smem=5,
        name="attention_forward",
        us=20,
        mib=60,
    )
    (pieces,) = gates([pieces], [parts[2], parts[4]])
    att_t = exchange(pieces).reshape(model, dev_rows)
    hid_x, ret_x = gates([hid_x, ret_x], [att_t])
    for w, first in ((w_hidden, hid_x), (w_return, ret_x)):
        parts += [w, first, swap_core(first)]

    g_sib, g_x = swap_core(g_rows), swap_x(gate(g_rows, [pieces]))

    left_rows = 15 * (half // CHIPS)
    share_rows = left_rows + 2 * (model // 128) * dev_rows + 16
    stream, dy, datt_t, f_own, f_sib, f_x, f_xs = call(
        rows_body,
        [
            ((dev_rows, model), BF),
            ((dev_rows, model), F32),
            ((model, dev_rows), BF),
            ((share_rows, 128), BF),
            ((share_rows, 128), BF),
            ((share_rows, 128), BF),
            ((left_rows, 128), BF),
        ],
        [spot, att_t, x, g_rows, gains, *parts],
        specs=[vmem_spec] * 4 + [any_spec] * 11,
        scratch=[pltpu.VMEM((model, model), BF)] * 3
        + [pltpu.VMEM((3, model, dev_rows), BF), pltpu.SemaphoreType.DMA((3, 5))],
        smem=1,
        name="row_part",
        mib=60,
        us=10,
    )
    datt_t, g_x = gates([datt_t, g_x], ())
    grads = exchange(datt_t.reshape(GROUP, HD, dev_rows))
    g_xs = swap_core(g_x)

    from_x = swap_x(f_x)
    forward = swap_core(f_xs)
    from_sib, from_xs = swap_core(f_sib), swap_x(forward)

    def chunk_call(table, body, chunk, ins, outs, name, after):
        return call(
            body,
            outs,
            [spot, table, *ins],
            specs=[pl.BlockSpec((1, 256, model), lambda i, spot: (chunk, 0, 0))]
            + [whole(a.shape) for a in ins],
            out_specs=[whole(shape) for shape, _ in outs],
            smem=1,
            grid=(1,),
            after=after,
            name=name,
            us=2,
            mib=16,
        )

    def reduce_step(table, step, received, after):
        outs = chunk_call(
            table,
            functools.partial(reduce_step_body, step),
            4 - step,
            received,
            [((256, model if step else model // 2), BF)],
            "reduce_step",
            after,
        )
        return [ring_by_core(outs[0])], outs

    own, other, dq_pieces, scale_sum = call(
        backward_body,
        [
            ((chunks, 2 * HD, 256), F32),
            ((chunks, 2 * HD, 256), BF),
            ((GROUP, HD, 128), BF),
            ((HD, width), F32),
        ],
        [slots_out, begin, clear, qblock, scale_col, grads, q_t, att, lse, k_t, k_rows, v_rows],
        specs=[vmem_spec] * 6 + [any_spec] * 3,
        scratch=[
            pltpu.VMEM((tiles, HD, width), BF),
            pltpu.VMEM((tiles, 1, width), F32),
            pltpu.VMEM((tiles, HD, width), F32),
            pltpu.VMEM((2 * GROUP, HD, 64), BF),
            pltpu.VMEM((chunks, HD, 512), BF),
            pltpu.VMEM((chunks, 512, HD), BF),
            pltpu.VMEM((chunks, 512, HD), BF),
            pltpu.SemaphoreType.DMA((3,)),
        ],
        smem=3,
        after=[forward],
        name="attention_backward",
        us=25,
        mib=60,
    )
    other_x = swap_x(other)
    from_x, from_sib, from_xs, g_xs, norms_sib = gates(
        [from_x, from_sib, from_xs, g_xs, norms_sib], [own]
    )
    (partial,) = call(
        pooled_grad_body,
        [((5, 256, model), BF)],
        [f_own, from_sib, from_x, from_xs, swap_core(from_x), g_rows, g_sib, g_x, g_xs],
        name="pooled_grads",
        us=3,
        mib=24,
    )
    received, done = reduce_step(partial, 0, (), ())
    if groups > 1:
        own = sum_groups(own + other_x.astype(F32), BF)
        other_x = jnp.zeros_like(other_x)
    received, done = reduce_step(partial, 1, received, ())
    d_pieces, d_other = call(
        join_body,
        [((GROUP, 3 * HD, 128), BF), ((10, 3 * HD, 128), BF)],
        [slots_ctx, spot, dq_pieces, own, other_x],
        scratch=[pltpu.VMEM((blocks, 2 * HD, 64), BF)],
        smem=2,
        after=done,
        name="join",
        us=2,
        mib=24 if groups == 1 else 60,
    )
    d_near = swap_core(d_other)
    own_share, other_share = call(
        qkv_grad_body,
        [((3 * HD + 16, half), F32), ((3 * HD + 16, half), BF)],
        [place, spot, d_pieces, scale_sum, norms, norms_sib],
        scratch=[pltpu.VMEM((3 * HD, model), F32)],
        smem=2,
        name="qkv_grads",
        us=4.7,
        mib=24,
    )
    share_x = swap_x(other_share)
    received, done = reduce_step(partial, 2, received, [own_share])

    (table,) = call(
        products_body,
        [((5, 256, model), BF)],
        [spot, d_pieces, d_near, weight_t, weight_sib],
        smem=1,
        after=done,
        name="products",
        us=4,
        mib=24,
    )
    first, done = reduce_step(table, 0, (), ())
    (share,) = call(
        qkv_sum_body,
        [((3 * HD + 16, half), BF)],
        [own_share, share_x, slab],
        after=done,
        name="qkv_sum",
        us=1,
        mib=8,
    )
    share = sum_groups(share.astype(F32), BF).astype(BF) if groups > 1 else share
    share_near = swap_core(share)
    received, done = reduce_step(partial, 3, received, [share])
    received_near = swap_core(received[0])
    (chip_share,) = call(
        chip_pack_body,
        [((2 * (3 * HD + 16), half), BF)],
        [spot, share, share_near],
        smem=1,
        after=done,
        name="chip_pack",
        us=1,
        mib=8,
    )
    q_steps = [chip_share, ring_by_core(chip_share)]
    first, done = reduce_step(table, 1, first, [chip_share])
    (mine,) = chunk_call(
        partial,
        reduce_end_body,
        0,
        (*received, received_near),
        [((256, model), BF)],
        "reduce_end",
        [chip_share],
    )
    first, done = reduce_step(table, 2, first, [mine])
    mine = sum_groups(mine.astype(F32), BF).astype(BF) if groups > 1 else mine
    m_steps = [mine, ring_by_core(mine)]
    q_steps.append(ring_by_core(q_steps[-1]))
    first, done = reduce_step(table, 3, first, [*done, q_steps[2]])
    m_steps.append(ring_by_core(m_steps[-1]))
    q_steps.append(ring_by_core(q_steps[-1]))
    m_steps.append(ring_by_core(m_steps[-1]))
    q_near = [swap_core(a) for a in q_steps[1:3]]
    m_near = [swap_core(a) for a in m_steps[1:3]]
    elements = float(ctx_count * 2 * dev_rows * model)
    chunk = half // CHIPS
    grads_shape = [((half, model), F32)] * 3
    *rows_grads, gain_sums, tails = call(
        functools.partial(rows_place_body, True, elements),
        [*grads_shape, ((half, 128), F32), ((8, 128), F32)],
        [spot, *m_steps[:3], *m_near, w_hidden],
        out_specs=[any_spec] * 3 + [vmem_spec] * 2,
        scratch=[pltpu.VMEM((5, 3, chunk, model), F32), pltpu.SemaphoreType.DMA((5, 3))],
        smem=1,
        name="rows_place",
        us=4,
        mib=40,
    )

    first_near = swap_core(first[0])
    (d_in,) = chunk_call(
        table,
        inputs_grad_body,
        0,
        (*first, first_near, x, dy, gains),
        [((dev_rows, model), BF)],
        "inputs_grad",
        [m_steps[2], tails],
    )

    def last_step(a, axis):
        size = a.shape[axis] // 2
        return ring_by_core(lax.dynamic_slice_in_dim(a, k * size, size, axis))

    q_last = last_step(q_steps[-1], 0)
    m_held = m_steps[-1]
    m_last = last_step(m_held, 1)
    q_near += [swap_core(a) for a in q_steps[3:]]
    m_near += [swap_core(m_held)]
    grad_query, grad_key, grad_value, gain_one_grad, scale_grad = call(
        qkv_place_body,
        [((half, model), F32)] * 3 + [((half,), F32), ((part,), F32)],
        [spot, *q_steps, *q_near, q_last, swap_core(q_last), gain_attn, scale_row],
        scratch=[pltpu.VMEM((3, model, half), BF)],
        smem=1,
        name="qkv_place",
        us=6,
        mib=40,
    )
    (m_last,) = gates([m_last], [grad_query, d_in])
    ins = [spot, m_held, m_near[2], m_last, swap_core(m_last), w_hidden, gain_mlp, gain_sums, tails]
    grad_output, grad_hidden, grad_return, gain_two_grad, root_means = call(
        functools.partial(rows_place_body, False, elements),
        [*grads_shape, ((half,), F32), ((2,), F32)],
        [*ins, *rows_grads],
        specs=[vmem_spec] * (len(ins) - 1) + [any_spec] * 3,
        out_specs=[any_spec] * 3 + [vmem_spec] * 2,
        scratch=[
            pltpu.VMEM((3, 3, chunk, model), F32),
            pltpu.VMEM((half, 128), F32),
            pltpu.SemaphoreType.DMA((3, 3)),
        ],
        smem=1,
        aliases={len(ins) + at: at for at in range(3)},
        name="rows_place",
        us=3,
        mib=40,
    )
    return (
        stream.reshape(stream_in.shape),
        d_in.reshape(stream_in.shape),
        grad_query,
        grad_key,
        grad_value,
        grad_output,
        grad_hidden,
        grad_return,
        gain_one_grad,
        gain_two_grad,
        scale_grad,
        root_means,
    )


def solution(mesh):
    rows = P(None, ("ctx", "fsdp"), None)
    weight, vector = P("fsdp", None), P("fsdp")
    return jax.shard_map(
        functools.partial(per_device, mesh.shape["ctx"]),
        mesh=mesh,
        in_specs=(rows, P(), *([weight] * 6), *([vector] * 3), rows),
        out_specs=(rows, rows, *([weight] * 6), *([vector] * 3), P()),
        check_vma=False,
    )
```

```python
import functools

import jax
import jax.numpy as jnp
import numpy as np
from jax import lax
from jax.experimental import pallas as pl
from jax.experimental.pallas import tpu as pltpu
from jax.sharding import PartitionSpec as P

H = 16
HD = 80
EPSILON = 1e-06
LOWEST = -1e30
BF = jnp.bfloat16
F32 = jnp.float32
MIB = 1024 * 1024
FLOPS_A_US = 1.15e9

GROUP = 16
CHIPS = 8
RING = (0, 2, 4, 6, 7, 5, 3, 1)
ORDER = (
    ((0, 0), (0, 1))
    + tuple((off, core) for s in (1, 2, 3) for core in (0, 1) for off in (-s, s))
    + ((4, 0), (4, 1))
)
SOURCE = [
    [RING[(RING.index(h // 2) + off) % CHIPS] * 2 + ((h % 2) ^ core) for off, core in ORDER]
    for h in range(GROUP)
]
PLACE = [
    [((h % 2) ^ core) * CHIPS + (RING.index(h // 2) + off) % CHIPS for off, core in ORDER]
    for h in range(GROUP)
]

OWN_ENTRIES = (0, 2, 3, 6, 7, 10, 11, 14)
SIB_ENTRIES = (1, 4, 5, 8, 9, 12, 13, 15)

NN = (((1,), (0,)), ((), ()))
NT = (((1,), (1,)), ((), ()))
TN = (((0,), (0,)), ((), ()))


def dot(a, b, dims):
    return lax.dot_general(a, b, dims, preferred_element_type=F32)


def call(body, outs, ins, scratch=(), specs=None, out_specs=None, name=None, smem=0, after=(), grid=None, aliases=None, us=1.0, mib=24):
    given = len(ins)
    waits = len(after)

    def run(*refs):
        body(*refs[:given], *refs[given + waits :])

    if specs is None:
        specs = [pl.BlockSpec(memory_space=pltpu.VMEM)] * (given - smem)
    specs = list(specs) + [pl.BlockSpec(memory_space=pl.ANY)] * waits
    out_specs = out_specs or [pl.BlockSpec(memory_space=pltpu.VMEM)] * len(outs)
    if grid is None:
        how = dict(
            in_specs=[pl.BlockSpec(memory_space=pltpu.SMEM)] * smem + specs,
            out_specs=out_specs,
            scratch_shapes=list(scratch),
        )
    else:
        how = dict(
            grid_spec=pltpu.PrefetchScalarGridSpec(
                num_scalar_prefetch=smem,
                grid=grid,
                in_specs=specs,
                out_specs=out_specs,
                scratch_shapes=list(scratch),
            )
        )
    return pl.pallas_call(
        run,
        out_shape=[jax.ShapeDtypeStruct(shape, kind) for shape, kind in outs],
        compiler_params=pltpu.CompilerParams(vmem_limit_bytes=mib * MIB),
        cost_estimate=pl.CostEstimate(flops=int(us * FLOPS_A_US), bytes_accessed=1, transcendentals=0),
        input_output_aliases=aliases or {},
        name=name,
        **how,
    )(*ins, *after)


def start_copies(jobs, sems):
    copies = []
    for at, (source, target) in enumerate(jobs):
        copy = pltpu.make_async_copy(source, target, sems.at[at])
        copy.start()
        copies.append(copy)
    return copies


def slab_body(spot, q0, q1, k0, k1, v0, v1, gain_one, gain_two, scale, out, turned):
    start = spot[3] * HD
    off = pl.multiple_of(start - start // 128 * 128, 16)
    for w, (left, right) in enumerate(((q0, q1), (k0, k1), (v0, v1))):
        turned[:128] = left[...].astype(F32).T
        turned[128:] = right[...].astype(F32).T
        out[w * HD : w * HD + HD] = turned[pl.ds(off, HD)].astype(BF)
    width = out.shape[1]
    part = scale.shape[0]
    line = jnp.concatenate([line_of(scale), jnp.zeros((1, width - part), F32)], axis=1)
    tail = [line_of(gain_one), line_of(gain_two), line, jnp.zeros((13, width), F32)]
    out[3 * HD :] = jnp.concatenate(tail, axis=0).astype(BF)


def line_of(vector):
    return vector[...].astype(F32).reshape(1, vector.shape[0])


def setup_body(spot, slab, slab_x, weight, gains, scale_col, scale_row):
    width = slab.shape[1]
    f = spot[0]
    mine, theirs = slab[...], slab_x[...]
    left = jnp.where(f == 0, mine, theirs)
    right = jnp.where(f == 0, theirs, mine)
    weight[:, :width] = left[: 3 * HD]
    weight[:, width:] = right[: 3 * HD]
    left, right = left[3 * HD :].astype(F32), right[3 * HD :].astype(F32)
    gains[...] = jnp.concatenate([left[:8], right[:8]], axis=1)
    part = HD // 2
    row = jnp.concatenate([left[2:3, :part], right[2:3, :part], jnp.zeros((1, 128 - HD), F32)], axis=1)
    row = jnp.broadcast_to(row, (128, 128))
    scale_row[...] = row[:8]
    scale_col[...] = row.T[:HD, :1] * HD ** (-0.5)


def project_body(layout, spot, *refs):
    count, pieces, carried, slot = layout
    xs, refs = refs[:count], refs[count:]
    (gains, weight, weight_sib, scale), refs = refs[:4], refs[4:]
    moved, refs = refs[:carried], refs[carried:]
    refs = refs if slot == 0 else refs[1:]
    (norm_out, q_out, kv_out, near_out, far_out), refs = refs[:5], refs[5:]
    outs, (norm_vmem, sems, norm_sem) = refs[:-3], refs[-3:]
    copies = []
    for w, out in zip(moved, outs):
        size = out.shape[0]
        rows = pl.ds(pl.multiple_of(spot[1] * size, 16), size)
        copies.append((w.at[rows], out))
    copies = start_copies(copies, sems)
    x = jnp.concatenate([r[...] for r in xs], axis=0).astype(F32)
    inv = lax.rsqrt(jnp.mean(x * x, axis=-1, keepdims=True) + EPSILON)
    norm = (x * inv * gains[0:1]).astype(BF)
    norm_vmem[...] = norm.reshape(norm_vmem.shape)
    keep = pltpu.make_async_copy(norm_vmem, norm_out.at[pl.ds(slot, pieces)], norm_sem)
    keep.start()
    for table, other in ((weight, False), (weight_sib, True)):
        out = dot(table[...], norm, NT)
        q = (out[:HD] * scale[...]).astype(BF)
        kv = out[HD:].astype(BF)
        for j in range(pieces):
            lanes = slice(j * 128, (j + 1) * 128)
            if other:
                near_out[j, :HD] = q[:, lanes]
                near_out[j, HD:] = kv[:, lanes]
                far_out[j] = kv[:, lanes]
            else:
                q_out[j] = q[:, lanes]
                kv_out[j] = kv[:, lanes]
    for copy in copies:
        copy.wait()
    keep.wait()


def forward_body(layout, chunks, slots_q, slots_k, slots_out, full, total, qblock, *refs):
    count = layout["arrays"]
    arrays, refs = refs[:count], refs[count:]
    (pieces, q_t, k_t, k_rows, v_rows, att, lse), refs = refs[:7], refs[7:]
    block_q, block_kv, v_t, scores, block_out = refs
    for kind, which, index, entry, side in layout["blocks"]:
        for half in range(2):
            lanes = slice(half * 64, half * 64 + 64)
            if kind == "q":
                block_q[slots_q[entry, half]] = arrays[which][index, :HD, lanes]
            else:
                value = arrays[which][index, :, lanes]
                block_kv[side, slots_k[entry, half]] = value[value.shape[0] - 2 * HD :]
    rows = 2 * 256
    ones_row = jnp.where(lax.broadcasted_iota(jnp.int32, (16, rows), 0) == 0, 1.0, 0.0).astype(BF)

    @pl.loop(0, chunks)
    def _(c):
        tile = jnp.concatenate(
            [block_kv[side, 4 * c + m] for side in range(2) for m in range(4)], axis=1
        )
        k_t[c] = tile[:HD]
        k_rows[c] = tile[:HD].astype(F32).T.astype(BF)
        v_rows[c] = tile[HD:].astype(F32).T.astype(BF)
        v_t[c] = jnp.concatenate([tile[HD:], ones_row], axis=0)

    width = q_t.shape[2]
    per = width // 64

    @pl.loop(0, q_t.shape[0])
    def _(i):
        query = jnp.concatenate([block_q[per * i + m] for m in range(per)], axis=1)
        q_t[i] = query
        ids = qblock[i]

        def scan_max(masked, c, top):
            s = dot(k_rows[c], query, NN)
            if masked:
                s = jnp.where(block_of_row(width) + 4 * c <= ids, s, LOWEST)
            scores[c] = s
            return jnp.maximum(top, jnp.max(s.reshape(rows // 8, 8, width), axis=0))

        top = jnp.full((8, width), LOWEST, F32)
        top = lax.fori_loop(0, full[i], functools.partial(scan_max, False), top)
        top = lax.fori_loop(full[i], total[i], functools.partial(scan_max, True), top)
        top = jnp.max(top, axis=0, keepdims=True)

        def gather(c, acc):
            w = jnp.exp(scores[c] - top).astype(BF)
            return acc + dot(v_t[c], w, NN)

        acc = lax.fori_loop(0, total[i], gather, jnp.zeros((HD + 16, width), F32))
        sums = acc[HD : HD + 1]
        out = acc[:HD] / sums
        att[i] = out
        lse[i] = top + jnp.log(sums)
        low = out.astype(BF)
        for m in range(per):
            block_out[per * i + m] = low[:, m * 64 : m * 64 + 64]

    for c in range(GROUP):
        pieces[c] = jnp.concatenate(
            [block_out[slots_out[c, 0]], block_out[slots_out[c, 1]]], axis=1
        )


def block_of_row(width):
    return lax.broadcasted_iota(jnp.int32, (512, width), 0) % 256 // 64


def backward_body(
    slots_out,
    begin,
    clear,
    qblock,
    scale,
    grads,
    q_t,
    att,
    lse,
    k_t_in,
    k_rows_in,
    v_rows_in,
    dkv_own,
    dkv_other,
    dq_pieces,
    scale_sum,
    grad_t,
    delta,
    dq,
    blocks,
    k_t,
    k_rows,
    v_rows,
    sems,
):
    copies = start_copies([(k_t_in, k_t), (k_rows_in, k_rows), (v_rows_in, v_rows)], sems)
    tiles, _, width = q_t.shape
    per = width // 64
    for c in range(GROUP):
        for half in range(2):
            blocks[slots_out[c, half]] = grads[c, :, half * 64 : half * 64 + 64]

    @pl.loop(0, tiles)
    def _(i):
        grad = jnp.concatenate([blocks[per * i + m] for m in range(per)], axis=1)
        grad_t[i] = grad
        delta[i] = jnp.sum(grad.astype(F32) * att[i], axis=0, keepdims=True)
        dq[i] = jnp.zeros((HD, width), F32)

    for copy in copies:
        copy.wait()

    @pl.loop(0, k_t.shape[0])
    def _(c):
        def step(masked, i, carry):
            d_k, d_v = carry
            query, grad = q_t[i], grad_t[i]
            prob = jnp.exp(dot(k_rows[c], query, NN) - lse[i])
            if masked:
                prob = jnp.where(block_of_row(width) + 4 * c <= qblock[i], prob, 0.0)
            d_score = (prob * (dot(v_rows[c], grad, NN) - delta[i])).astype(BF)
            dq[i] += dot(k_t[c], d_score, NN)
            return d_k + dot(query, d_score, NT), d_v + dot(grad, prob.astype(BF), NT)

        carry = (jnp.zeros((HD, 512), F32), jnp.zeros((HD, 512), F32))
        carry = lax.fori_loop(begin[c], clear[c], functools.partial(step, True), carry)
        d_k, d_v = lax.fori_loop(clear[c], tiles, functools.partial(step, False), carry)
        dkv_own[c, :HD] = d_k[:, :256]
        dkv_own[c, HD:] = d_v[:, :256]
        dkv_other[c, :HD] = d_k[:, 256:].astype(BF)
        dkv_other[c, HD:] = d_v[:, 256:].astype(BF)

    total = jnp.zeros((HD, width), F32)
    for i in range(tiles):
        total = total + dq[i] * q_t[i].astype(F32)
        rounded = (dq[i] * scale[...]).astype(BF)
        for m in range(per):
            blocks[per * i + m] = rounded[:, m * 64 : m * 64 + 64]
    scale_sum[...] = total
    for c in range(GROUP):
        dq_pieces[c] = jnp.concatenate(
            [blocks[slots_out[c, 0]], blocks[slots_out[c, 1]]], axis=1
        )


def join_body(slots_kv, spot, dq_pieces, own, received, pieces, other, blocks):
    @pl.loop(0, own.shape[0])
    def _(c):
        tile = (own[c] + received[c].astype(F32)).astype(BF)
        for m in range(4):
            blocks[4 * c + m] = tile[:, m * 64 : m * 64 + 64]

    for p in range(CHIPS):
        for core in range(2):
            c = RING[p] * 2 + core
            pieces[2 * p + core, :HD] = dq_pieces[c]
            pieces[2 * p + core, HD:] = jnp.concatenate(
                [blocks[slots_kv[c, 0]], blocks[slots_kv[c, 1]]], axis=1
            )
    sign = 1 - 2 * spot[1]
    for j in range(5):
        pos = lax.rem(spot[2] + CHIPS - sign * j, CHIPS)
        for core in range(2):
            other[2 * j + core] = pieces[2 * pos + core]


def products_body(spot, pieces, near, weight, weight_sib, out):
    sign = 1 - 2 * spot[1]
    for j in range(5):
        pos = lax.rem(spot[2] + CHIPS + sign * j, CHIPS)
        for core in range(2):
            total = dot(pieces[2 * pos + core], weight[...], TN)
            total = total + dot(near[2 * j + core], weight_sib[...], TN)
            out[j, core * 128 : core * 128 + 128] = total.astype(BF)


def qkv_grad_body(place, spot, pieces, scale_sum, *refs):
    norms, (own, other, table) = refs[:-3], refs[-3:]
    total = jnp.zeros((3 * HD, table.shape[1]), F32)
    for norm, entries in zip(norms, (OWN_ENTRIES, SIB_ENTRIES)):
        for j, entry in enumerate(entries):
            at = 2 * lax.rem(place[entry], CHIPS) + place[entry] // CHIPS
            total = total + dot(pieces[at], norm[j], NN)
    table[...] = total
    width = table.shape[1] // 2
    f = spot[0]
    own[: 3 * HD] = table[:, pl.ds(pl.multiple_of(f * width, 128), width)]
    other[: 3 * HD] = table[:, pl.ds(pl.multiple_of((1 - f) * width, 128), width)].astype(BF)
    column = jnp.broadcast_to(jnp.sum(scale_sum[...], axis=1, keepdims=True), (HD, 128))
    line = column.T[:1]
    high = line.astype(BF)
    low = (line - high.astype(F32)).astype(BF)
    own[3 * HD :] = jnp.zeros((16, width), F32)
    own[3 * HD : 3 * HD + 1, :HD] = line
    tail = jnp.concatenate([high.astype(F32), low.astype(F32), jnp.zeros((14, HD), F32)], axis=0)
    other[3 * HD :] = jnp.concatenate([tail, jnp.zeros((16, width - HD), F32)], axis=1).astype(BF)


def qkv_sum_body(own, received, slab, out):
    width = own.shape[1]
    total = own[: 3 * HD] + received[: 3 * HD].astype(F32)
    out[: 3 * HD] = total.astype(BF)
    gain = jnp.sum(total * slab[: 3 * HD].astype(F32), axis=0, keepdims=True)
    tail = received[3 * HD :].astype(F32)
    line = own[3 * HD : 3 * HD + 1] + tail[0:1] + tail[1:2]
    rows = []
    for value in (gain, line):
        high = value.astype(BF).astype(F32)
        rows += [high, value - high]
    out[3 * HD :] = jnp.concatenate(rows + [jnp.zeros((12, width), F32)], axis=0).astype(BF)


def chip_pack_body(spot, own, near, out):
    rows = own.shape[0]
    out[pl.ds(pl.multiple_of(spot[1] * rows, 16), rows)] = own[...]
    out[pl.ds(pl.multiple_of((1 - spot[1]) * rows, 16), rows)] = near[...]


def ring_positions(spot):
    sign = 1 - 2 * spot[1]
    offsets = [0] + [-sign * s for s in (1, 2, 3)] + [sign * s for s in (1, 2, 3)] + [4]
    return [lax.rem(spot[2] + CHIPS + off, CHIPS) for off in offsets]


def qkv_place_body(spot, *refs):
    arrays, (gain, scale_row), refs = refs[:9], refs[9:11], refs[11:]
    outs, (gain_out, scale_out, table) = refs[:3], refs[3:]
    width = gain.shape[0]
    size = 3 * HD + 16
    tail = jnp.zeros((16, width), F32)
    positions = ring_positions(spot)
    blocks = [(arrays[at], c * size, positions[at], c) for at in range(7) for c in range(2)]
    blocks += [(arrays[7], 0, positions[7], spot[1]), (arrays[8], 0, positions[7], 1 - spot[1])]
    for ref, row, pos, core in blocks:
        chip = jnp.where(pos < 4, 2 * pos, 15 - 2 * pos)
        head = pl.multiple_of((2 * chip + core) * HD, 16)
        for w in range(3):
            table[w, pl.ds(head, HD)] = ref[row + w * HD : row + w * HD + HD]
        tail = tail + ref[row + 3 * HD : row + size].astype(F32)
    for w in range(3):
        for at in range(0, H * HD, 256):
            outs[w][:, at : at + 256] = table[w, at : at + 256].astype(F32).T
    gain_out[...] = ((tail[0:1] + tail[1:2]) / line_of(gain)).reshape(width)
    scale = (tail[2:3, :128] + tail[3:4, :128]) / scale_row[0:1]
    part = scale_out.shape[0]
    chosen = jnp.where(spot[0] == 0, scale[:, :part], scale[:, part : 2 * part])
    scale_out[...] = chosen.reshape(part)


def rows_body(
    spot,
    att_t,
    x_in,
    g_in,
    gain_in,
    *refs,
):
    weights = (refs[:5], refs[5:8], refs[8:11])
    refs = refs[11:]
    (stream_out, dy_out, datt_out), outs = refs[:3], refs[3:7]
    full = refs[7:10]
    turned, sems = refs[10:]
    f, k = spot[0], spot[1]
    half = weights[0][0].shape[0]
    quarter = half // 2
    early = weights[0][1].shape[0]
    places = [
        [k * quarter, (1 - k) * quarter, k * quarter + early, (1 - k) * quarter + early],
        *[[k * quarter, (1 - k) * quarter]] * 2,
    ]
    copies = []
    for w in range(3):
        mine, *theirs = weights[w]
        jobs = [(mine, full[w].at[pl.ds(pl.multiple_of(f * half, 16), half)])]
        for piece, start in zip(theirs, places[w]):
            rows = pl.ds(pl.multiple_of((1 - f) * half + start, 16), piece.shape[0])
            jobs.append((piece, full[w].at[rows]))
        copies.append(start_copies(jobs, sems.at[w]))
    w_out, w_hid, w_ret = full
    x = x_in[...].astype(F32)
    gain = gain_in[1:2]
    for copy in copies[0]:
        copy.wait()
    attn = dot(att_t[...], w_out[...], TN)
    y1 = x + attn
    inv = lax.rsqrt(jnp.mean(y1 * y1, axis=-1, keepdims=True) + EPSILON)
    unit = y1 * inv
    norm = (unit * gain).astype(BF)
    for copy in copies[1]:
        copy.wait()
    h = dot(norm, w_hid[...], NN)
    sig = jax.nn.sigmoid(h)
    act = (h * sig).astype(BF)
    for copy in copies[2]:
        copy.wait()
    stream = y1 + dot(act, w_ret[...], NN)
    stream_out[...] = stream.astype(BF)
    squares = jnp.where(
        lax.broadcasted_iota(jnp.int32, (8, 128), 0) == 0,
        jnp.sum(stream * stream),
        jnp.sum(attn * attn),
    )
    g = g_in[...]
    d_act = dot(g, w_ret[...], NT)
    d_h = (d_act * sig * (1.0 + h * (1.0 - sig))).astype(BF)
    d_norm = dot(d_h, w_hid[...], NT)
    c2 = d_norm * gain
    dy = inv * (c2 - unit * jnp.mean(c2 * unit, axis=-1, keepdims=True)) + g.astype(F32)
    dy_out[...] = dy
    dy_b = dy.astype(BF)
    datt_out[...] = dot(w_out[...], dy_b, NT).astype(BF)
    turned[0] = att_t[...]
    turned[1] = norm.astype(F32).T.astype(BF)
    turned[2] = act.astype(F32).T.astype(BF)
    rows = x.shape[0]
    columns = x.shape[1] // 128
    chunk = half // CHIPS
    sign = 1 - 2 * k
    for ref, part, way in zip(outs, (f, f, 1 - f, 1 - f), (sign, -sign, sign, -sign)):
        for j in range(5):
            pos = lax.rem(spot[2] + CHIPS + way * j, CHIPS)
            at = pl.multiple_of(part * half + pos * chunk, 16)
            for w in range(3):
                start = (w * 5 + j) * chunk
                ref[start : start + chunk] = turned[w, pl.ds(at, chunk)]
    line = sums_line(squares)
    tail = jnp.concatenate([sums_tail(line, 128), jnp.zeros((8, 128), F32)], axis=0).astype(BF)
    for ref in outs[:3]:
        start = 15 * chunk
        for right in (dy_b, d_h):
            for c in range(columns):
                ref[start : start + rows] = right[:, c * 128 : (c + 1) * 128]
                start += rows
        ref[start : start + 16] = tail


def sums_tail(line, width):
    high = line.astype(BF).astype(F32)
    row = lax.broadcasted_iota(jnp.int32, (8, 128), 0)
    tail = jnp.where(row == 0, high, jnp.where(row == 1, line - high, 0.0))
    return tail if width == 128 else jnp.concatenate([tail, jnp.zeros((8, width - 128), F32)], axis=1)


def sums_line(sums):
    lane = lax.broadcasted_iota(jnp.int32, (1, 128), 1)
    return jnp.where(lane == 0, sums[0:1], jnp.where(lane == 1, sums[1:2], 0.0))


def pooled_grad_body(own, sib, far, far_left, far_right, *refs):
    gs, out = refs[:4], refs[4]
    model = out.shape[2]
    columns = model // 128
    group = far_left.shape[0] // 3
    chunk = group // 5
    rows = 128
    totals = []
    for w in range(3):
        lefts, rights = [], []
        for at, (left, right) in enumerate(
            ((own, own), (sib, sib), (far, far), (far_left, far_right))
        ):
            lefts.append(left[w * group : (w + 1) * group])
            start = 3 * group + w * columns * rows
            if w == 2:
                rights.append(gs[at][...])
                continue
            rights.append(
                jnp.concatenate(
                    [right[start + c * rows : start + (c + 1) * rows] for c in range(columns)], axis=1
                )
            )
        left, right = jnp.concatenate(lefts, axis=1), jnp.concatenate(rights, axis=0)
        totals.append(dot(left, right, NN))
    line = jnp.zeros((1, 128), F32)
    for ref in (own, sib, far, far_right):
        tail = ref[ref.shape[0] - 16 :].astype(F32)
        line = line + tail[0:1] + tail[1:2]
    for j in range(5):
        parts = [t[chunk * j : chunk * (j + 1)] for t in totals]
        tail = jnp.zeros((16, model), F32)
        if j == 0:
            tail = jnp.concatenate([sums_tail(line, model), tail[:8]], axis=0)
        out[j] = jnp.concatenate([*parts, tail], axis=0).astype(BF)


def reduce_step_body(step, spot, block, *refs):
    received, out = refs[:-1], refs[-1]
    half = block.shape[2] // 2
    near = pl.ds(pl.multiple_of(spot[1] * half, 128), half)
    if step == 0:
        out[...] = block[0, :, near]
    elif step == 1:
        out[...] = block[0]
        out[:, near] = (block[0, :, near].astype(F32) + received[0][...].astype(F32)).astype(BF)
    else:
        out[...] = (block[0].astype(F32) + received[0][...].astype(F32)).astype(BF)


def reduce_end_body(spot, block, mine, near, out):
    out[...] = (block[0].astype(F32) + mine[...].astype(F32) + near[...].astype(F32)).astype(BF)


def rows_place_body(first, elements, spot, *refs):
    use = (0, 1, 2, 4, 5) if first else (3, 6, 7, 8)
    arrays, refs = refs[: len(use)], refs[len(use) :]
    if first:
        w_hidden, *outs, sums_out, tail_out, staged, sems = refs
    else:
        (w_hidden, gain, sums_in, tail_in), refs = refs[:4], refs[4:]
        outs, (gain_out, means_out, staged, sums, sems) = refs[3:6], refs[6:]
        sums[...] = sums_in[...]
        sums_out = sums
    rows = staged.shape[2]
    half, model = w_hidden.shape
    if first:
        sums_out[...] = jnp.zeros_like(sums_out)
    tail = jnp.zeros((8, 128), F32)
    positions = ring_positions(spot)
    copies = []
    for at, ref in zip(use, arrays):
        block = ref[...].astype(F32)
        place = pl.ds(pl.multiple_of(positions[min(at, 7)] * rows, 16), rows)
        core = spot[1] if at == 7 else 1 - spot[1]
        width = block.shape[1]
        lanes = pl.ds(pl.multiple_of(core * width, 128), width) if at >= 7 else pl.ds(0, width)
        slot = at % 4 if first else min(use.index(at), 2)
        stage = {0: 0, 1: 1, 2: 2, 4: 3, 5: 4}[at] if first else slot
        for w in range(3):
            staged[stage, w, :, lanes] = block[w * rows : (w + 1) * rows]
        total = jnp.zeros((rows, 128), F32)
        weight = w_hidden[place, lanes].astype(F32)
        for c in range(0, width, 128):
            total = total + block[rows : 2 * rows, c : c + 128] * weight[:, c : c + 128]
        sums_out[place] = sums_out[place] + total
        extra = block[3 * rows : 3 * rows + 8, :128]
        tail = tail + (extra if at < 7 else jnp.where(core == 0, extra, 0.0))
        if at != 7:
            for w in range(3):
                copy = pltpu.make_async_copy(staged.at[stage, w], outs[w].at[place], sems.at[stage, w])
                copy.start()
                copies.append(copy)
    if first:
        tail_out[...] = tail
    else:
        tail = tail + tail_in[...]
        means_out[...] = jnp.sqrt((tail[0:1, :2] + tail[1:2, :2]) / elements).reshape(2)
        line = jnp.sum(sums[...].T, axis=0, keepdims=True) / line_of(gain)
        gain_out[...] = line.reshape(half)
    for copy in copies:
        copy.wait()


def inputs_grad_body(spot, block, mine, near, x_in, dy_in, gains, out):
    size = out.shape[0]
    rows = pl.ds(pl.multiple_of(spot[1] * size, 16), size)
    d_norm = block[0, rows].astype(F32) + mine[rows].astype(F32) + near[rows].astype(F32)
    x = x_in[...].astype(F32)
    inv = lax.rsqrt(jnp.mean(x * x, axis=-1, keepdims=True) + EPSILON)
    unit = x * inv
    c1 = d_norm * gains[0:1]
    dx = inv * (c1 - unit * jnp.mean(c1 * unit, axis=-1, keepdims=True)) + dy_in[...]
    out[...] = dx.astype(BF)


def per_device(
    ctx_count,
    stream_in,
    pairing,
    w_query,
    w_key,
    w_value,
    w_output,
    w_hidden,
    w_return,
    gain_attn,
    gain_mlp,
    query_scale,
    cotangent,
):
    sequences, dev_rows, model = stream_in.shape
    half = w_query.shape[0]
    quarter = half // 2
    groups = ctx_count // GROUP
    blocks = 2 * ctx_count
    chunks = blocks // 4
    ctx = lax.axis_index("ctx")
    f = lax.axis_index("fsdp")
    head = ctx % GROUP
    k = head % 2

    def ring(a, shift):
        pairs = [
            (
                g * GROUP + RING[i] * 2 + core,
                g * GROUP + RING[(i + shift) % CHIPS] * 2 + core,
            )
            for g in range(groups)
            for i in range(CHIPS)
            for core in range(2)
        ]
        return lax.ppermute(a, "ctx", pairs)

    def ring_by_core(a):
        pairs = [
            (
                g * GROUP + RING[i] * 2 + core,
                g * GROUP + RING[(i + 1 - 2 * core) % CHIPS] * 2 + core,
            )
            for g in range(groups)
            for i in range(CHIPS)
            for core in range(2)
        ]
        return lax.ppermute(a, "ctx", pairs)

    def swap_core(a):
        return lax.ppermute(a, "ctx", [(c, c ^ 1) for c in range(ctx_count)])

    def swap_far(a):
        pairs = [
            (2 * c + side, 2 * (c ^ 1) + 1 - side) for c in range(ctx_count) for side in range(2)
        ]
        return lax.ppermute(a, ("ctx", "fsdp"), pairs)

    def swap_x(a):
        return lax.ppermute(a, "fsdp", [(0, 1), (1, 0)])

    def turn_groups(a, by):
        return lax.ppermute(
            a, "ctx", [(c, (c + by * GROUP) % ctx_count) for c in range(ctx_count)]
        )

    def sum_groups(a, kind):
        total = a
        for by in range(1, groups):
            total = total + turn_groups(a.astype(kind), by).astype(a.dtype)
        return total

    def exchange(a):
        which = (
            None
            if groups == 1
            else [[g * GROUP + h for h in range(GROUP)] for g in range(groups)]
        )
        return lax.all_to_all(a, "ctx", 0, 0, axis_index_groups=which, tiled=True)

    def swap_cores(arrays):
        swapped = []
        for a in arrays:
            swapped.append(swap_core(a))
        return swapped

    def ring_step(up, down):
        return ring(up, 1), ring(down, -1)

    source = jnp.asarray(SOURCE, jnp.int32)[head]
    place = jnp.asarray(PLACE, jnp.int32)[head]
    chip = head // 2
    ring_at = jnp.where(chip % 2 == 0, chip // 2, CHIPS - 1 - chip // 2)
    spot = jnp.stack([f, k, ring_at, head]).astype(jnp.int32)
    group = ctx // GROUP

    def pairs_of(which):
        return lax.dynamic_slice_in_dim(pairing, which * GROUP, GROUP, 0)

    def slots_of(pairs):
        return jnp.stack([pairs, blocks - 1 - pairs], axis=1).astype(jnp.int32)

    my_pairs = pairs_of(group)
    slots_ctx = slots_of(my_pairs)
    slots_ring = slots_ctx[source]
    if groups == 1:
        ids = np.arange(2 * GROUP, dtype=np.int32)
        slots_q, slots_out = slots_ring, slots_ctx
        slots_k = slots_ring
    else:
        flat = slots_ctx.reshape(-1)
        rank = jnp.sum((flat[None, :] < flat[:, None]).astype(jnp.int32), axis=1)
        ids = jnp.sum(
            jnp.where(rank[None, :] == jnp.arange(2 * GROUP)[:, None], flat[None, :], 0), axis=1
        ).astype(jnp.int32)
        slots_out = rank.reshape(GROUP, 2).astype(jnp.int32)
        slots_q = slots_out[source]
        slots_k = jnp.concatenate(
            [slots_of(pairs_of((group - by) % groups))[source] for by in range(groups)], axis=0
        )
    tiles, width = (4, 512) if groups == 1 else (8, 256)
    by_tile = ids.reshape(tiles, width // 64)
    full = jnp.asarray((by_tile[:, 0] + 1) // 4, jnp.int32)
    total = jnp.asarray(by_tile[:, -1] // 4 + 1, jnp.int32)
    every = np.arange(chunks)[:, None]
    begin = (total[None, :] <= every).sum(axis=1).astype(jnp.int32)
    clear = (full[None, :] <= every).sum(axis=1).astype(jnp.int32)
    qblock = jnp.asarray(ids.repeat(64).reshape(tiles, 1, width), jnp.int32)
    if groups == 1:
        full, total, begin, clear = [
            jnp.asarray(a, jnp.int32)
            for a in (
                (by_tile[:, 0] + 1) // 4,
                by_tile[:, -1] // 4 + 1,
                (by_tile[None, :, -1] // 4 + 1 <= every).sum(axis=1),
                ((by_tile[None, :, 0] + 1) // 4 <= every).sum(axis=1),
            )
        ]

    any_spec = pl.BlockSpec(memory_space=pl.ANY)
    vmem_spec = pl.BlockSpec(memory_space=pltpu.VMEM)
    x = stream_in.reshape(dev_rows, model)
    g_rows = cotangent.reshape(dev_rows, model)
    last = model // 128 - 1

    def columns(more):
        def at(i, spot):
            return (0, jnp.minimum(spot[3] * HD // 128 + more, last))

        return pl.BlockSpec((half, 128), at)

    def whole(shape):
        return pl.BlockSpec(shape, lambda i, spot: (0,) * len(shape))

    part = query_scale.shape[0]
    def gates(arrays, after):
        return call(
            lambda *refs: None,
            [(a.shape, a.dtype) for a in arrays],
            arrays,
            specs=[any_spec] * len(arrays),
            out_specs=[any_spec] * len(arrays),
            after=after,
            aliases={at: at for at in range(len(arrays))},
            name="gate",
        mib=1,
        us=0.1,
        )

    def gate(a, after):
        return gates([a], after)[0]

    steps = [(x,), ring_step(x, x)]
    for _ in range(2):
        steps.append(ring_step(*steps[-1]))
    early = quarter // 5 * 2
    out_xs = [swap_x(lax.dynamic_slice_in_dim(w_output, k * quarter, early, 0))]
    (slab,) = call(
        slab_body,
        [((3 * HD + 16, half), BF)],
        [
            spot,
            *[w for w in (w_query, w_key, w_value) for _ in range(2)],
            gain_attn,
            gain_mlp,
            query_scale,
        ],
        specs=[columns(0), columns(1)] * 3
        + [pl.BlockSpec((n,), lambda i, spot: (0,)) for n in (half, half, part)],
        out_specs=[whole((3 * HD + 16, half))],
        scratch=[pltpu.VMEM((256, half), F32)],
        smem=1,
        grid=(1,),
        name="slab",
        us=3,
        mib=60,
    )
    slab_x = swap_x(slab)
    late = lax.dynamic_slice_in_dim(w_output, k * quarter + early, quarter - early, 0)
    late, slab_x = gates([late, slab_x], out_xs)
    out_xs.append(swap_x(late))
    weight_t, gains, scale_col, scale_row = call(
        setup_body,
        [((3 * HD, model), BF), ((8, model), F32), ((HD, 1), F32), ((8, 128), F32)],
        [spot, slab, slab_x],
        smem=1,
        after=[*steps[2], *out_xs[:1]],
        name="setup",
        mib=60,
        us=2,
    )
    weight_sib = swap_core(weight_t)

    norms = None
    queries, keys, far_keys, near = [], [], [], []
    norms = None
    slot = 0
    for step in range(2):
        if step:
            up, down = gates(steps[3], queries)
            arrays = [up, down, *ring_step(up[: dev_rows // 2], down[dev_rows // 2 :])]
        else:
            arrays = [x, *steps[1], *steps[2]]
        count = sum(a.shape[0] for a in arrays) // dev_rows
        moved = (w_hidden, w_return) if step else ()
        outs = [((CHIPS, dev_rows, model), BF)]
        outs += [((count, HD, 128), BF), ((count, 2 * HD, 128), BF)]
        outs += [((count, 3 * HD, 128), BF), ((count, 2 * HD, 128), BF)]
        outs += [((quarter, model), BF)] * len(moved)
        ins = [spot, *arrays, gains, weight_t, weight_sib, scale_col, *moved]
        ins += [norms] if step else []
        norms, q_part, kv_part, near_part, far_part, *moved_parts = call(
            functools.partial(project_body, (len(arrays), count, len(moved), slot)),
            outs,
            ins,
            specs=[vmem_spec] * (len(arrays) + 4) + [any_spec] * (len(moved) + bool(step)),
            out_specs=[any_spec] + [vmem_spec] * (len(outs) - 1),
            scratch=[
                pltpu.VMEM((count, dev_rows, model), BF),
                pltpu.SemaphoreType.DMA((max(1, len(moved)),)),
                pltpu.SemaphoreType.DMA,
            ],
            smem=1,
            after=[(), out_xs[1:]][step],
            aliases={len(ins) - 1: 0} if step else None,
            name="project",
            us=[3, 3][step],
            mib=60,
        )
        slot += count
        queries.append(q_part)
        keys.append(kv_part)
        far_keys += [swap_x(kv_part), swap_far(far_part)]
        near.append(swap_core(near_part))
    hid_part, ret_part = moved_parts
    norms_sib = swap_core(norms)
    parts = [w_output]
    for out_x in out_xs:
        out_x = gate(out_x, [norms])
        parts += [out_x, swap_core(out_x)]
    hid_x = swap_x(gate(hid_part, far_keys))
    ret_x = swap_x(gate(ret_part, far_keys))

    arrays, places = [], []
    at = 0
    for step, q_part in enumerate(queries):
        mine, theirs = (q_part, keys[step], far_keys[2 * step]), (near[step], far_keys[2 * step + 1])
        count = q_part.shape[0]
        for entries, blocks_of in ((OWN_ENTRIES, mine), (SIB_ENTRIES, theirs)):
            for j in range(count):
                entry = entries[at + j]
                last = len(arrays) + len(blocks_of) - 1
                places.append(("q", len(arrays), j, entry, 0))
                places.append(("kv", last - 1, j, entry, 0))
                places.append(("kv", last, j, entry, 1))
            arrays += blocks_of
        at += count
    if groups > 1:
        order = OWN_ENTRIES + SIB_ENTRIES
        mine = jnp.concatenate([*keys, *[a[:, HD:] for a in near]], axis=0)
        theirs = jnp.concatenate([*far_keys[::2], *far_keys[1::2]], axis=0)
        for by in range(1, groups):
            for side, a in enumerate((mine, theirs)):
                places += [
                    ("kv", len(arrays), j, by * GROUP + order[j], side) for j in range(GROUP)
                ]
                arrays.append(turn_groups(a, by))
    pieces, q_t, k_t, k_rows, v_rows, att, lse = call(
        functools.partial(forward_body, {"arrays": len(arrays), "blocks": places}, chunks),
        [
            ((GROUP, HD, 128), BF),
            ((tiles, HD, width), BF),
            ((chunks, HD, 512), BF),
            ((chunks, 512, HD), BF),
            ((chunks, 512, HD), BF),
            ((tiles, HD, width), F32),
            ((tiles, 1, width), F32),
        ],
        [slots_q, slots_k, slots_out, full, total, qblock, *arrays],
        scratch=[
            pltpu.VMEM((2 * GROUP, HD, 64), BF),
            pltpu.VMEM((2, blocks, 2 * HD, 64), BF),
            pltpu.VMEM((chunks, HD + 16, 512), BF),
            pltpu.VMEM((chunks, 512, width), F32),
            pltpu.VMEM((2 * GROUP, HD, 64), BF),
        ],
        smem=5,
        name="attention_forward",
        us=20,
        mib=60,
    )
    (pieces,) = gates([pieces], [parts[2], parts[4]])
    att_t = exchange(pieces).reshape(model, dev_rows)
    hid_x, ret_x = gates([hid_x, ret_x], [att_t])
    for w, first in ((w_hidden, hid_x), (w_return, ret_x)):
        parts += [w, first, swap_core(first)]

    g_sib, g_x = swap_core(g_rows), swap_x(gate(g_rows, [pieces]))

    left_rows = 15 * (half // CHIPS)
    share_rows = left_rows + 2 * (model // 128) * dev_rows + 16
    stream, dy, datt_t, f_own, f_sib, f_x, f_xs = call(
        rows_body,
        [
            ((dev_rows, model), BF),
            ((dev_rows, model), F32),
            ((model, dev_rows), BF),
            ((share_rows, 128), BF),
            ((share_rows, 128), BF),
            ((share_rows, 128), BF),
            ((left_rows, 128), BF),
        ],
        [spot, att_t, x, g_rows, gains, *parts],
        specs=[vmem_spec] * 4 + [any_spec] * 11,
        scratch=[pltpu.VMEM((model, model), BF)] * 3
        + [pltpu.VMEM((3, model, dev_rows), BF), pltpu.SemaphoreType.DMA((3, 5))],
        smem=1,
        name="row_part",
        mib=60,
        us=10,
    )
    datt_t, g_x = gates([datt_t, g_x], ())
    grads = exchange(datt_t.reshape(GROUP, HD, dev_rows))
    g_xs = swap_core(g_x)

    from_x = swap_x(f_x)
    forward = swap_core(f_xs)
    from_sib, from_xs = swap_core(f_sib), swap_x(forward)

    def chunk_call(table, body, chunk, ins, outs, name, after):
        return call(
            body,
            outs,
            [spot, table, *ins],
            specs=[pl.BlockSpec((1, 256, model), lambda i, spot: (chunk, 0, 0))]
            + [whole(a.shape) for a in ins],
            out_specs=[whole(shape) for shape, _ in outs],
            smem=1,
            grid=(1,),
            after=after,
            name=name,
            us=2,
            mib=16,
        )

    def reduce_step(table, step, received, after):
        outs = chunk_call(
            table,
            functools.partial(reduce_step_body, step),
            4 - step,
            received,
            [((256, model if step else model // 2), BF)],
            "reduce_step",
            after,
        )
        return [ring_by_core(outs[0])], outs

    own, other, dq_pieces, scale_sum = call(
        backward_body,
        [
            ((chunks, 2 * HD, 256), F32),
            ((chunks, 2 * HD, 256), BF),
            ((GROUP, HD, 128), BF),
            ((HD, width), F32),
        ],
        [slots_out, begin, clear, qblock, scale_col, grads, q_t, att, lse, k_t, k_rows, v_rows],
        specs=[vmem_spec] * 6 + [any_spec] * 3,
        scratch=[
            pltpu.VMEM((tiles, HD, width), BF),
            pltpu.VMEM((tiles, 1, width), F32),
            pltpu.VMEM((tiles, HD, width), F32),
            pltpu.VMEM((2 * GROUP, HD, 64), BF),
            pltpu.VMEM((chunks, HD, 512), BF),
            pltpu.VMEM((chunks, 512, HD), BF),
            pltpu.VMEM((chunks, 512, HD), BF),
            pltpu.SemaphoreType.DMA((3,)),
        ],
        smem=3,
        after=[forward],
        name="attention_backward",
        us=25,
        mib=60,
    )
    other_x = swap_x(other)
    from_x, from_sib, from_xs, g_xs, norms_sib = gates(
        [from_x, from_sib, from_xs, g_xs, norms_sib], [own]
    )
    (partial,) = call(
        pooled_grad_body,
        [((5, 256, model), BF)],
        [f_own, from_sib, from_x, from_xs, swap_core(from_x), g_rows, g_sib, g_x, g_xs],
        name="pooled_grads",
        us=3,
        mib=24,
    )
    received, done = reduce_step(partial, 0, (), ())
    if groups > 1:
        own = sum_groups(own + other_x.astype(F32), BF)
        other_x = jnp.zeros_like(other_x)
    received, done = reduce_step(partial, 1, received, ())
    d_pieces, d_other = call(
        join_body,
        [((GROUP, 3 * HD, 128), BF), ((10, 3 * HD, 128), BF)],
        [slots_ctx, spot, dq_pieces, own, other_x],
        scratch=[pltpu.VMEM((blocks, 2 * HD, 64), BF)],
        smem=2,
        after=done,
        name="join",
        us=2,
        mib=24 if groups == 1 else 60,
    )
    d_near = swap_core(d_other)
    own_share, other_share = call(
        qkv_grad_body,
        [((3 * HD + 16, half), F32), ((3 * HD + 16, half), BF)],
        [place, spot, d_pieces, scale_sum, norms, norms_sib],
        scratch=[pltpu.VMEM((3 * HD, model), F32)],
        smem=2,
        name="qkv_grads",
        us=4.7,
        mib=24,
    )
    share_x = swap_x(other_share)
    received, done = reduce_step(partial, 2, received, [own_share])

    (table,) = call(
        products_body,
        [((5, 256, model), BF)],
        [spot, d_pieces, d_near, weight_t, weight_sib],
        smem=1,
        after=done,
        name="products",
        us=4,
        mib=24,
    )
    first, done = reduce_step(table, 0, (), ())
    (share,) = call(
        qkv_sum_body,
        [((3 * HD + 16, half), BF)],
        [own_share, share_x, slab],
        after=done,
        name="qkv_sum",
        us=1,
        mib=8,
    )
    share = sum_groups(share.astype(F32), BF).astype(BF) if groups > 1 else share
    share_near = swap_core(share)
    received, done = reduce_step(partial, 3, received, [share])
    received_near = swap_core(received[0])
    (chip_share,) = call(
        chip_pack_body,
        [((2 * (3 * HD + 16), half), BF)],
        [spot, share, share_near],
        smem=1,
        after=done,
        name="chip_pack",
        us=1,
        mib=8,
    )
    q_steps = [chip_share, ring_by_core(chip_share)]
    first, done = reduce_step(table, 1, first, [chip_share])
    (mine,) = chunk_call(
        partial,
        reduce_end_body,
        0,
        (*received, received_near),
        [((256, model), BF)],
        "reduce_end",
        [chip_share],
    )
    first, done = reduce_step(table, 2, first, [mine])
    mine = sum_groups(mine.astype(F32), BF).astype(BF) if groups > 1 else mine
    m_steps = [mine, ring_by_core(mine)]
    q_steps.append(ring_by_core(q_steps[-1]))
    first, done = reduce_step(table, 3, first, [*done, q_steps[2]])
    m_steps.append(ring_by_core(m_steps[-1]))
    q_steps.append(ring_by_core(q_steps[-1]))
    m_steps.append(ring_by_core(m_steps[-1]))
    q_near = [swap_core(a) for a in q_steps[1:3]]
    m_near = [swap_core(a) for a in m_steps[1:3]]
    elements = float(ctx_count * 2 * dev_rows * model)
    chunk = half // CHIPS
    grads_shape = [((half, model), F32)] * 3
    *rows_grads, gain_sums, tails = call(
        functools.partial(rows_place_body, True, elements),
        [*grads_shape, ((half, 128), F32), ((8, 128), F32)],
        [spot, *m_steps[:3], *m_near, w_hidden],
        out_specs=[any_spec] * 3 + [vmem_spec] * 2,
        scratch=[pltpu.VMEM((5, 3, chunk, model), F32), pltpu.SemaphoreType.DMA((5, 3))],
        smem=1,
        name="rows_place",
        us=4,
        mib=40,
    )

    first_near = swap_core(first[0])
    (d_in,) = chunk_call(
        table,
        inputs_grad_body,
        0,
        (*first, first_near, x, dy, gains),
        [((dev_rows, model), BF)],
        "inputs_grad",
        [m_steps[2], tails],
    )

    def last_step(a, axis):
        size = a.shape[axis] // 2
        return ring_by_core(lax.dynamic_slice_in_dim(a, k * size, size, axis))

    q_last = last_step(q_steps[-1], 0)
    m_held = m_steps[-1]
    m_last = last_step(m_held, 1)
    q_near += [swap_core(a) for a in q_steps[3:]]
    m_near += [swap_core(m_held)]
    grad_query, grad_key, grad_value, gain_one_grad, scale_grad = call(
        qkv_place_body,
        [((half, model), F32)] * 3 + [((half,), F32), ((part,), F32)],
        [spot, *q_steps, *q_near, q_last, swap_core(q_last), gain_attn, scale_row],
        scratch=[pltpu.VMEM((3, model, half), BF)],
        smem=1,
        name="qkv_place",
        us=6,
        mib=40,
    )
    (m_last,) = gates([m_last], [grad_query, d_in])
    ins = [spot, m_held, m_near[2], m_last, swap_core(m_last), w_hidden, gain_mlp, gain_sums, tails]
    grad_output, grad_hidden, grad_return, gain_two_grad, root_means = call(
        functools.partial(rows_place_body, False, elements),
        [*grads_shape, ((half,), F32), ((2,), F32)],
        [*ins, *rows_grads],
        specs=[vmem_spec] * (len(ins) - 1) + [any_spec] * 3,
        out_specs=[any_spec] * 3 + [vmem_spec] * 2,
        scratch=[
            pltpu.VMEM((3, 3, chunk, model), F32),
            pltpu.VMEM((half, 128), F32),
            pltpu.SemaphoreType.DMA((3, 3)),
        ],
        smem=1,
        aliases={len(ins) + at: at for at in range(3)},
        name="rows_place",
        us=3,
        mib=40,
    )
    return (
        stream.reshape(stream_in.shape),
        d_in.reshape(stream_in.shape),
        grad_query,
        grad_key,
        grad_value,
        grad_output,
        grad_hidden,
        grad_return,
        gain_one_grad,
        gain_two_grad,
        scale_grad,
        root_means,
    )


def solution(mesh):
    rows = P(None, ("ctx", "fsdp"), None)
    weight, vector = P("fsdp", None), P("fsdp")
    return jax.shard_map(
        functools.partial(per_device, mesh.shape["ctx"]),
        mesh=mesh,
        in_specs=(rows, P(), *([weight] * 6), *([vector] * 3), rows),
        out_specs=(rows, rows, *([weight] * 6), *([vector] * 3), P()),
        check_vma=False,
    )
```

```python
import functools

import jax
import jax.numpy as jnp
import numpy as np
from jax import lax
from jax.experimental import pallas as pl
from jax.experimental.pallas import tpu as pltpu
from jax.sharding import PartitionSpec as P

H = 16
HD = 80
EPSILON = 1e-06
LOWEST = -1e30
BF = jnp.bfloat16
F32 = jnp.float32
MIB = 1024 * 1024
FLOPS_A_US = 1.15e9

GROUP = 16
CHIPS = 8
RING = (0, 2, 4, 6, 7, 5, 3, 1)
ORDER = (
    ((0, 0), (0, 1))
    + tuple((off, core) for s in (1, 2, 3) for core in (0, 1) for off in (-s, s))
    + ((4, 0), (4, 1))
)
SOURCE = [
    [RING[(RING.index(h // 2) + off) % CHIPS] * 2 + ((h % 2) ^ core) for off, core in ORDER]
    for h in range(GROUP)
]
PLACE = [
    [((h % 2) ^ core) * CHIPS + (RING.index(h // 2) + off) % CHIPS for off, core in ORDER]
    for h in range(GROUP)
]

OWN_ENTRIES = (0, 2, 3, 6, 7, 10, 11, 14)
SIB_ENTRIES = (1, 4, 5, 8, 9, 12, 13, 15)

NN = (((1,), (0,)), ((), ()))
NT = (((1,), (1,)), ((), ()))
TN = (((0,), (0,)), ((), ()))


def dot(a, b, dims):
    return lax.dot_general(a, b, dims, preferred_element_type=F32)


def call(body, outs, ins, scratch=(), specs=None, out_specs=None, name=None, smem=0, after=(), grid=None, aliases=None, us=1.0, mib=24):
    given = len(ins)
    waits = len(after)

    def run(*refs):
        body(*refs[:given], *refs[given + waits :])

    if specs is None:
        specs = [pl.BlockSpec(memory_space=pltpu.VMEM)] * (given - smem)
    specs = list(specs) + [pl.BlockSpec(memory_space=pl.ANY)] * waits
    out_specs = out_specs or [pl.BlockSpec(memory_space=pltpu.VMEM)] * len(outs)
    if grid is None:
        how = dict(
            in_specs=[pl.BlockSpec(memory_space=pltpu.SMEM)] * smem + specs,
            out_specs=out_specs,
            scratch_shapes=list(scratch),
        )
    else:
        how = dict(
            grid_spec=pltpu.PrefetchScalarGridSpec(
                num_scalar_prefetch=smem,
                grid=grid,
                in_specs=specs,
                out_specs=out_specs,
                scratch_shapes=list(scratch),
            )
        )
    return pl.pallas_call(
        run,
        out_shape=[jax.ShapeDtypeStruct(shape, kind) for shape, kind in outs],
        compiler_params=pltpu.CompilerParams(vmem_limit_bytes=mib * MIB),
        cost_estimate=pl.CostEstimate(flops=int(us * FLOPS_A_US), bytes_accessed=1, transcendentals=0),
        input_output_aliases=aliases or {},
        name=name,
        **how,
    )(*ins, *after)


def start_copies(jobs, sems):
    copies = []
    for at, (source, target) in enumerate(jobs):
        copy = pltpu.make_async_copy(source, target, sems.at[at])
        copy.start()
        copies.append(copy)
    return copies


def slab_body(spot, q0, q1, k0, k1, v0, v1, gain_one, gain_two, scale, out, turned):
    start = spot[3] * HD
    off = pl.multiple_of(start - start // 128 * 128, 16)
    for w, (left, right) in enumerate(((q0, q1), (k0, k1), (v0, v1))):
        turned[:128] = left[...].astype(F32).T
        turned[128:] = right[...].astype(F32).T
        out[w * HD : w * HD + HD] = turned[pl.ds(off, HD)].astype(BF)
    width = out.shape[1]
    part = scale.shape[0]
    line = jnp.concatenate([line_of(scale), jnp.zeros((1, width - part), F32)], axis=1)
    tail = [line_of(gain_one), line_of(gain_two), line, jnp.zeros((13, width), F32)]
    out[3 * HD :] = jnp.concatenate(tail, axis=0).astype(BF)


def line_of(vector):
    return vector[...].astype(F32).reshape(1, vector.shape[0])


def setup_body(spot, slab, slab_x, weight, gains, scale_col, scale_row):
    width = slab.shape[1]
    f = spot[0]
    mine, theirs = slab[...], slab_x[...]
    left = jnp.where(f == 0, mine, theirs)
    right = jnp.where(f == 0, theirs, mine)
    weight[:, :width] = left[: 3 * HD]
    weight[:, width:] = right[: 3 * HD]
    left, right = left[3 * HD :].astype(F32), right[3 * HD :].astype(F32)
    gains[...] = jnp.concatenate([left[:8], right[:8]], axis=1)
    part = HD // 2
    row = jnp.concatenate([left[2:3, :part], right[2:3, :part], jnp.zeros((1, 128 - HD), F32)], axis=1)
    row = jnp.broadcast_to(row, (128, 128))
    scale_row[...] = row[:8]
    scale_col[...] = row.T[:HD, :1] * HD ** (-0.5)


def project_body(layout, spot, *refs):
    count, pieces, carried, slot = layout
    xs, refs = refs[:count], refs[count:]
    (gains, weight, weight_sib, scale), refs = refs[:4], refs[4:]
    moved, refs = refs[:carried], refs[carried:]
    refs = refs if slot == 0 else refs[1:]
    (norm_out, q_out, kv_out, near_out, far_out), refs = refs[:5], refs[5:]
    outs, (norm_vmem, sems, norm_sem) = refs[:-3], refs[-3:]
    copies = []
    for w, out in zip(moved, outs):
        size = out.shape[0]
        rows = pl.ds(pl.multiple_of(spot[1] * size, 16), size)
        copies.append((w.at[rows], out))
    copies = start_copies(copies, sems)
    x = jnp.concatenate([r[...] for r in xs], axis=0).astype(F32)
    inv = lax.rsqrt(jnp.mean(x * x, axis=-1, keepdims=True) + EPSILON)
    norm = (x * inv * gains[0:1]).astype(BF)
    norm_vmem[...] = norm.reshape(norm_vmem.shape)
    keep = pltpu.make_async_copy(norm_vmem, norm_out.at[pl.ds(slot, pieces)], norm_sem)
    keep.start()
    for table, other in ((weight, False), (weight_sib, True)):
        out = dot(table[...], norm, NT)
        q = (out[:HD] * scale[...]).astype(BF)
        kv = out[HD:].astype(BF)
        for j in range(pieces):
            lanes = slice(j * 128, (j + 1) * 128)
            if other:
                near_out[j, :HD] = q[:, lanes]
                near_out[j, HD:] = kv[:, lanes]
                far_out[j] = kv[:, lanes]
            else:
                q_out[j] = q[:, lanes]
                kv_out[j] = kv[:, lanes]
    for copy in copies:
        copy.wait()
    keep.wait()


def forward_body(layout, chunks, slots_q, slots_k, slots_out, full, total, qblock, *refs):
    count = layout["arrays"]
    arrays, refs = refs[:count], refs[count:]
    (pieces, q_t, k_t, k_rows, v_rows, att, lse), refs = refs[:7], refs[7:]
    block_q, block_kv, v_t, scores, block_out = refs
    for kind, which, index, entry, side in layout["blocks"]:
        for half in range(2):
            lanes = slice(half * 64, half * 64 + 64)
            if kind == "q":
                block_q[slots_q[entry, half]] = arrays[which][index, :HD, lanes]
            else:
                value = arrays[which][index, :, lanes]
                block_kv[side, slots_k[entry, half]] = value[value.shape[0] - 2 * HD :]
    rows = 2 * 256
    ones_row = jnp.where(lax.broadcasted_iota(jnp.int32, (16, rows), 0) == 0, 1.0, 0.0).astype(BF)

    @pl.loop(0, chunks)
    def _(c):
        tile = jnp.concatenate(
            [block_kv[side, 4 * c + m] for side in range(2) for m in range(4)], axis=1
        )
        k_t[c] = tile[:HD]
        k_rows[c] = tile[:HD].astype(F32).T.astype(BF)
        v_rows[c] = tile[HD:].astype(F32).T.astype(BF)
        v_t[c] = jnp.concatenate([tile[HD:], ones_row], axis=0)

    width = q_t.shape[2]
    per = width // 64

    @pl.loop(0, q_t.shape[0])
    def _(i):
        query = jnp.concatenate([block_q[per * i + m] for m in range(per)], axis=1)
        q_t[i] = query
        ids = qblock[i]

        def scan_max(masked, c, top):
            s = dot(k_rows[c], query, NN)
            if masked:
                s = jnp.where(block_of_row(width) + 4 * c <= ids, s, LOWEST)
            scores[c] = s
            return jnp.maximum(top, jnp.max(s.reshape(rows // 8, 8, width), axis=0))

        top = jnp.full((8, width), LOWEST, F32)
        top = lax.fori_loop(0, full[i], functools.partial(scan_max, False), top)
        top = lax.fori_loop(full[i], total[i], functools.partial(scan_max, True), top)
        top = jnp.max(top, axis=0, keepdims=True)

        def gather(c, acc):
            w = jnp.exp(scores[c] - top).astype(BF)
            return acc + dot(v_t[c], w, NN)

        acc = lax.fori_loop(0, total[i], gather, jnp.zeros((HD + 16, width), F32))
        sums = acc[HD : HD + 1]
        out = acc[:HD] / sums
        att[i] = out
        lse[i] = top + jnp.log(sums)
        low = out.astype(BF)
        for m in range(per):
            block_out[per * i + m] = low[:, m * 64 : m * 64 + 64]

    for c in range(GROUP):
        pieces[c] = jnp.concatenate(
            [block_out[slots_out[c, 0]], block_out[slots_out[c, 1]]], axis=1
        )


def block_of_row(width):
    return lax.broadcasted_iota(jnp.int32, (512, width), 0) % 256 // 64


def backward_body(
    slots_out,
    begin,
    clear,
    qblock,
    scale,
    grads,
    q_t,
    att,
    lse,
    k_t_in,
    k_rows_in,
    v_rows_in,
    dkv_own,
    dkv_other,
    dq_pieces,
    scale_sum,
    grad_t,
    delta,
    dq,
    blocks,
    k_t,
    k_rows,
    v_rows,
    sems,
):
    copies = start_copies([(k_t_in, k_t), (k_rows_in, k_rows), (v_rows_in, v_rows)], sems)
    tiles, _, width = q_t.shape
    per = width // 64
    for c in range(GROUP):
        for half in range(2):
            blocks[slots_out[c, half]] = grads[c, :, half * 64 : half * 64 + 64]

    @pl.loop(0, tiles)
    def _(i):
        grad = jnp.concatenate([blocks[per * i + m] for m in range(per)], axis=1)
        grad_t[i] = grad
        delta[i] = jnp.sum(grad.astype(F32) * att[i], axis=0, keepdims=True)
        dq[i] = jnp.zeros((HD, width), F32)

    for copy in copies:
        copy.wait()

    @pl.loop(0, k_t.shape[0])
    def _(c):
        def step(masked, i, carry):
            d_k, d_v = carry
            query, grad = q_t[i], grad_t[i]
            prob = jnp.exp(dot(k_rows[c], query, NN) - lse[i])
            if masked:
                prob = jnp.where(block_of_row(width) + 4 * c <= qblock[i], prob, 0.0)
            d_score = (prob * (dot(v_rows[c], grad, NN) - delta[i])).astype(BF)
            dq[i] += dot(k_t[c], d_score, NN)
            return d_k + dot(query, d_score, NT), d_v + dot(grad, prob.astype(BF), NT)

        carry = (jnp.zeros((HD, 512), F32), jnp.zeros((HD, 512), F32))
        carry = lax.fori_loop(begin[c], clear[c], functools.partial(step, True), carry)
        d_k, d_v = lax.fori_loop(clear[c], tiles, functools.partial(step, False), carry)
        dkv_own[c, :HD] = d_k[:, :256]
        dkv_own[c, HD:] = d_v[:, :256]
        dkv_other[c, :HD] = d_k[:, 256:].astype(BF)
        dkv_other[c, HD:] = d_v[:, 256:].astype(BF)

    total = jnp.zeros((HD, width), F32)
    for i in range(tiles):
        total = total + dq[i] * q_t[i].astype(F32)
        rounded = (dq[i] * scale[...]).astype(BF)
        for m in range(per):
            blocks[per * i + m] = rounded[:, m * 64 : m * 64 + 64]
    scale_sum[...] = total
    for c in range(GROUP):
        dq_pieces[c] = jnp.concatenate(
            [blocks[slots_out[c, 0]], blocks[slots_out[c, 1]]], axis=1
        )


def join_body(slots_kv, spot, dq_pieces, own, received, pieces, other, blocks):
    @pl.loop(0, own.shape[0])
    def _(c):
        tile = (own[c] + received[c].astype(F32)).astype(BF)
        for m in range(4):
            blocks[4 * c + m] = tile[:, m * 64 : m * 64 + 64]

    for p in range(CHIPS):
        for core in range(2):
            c = RING[p] * 2 + core
            pieces[2 * p + core, :HD] = dq_pieces[c]
            pieces[2 * p + core, HD:] = jnp.concatenate(
                [blocks[slots_kv[c, 0]], blocks[slots_kv[c, 1]]], axis=1
            )
    sign = 1 - 2 * spot[1]
    for j in range(5):
        pos = lax.rem(spot[2] + CHIPS - sign * j, CHIPS)
        for core in range(2):
            other[2 * j + core] = pieces[2 * pos + core]


def products_body(spot, pieces, near, weight, weight_sib, out):
    sign = 1 - 2 * spot[1]
    for j in range(5):
        pos = lax.rem(spot[2] + CHIPS + sign * j, CHIPS)
        for core in range(2):
            total = dot(pieces[2 * pos + core], weight[...], TN)
            total = total + dot(near[2 * j + core], weight_sib[...], TN)
            out[j, core * 128 : core * 128 + 128] = total.astype(BF)


def qkv_grad_body(place, spot, pieces, scale_sum, *refs):
    norms, (own, other, table) = refs[:-3], refs[-3:]
    total = jnp.zeros((3 * HD, table.shape[1]), F32)
    for norm, entries in zip(norms, (OWN_ENTRIES, SIB_ENTRIES)):
        for j, entry in enumerate(entries):
            at = 2 * lax.rem(place[entry], CHIPS) + place[entry] // CHIPS
            total = total + dot(pieces[at], norm[j], NN)
    table[...] = total
    width = table.shape[1] // 2
    f = spot[0]
    own[: 3 * HD] = table[:, pl.ds(pl.multiple_of(f * width, 128), width)]
    other[: 3 * HD] = table[:, pl.ds(pl.multiple_of((1 - f) * width, 128), width)].astype(BF)
    column = jnp.broadcast_to(jnp.sum(scale_sum[...], axis=1, keepdims=True), (HD, 128))
    line = column.T[:1]
    high = line.astype(BF)
    low = (line - high.astype(F32)).astype(BF)
    own[3 * HD :] = jnp.zeros((16, width), F32)
    own[3 * HD : 3 * HD + 1, :HD] = line
    tail = jnp.concatenate([high.astype(F32), low.astype(F32), jnp.zeros((14, HD), F32)], axis=0)
    other[3 * HD :] = jnp.concatenate([tail, jnp.zeros((16, width - HD), F32)], axis=1).astype(BF)


def qkv_sum_body(own, received, slab, out):
    width = own.shape[1]
    total = own[: 3 * HD] + received[: 3 * HD].astype(F32)
    out[: 3 * HD] = total.astype(BF)
    gain = jnp.sum(total * slab[: 3 * HD].astype(F32), axis=0, keepdims=True)
    tail = received[3 * HD :].astype(F32)
    line = own[3 * HD : 3 * HD + 1] + tail[0:1] + tail[1:2]
    rows = []
    for value in (gain, line):
        high = value.astype(BF).astype(F32)
        rows += [high, value - high]
    out[3 * HD :] = jnp.concatenate(rows + [jnp.zeros((12, width), F32)], axis=0).astype(BF)


def chip_pack_body(spot, own, near, out):
    rows = own.shape[0]
    out[pl.ds(pl.multiple_of(spot[1] * rows, 16), rows)] = own[...]
    out[pl.ds(pl.multiple_of((1 - spot[1]) * rows, 16), rows)] = near[...]


def ring_positions(spot):
    sign = 1 - 2 * spot[1]
    offsets = [0] + [-sign * s for s in (1, 2, 3)] + [sign * s for s in (1, 2, 3)] + [4]
    return [lax.rem(spot[2] + CHIPS + off, CHIPS) for off in offsets]


def qkv_place_body(spot, *refs):
    arrays, (gain, scale_row), refs = refs[:9], refs[9:11], refs[11:]
    outs, (gain_out, scale_out, table) = refs[:3], refs[3:]
    width = gain.shape[0]
    size = 3 * HD + 16
    tail = jnp.zeros((16, width), F32)
    positions = ring_positions(spot)
    blocks = [(arrays[at], c * size, positions[at], c) for at in range(7) for c in range(2)]
    blocks += [(arrays[7], 0, positions[7], spot[1]), (arrays[8], 0, positions[7], 1 - spot[1])]
    for ref, row, pos, core in blocks:
        chip = jnp.where(pos < 4, 2 * pos, 15 - 2 * pos)
        head = pl.multiple_of((2 * chip + core) * HD, 16)
        for w in range(3):
            table[w, pl.ds(head, HD)] = ref[row + w * HD : row + w * HD + HD]
        tail = tail + ref[row + 3 * HD : row + size].astype(F32)
    for w in range(3):
        for at in range(0, H * HD, 256):
            outs[w][:, at : at + 256] = table[w, at : at + 256].astype(F32).T
    gain_out[...] = ((tail[0:1] + tail[1:2]) / line_of(gain)).reshape(width)
    scale = (tail[2:3, :128] + tail[3:4, :128]) / scale_row[0:1]
    part = scale_out.shape[0]
    chosen = jnp.where(spot[0] == 0, scale[:, :part], scale[:, part : 2 * part])
    scale_out[...] = chosen.reshape(part)


def rows_body(
    spot,
    att_t,
    x_in,
    g_in,
    gain_in,
    *refs,
):
    weights = (refs[:5], refs[5:8], refs[8:11])
    refs = refs[11:]
    (stream_out, dy_out, datt_out), outs = refs[:3], refs[3:7]
    full = refs[7:10]
    turned, sems = refs[10:]
    f, k = spot[0], spot[1]
    half = weights[0][0].shape[0]
    quarter = half // 2
    early = weights[0][1].shape[0]
    places = [
        [k * quarter, (1 - k) * quarter, k * quarter + early, (1 - k) * quarter + early],
        *[[k * quarter, (1 - k) * quarter]] * 2,
    ]
    copies = []
    for w in range(3):
        mine, *theirs = weights[w]
        jobs = [(mine, full[w].at[pl.ds(pl.multiple_of(f * half, 16), half)])]
        for piece, start in zip(theirs, places[w]):
            rows = pl.ds(pl.multiple_of((1 - f) * half + start, 16), piece.shape[0])
            jobs.append((piece, full[w].at[rows]))
        copies.append(start_copies(jobs, sems.at[w]))
    w_out, w_hid, w_ret = full
    x = x_in[...].astype(F32)
    gain = gain_in[1:2]
    for copy in copies[0]:
        copy.wait()
    attn = dot(att_t[...], w_out[...], TN)
    y1 = x + attn
    inv = lax.rsqrt(jnp.mean(y1 * y1, axis=-1, keepdims=True) + EPSILON)
    unit = y1 * inv
    norm = (unit * gain).astype(BF)
    for copy in copies[1]:
        copy.wait()
    h = dot(norm, w_hid[...], NN)
    sig = jax.nn.sigmoid(h)
    act = (h * sig).astype(BF)
    for copy in copies[2]:
        copy.wait()
    stream = y1 + dot(act, w_ret[...], NN)
    stream_out[...] = stream.astype(BF)
    squares = jnp.where(
        lax.broadcasted_iota(jnp.int32, (8, 128), 0) == 0,
        jnp.sum(stream * stream),
        jnp.sum(attn * attn),
    )
    g = g_in[...]
    d_act = dot(g, w_ret[...], NT)
    d_h = (d_act * sig * (1.0 + h * (1.0 - sig))).astype(BF)
    d_norm = dot(d_h, w_hid[...], NT)
    c2 = d_norm * gain
    dy = inv * (c2 - unit * jnp.mean(c2 * unit, axis=-1, keepdims=True)) + g.astype(F32)
    dy_out[...] = dy
    dy_b = dy.astype(BF)
    datt_out[...] = dot(w_out[...], dy_b, NT).astype(BF)
    turned[0] = att_t[...]
    turned[1] = norm.astype(F32).T.astype(BF)
    turned[2] = act.astype(F32).T.astype(BF)
    rows = x.shape[0]
    columns = x.shape[1] // 128
    chunk = half // CHIPS
    sign = 1 - 2 * k
    for ref, part, way in zip(outs, (f, f, 1 - f, 1 - f), (sign, -sign, sign, -sign)):
        for j in range(5):
            pos = lax.rem(spot[2] + CHIPS + way * j, CHIPS)
            at = pl.multiple_of(part * half + pos * chunk, 16)
            for w in range(3):
                start = (w * 5 + j) * chunk
                ref[start : start + chunk] = turned[w, pl.ds(at, chunk)]
    line = sums_line(squares)
    tail = jnp.concatenate([sums_tail(line, 128), jnp.zeros((8, 128), F32)], axis=0).astype(BF)
    for ref in outs[:3]:
        start = 15 * chunk
        for right in (dy_b, d_h):
            for c in range(columns):
                ref[start : start + rows] = right[:, c * 128 : (c + 1) * 128]
                start += rows
        ref[start : start + 16] = tail


def sums_tail(line, width):
    high = line.astype(BF).astype(F32)
    row = lax.broadcasted_iota(jnp.int32, (8, 128), 0)
    tail = jnp.where(row == 0, high, jnp.where(row == 1, line - high, 0.0))
    return tail if width == 128 else jnp.concatenate([tail, jnp.zeros((8, width - 128), F32)], axis=1)


def sums_line(sums):
    lane = lax.broadcasted_iota(jnp.int32, (1, 128), 1)
    return jnp.where(lane == 0, sums[0:1], jnp.where(lane == 1, sums[1:2], 0.0))


def pooled_grad_body(own, sib, far, far_left, far_right, *refs):
    gs, out = refs[:4], refs[4]
    model = out.shape[2]
    columns = model // 128
    group = far_left.shape[0] // 3
    chunk = group // 5
    rows = 128
    totals = []
    for w in range(3):
        lefts, rights = [], []
        for at, (left, right) in enumerate(
            ((own, own), (sib, sib), (far, far), (far_left, far_right))
        ):
            lefts.append(left[w * group : (w + 1) * group])
            start = 3 * group + w * columns * rows
            if w == 2:
                rights.append(gs[at][...])
                continue
            rights.append(
                jnp.concatenate(
                    [right[start + c * rows : start + (c + 1) * rows] for c in range(columns)], axis=1
                )
            )
        left, right = jnp.concatenate(lefts, axis=1), jnp.concatenate(rights, axis=0)
        totals.append(dot(left, right, NN))
    line = jnp.zeros((1, 128), F32)
    for ref in (own, sib, far, far_right):
        tail = ref[ref.shape[0] - 16 :].astype(F32)
        line = line + tail[0:1] + tail[1:2]
    for j in range(5):
        parts = [t[chunk * j : chunk * (j + 1)] for t in totals]
        tail = jnp.zeros((16, model), F32)
        if j == 0:
            tail = jnp.concatenate([sums_tail(line, model), tail[:8]], axis=0)
        out[j] = jnp.concatenate([*parts, tail], axis=0).astype(BF)


def reduce_step_body(step, spot, block, *refs):
    received, out = refs[:-1], refs[-1]
    half = block.shape[2] // 2
    near = pl.ds(pl.multiple_of(spot[1] * half, 128), half)
    if step == 0:
        out[...] = block[0, :, near]
    elif step == 1:
        out[...] = block[0]
        out[:, near] = (block[0, :, near].astype(F32) + received[0][...].astype(F32)).astype(BF)
    else:
        out[...] = (block[0].astype(F32) + received[0][...].astype(F32)).astype(BF)


def reduce_end_body(spot, block, mine, near, out):
    out[...] = (block[0].astype(F32) + mine[...].astype(F32) + near[...].astype(F32)).astype(BF)


def rows_place_body(first, elements, spot, *refs):
    use = (0, 1, 2, 4, 5) if first else (3, 6, 7, 8)
    arrays, refs = refs[: len(use)], refs[len(use) :]
    if first:
        w_hidden, *outs, sums_out, tail_out, staged, sems = refs
    else:
        (w_hidden, gain, sums_in, tail_in), refs = refs[:4], refs[4:]
        outs, (gain_out, means_out, staged, sums, sems) = refs[3:6], refs[6:]
        sums[...] = sums_in[...]
        sums_out = sums
    rows = staged.shape[2]
    half, model = w_hidden.shape
    if first:
        sums_out[...] = jnp.zeros_like(sums_out)
    tail = jnp.zeros((8, 128), F32)
    positions = ring_positions(spot)
    copies = []
    for at, ref in zip(use, arrays):
        block = ref[...].astype(F32)
        place = pl.ds(pl.multiple_of(positions[min(at, 7)] * rows, 16), rows)
        core = spot[1] if at == 7 else 1 - spot[1]
        width = block.shape[1]
        lanes = pl.ds(pl.multiple_of(core * width, 128), width) if at >= 7 else pl.ds(0, width)
        slot = at % 4 if first else min(use.index(at), 2)
        stage = {0: 0, 1: 1, 2: 2, 4: 3, 5: 4}[at] if first else slot
        for w in range(3):
            staged[stage, w, :, lanes] = block[w * rows : (w + 1) * rows]
        total = jnp.zeros((rows, 128), F32)
        weight = w_hidden[place, lanes].astype(F32)
        for c in range(0, width, 128):
            total = total + block[rows : 2 * rows, c : c + 128] * weight[:, c : c + 128]
        sums_out[place] = sums_out[place] + total
        extra = block[3 * rows : 3 * rows + 8, :128]
        tail = tail + (extra if at < 7 else jnp.where(core == 0, extra, 0.0))
        if at != 7:
            for w in range(3):
                copy = pltpu.make_async_copy(staged.at[stage, w], outs[w].at[place], sems.at[stage, w])
                copy.start()
                copies.append(copy)
    if first:
        tail_out[...] = tail
    else:
        tail = tail + tail_in[...]
        means_out[...] = jnp.sqrt((tail[0:1, :2] + tail[1:2, :2]) / elements).reshape(2)
        line = jnp.sum(sums[...].T, axis=0, keepdims=True) / line_of(gain)
        gain_out[...] = line.reshape(half)
    for copy in copies:
        copy.wait()


def inputs_grad_body(spot, block, mine, near, x_in, dy_in, gains, out):
    size = out.shape[0]
    rows = pl.ds(pl.multiple_of(spot[1] * size, 16), size)
    d_norm = block[0, rows].astype(F32) + mine[rows].astype(F32) + near[rows].astype(F32)
    x = x_in[...].astype(F32)
    inv = lax.rsqrt(jnp.mean(x * x, axis=-1, keepdims=True) + EPSILON)
    unit = x * inv
    c1 = d_norm * gains[0:1]
    dx = inv * (c1 - unit * jnp.mean(c1 * unit, axis=-1, keepdims=True)) + dy_in[...]
    out[...] = dx.astype(BF)


def per_device(
    ctx_count,
    stream_in,
    pairing,
    w_query,
    w_key,
    w_value,
    w_output,
    w_hidden,
    w_return,
    gain_attn,
    gain_mlp,
    query_scale,
    cotangent,
):
    sequences, dev_rows, model = stream_in.shape
    half = w_query.shape[0]
    quarter = half // 2
    groups = ctx_count // GROUP
    blocks = 2 * ctx_count
    chunks = blocks // 4
    ctx = lax.axis_index("ctx")
    f = lax.axis_index("fsdp")
    head = ctx % GROUP
    k = head % 2

    def ring(a, shift):
        pairs = [
            (
                g * GROUP + RING[i] * 2 + core,
                g * GROUP + RING[(i + shift) % CHIPS] * 2 + core,
            )
            for g in range(groups)
            for i in range(CHIPS)
            for core in range(2)
        ]
        return lax.ppermute(a, "ctx", pairs)

    def ring_by_core(a):
        pairs = [
            (
                g * GROUP + RING[i] * 2 + core,
                g * GROUP + RING[(i + 1 - 2 * core) % CHIPS] * 2 + core,
            )
            for g in range(groups)
            for i in range(CHIPS)
            for core in range(2)
        ]
        return lax.ppermute(a, "ctx", pairs)

    def swap_core(a):
        return lax.ppermute(a, "ctx", [(c, c ^ 1) for c in range(ctx_count)])

    def swap_far(a):
        pairs = [
            (2 * c + side, 2 * (c ^ 1) + 1 - side) for c in range(ctx_count) for side in range(2)
        ]
        return lax.ppermute(a, ("ctx", "fsdp"), pairs)

    def swap_x(a):
        return lax.ppermute(a, "fsdp", [(0, 1), (1, 0)])

    def turn_groups(a, by):
        return lax.ppermute(
            a, "ctx", [(c, (c + by * GROUP) % ctx_count) for c in range(ctx_count)]
        )

    def sum_groups(a, kind):
        total = a
        for by in range(1, groups):
            total = total + turn_groups(a.astype(kind), by).astype(a.dtype)
        return total

    def exchange(a):
        which = (
            None
            if groups == 1
            else [[g * GROUP + h for h in range(GROUP)] for g in range(groups)]
        )
        return lax.all_to_all(a, "ctx", 0, 0, axis_index_groups=which, tiled=True)

    def swap_cores(arrays):
        swapped = []
        for a in arrays:
            swapped.append(swap_core(a))
        return swapped

    def ring_step(up, down):
        return ring(up, 1), ring(down, -1)

    source = jnp.asarray(SOURCE, jnp.int32)[head]
    place = jnp.asarray(PLACE, jnp.int32)[head]
    chip = head // 2
    ring_at = jnp.where(chip % 2 == 0, chip // 2, CHIPS - 1 - chip // 2)
    spot = jnp.stack([f, k, ring_at, head]).astype(jnp.int32)
    group = ctx // GROUP

    def pairs_of(which):
        return lax.dynamic_slice_in_dim(pairing, which * GROUP, GROUP, 0)

    def slots_of(pairs):
        return jnp.stack([pairs, blocks - 1 - pairs], axis=1).astype(jnp.int32)

    my_pairs = pairs_of(group)
    slots_ctx = slots_of(my_pairs)
    slots_ring = slots_ctx[source]
    if groups == 1:
        ids = np.arange(2 * GROUP, dtype=np.int32)
        slots_q, slots_out = slots_ring, slots_ctx
        slots_k = slots_ring
    else:
        flat = slots_ctx.reshape(-1)
        rank = jnp.sum((flat[None, :] < flat[:, None]).astype(jnp.int32), axis=1)
        ids = jnp.sum(
            jnp.where(rank[None, :] == jnp.arange(2 * GROUP)[:, None], flat[None, :], 0), axis=1
        ).astype(jnp.int32)
        slots_out = rank.reshape(GROUP, 2).astype(jnp.int32)
        slots_q = slots_out[source]
        slots_k = jnp.concatenate(
            [slots_of(pairs_of((group - by) % groups))[source] for by in range(groups)], axis=0
        )
    tiles, width = (4, 512) if groups == 1 else (8, 256)
    by_tile = ids.reshape(tiles, width // 64)
    full = jnp.asarray((by_tile[:, 0] + 1) // 4, jnp.int32)
    total = jnp.asarray(by_tile[:, -1] // 4 + 1, jnp.int32)
    every = np.arange(chunks)[:, None]
    begin = (total[None, :] <= every).sum(axis=1).astype(jnp.int32)
    clear = (full[None, :] <= every).sum(axis=1).astype(jnp.int32)
    qblock = jnp.asarray(ids.repeat(64).reshape(tiles, 1, width), jnp.int32)
    if groups == 1:
        full, total, begin, clear = [
            jnp.asarray(a, jnp.int32)
            for a in (
                (by_tile[:, 0] + 1) // 4,
                by_tile[:, -1] // 4 + 1,
                (by_tile[None, :, -1] // 4 + 1 <= every).sum(axis=1),
                ((by_tile[None, :, 0] + 1) // 4 <= every).sum(axis=1),
            )
        ]

    any_spec = pl.BlockSpec(memory_space=pl.ANY)
    vmem_spec = pl.BlockSpec(memory_space=pltpu.VMEM)
    x = stream_in.reshape(dev_rows, model)
    g_rows = cotangent.reshape(dev_rows, model)
    last = model // 128 - 1

    def columns(more):
        def at(i, spot):
            return (0, jnp.minimum(spot[3] * HD // 128 + more, last))

        return pl.BlockSpec((half, 128), at)

    def whole(shape):
        return pl.BlockSpec(shape, lambda i, spot: (0,) * len(shape))

    part = query_scale.shape[0]
    def gates(arrays, after):
        return call(
            lambda *refs: None,
            [(a.shape, a.dtype) for a in arrays],
            arrays,
            specs=[any_spec] * len(arrays),
            out_specs=[any_spec] * len(arrays),
            after=after,
            aliases={at: at for at in range(len(arrays))},
            name="gate",
        mib=1,
        us=0.1,
        )

    def gate(a, after):
        return gates([a], after)[0]

    steps = [(x,), ring_step(x, x)]
    for _ in range(2):
        steps.append(ring_step(*steps[-1]))
    early = quarter // 5 * 2
    out_xs = [swap_x(lax.dynamic_slice_in_dim(w_output, k * quarter, early, 0))]
    (slab,) = call(
        slab_body,
        [((3 * HD + 16, half), BF)],
        [
            spot,
            *[w for w in (w_query, w_key, w_value) for _ in range(2)],
            gain_attn,
            gain_mlp,
            query_scale,
        ],
        specs=[columns(0), columns(1)] * 3
        + [pl.BlockSpec((n,), lambda i, spot: (0,)) for n in (half, half, part)],
        out_specs=[whole((3 * HD + 16, half))],
        scratch=[pltpu.VMEM((256, half), F32)],
        smem=1,
        grid=(1,),
        name="slab",
        us=3,
        mib=60,
    )
    slab_x = swap_x(slab)
    late = lax.dynamic_slice_in_dim(w_output, k * quarter + early, quarter - early, 0)
    late, slab_x = gates([late, slab_x], out_xs)
    out_xs.append(swap_x(late))
    weight_t, gains, scale_col, scale_row = call(
        setup_body,
        [((3 * HD, model), BF), ((8, model), F32), ((HD, 1), F32), ((8, 128), F32)],
        [spot, slab, slab_x],
        smem=1,
        after=[*steps[2], *out_xs[:1]],
        name="setup",
        mib=60,
        us=2,
    )
    weight_sib = swap_core(weight_t)

    norms = None
    queries, keys, far_keys, near = [], [], [], []
    norms = None
    slot = 0
    for step in range(2):
        if step:
            up, down = gates(steps[3], queries)
            arrays = [up, down, *ring_step(up[: dev_rows // 2], down[dev_rows // 2 :])]
        else:
            arrays = [x, *steps[1], *steps[2]]
        count = sum(a.shape[0] for a in arrays) // dev_rows
        moved = (w_hidden, w_return) if step else ()
        outs = [((CHIPS, dev_rows, model), BF)]
        outs += [((count, HD, 128), BF), ((count, 2 * HD, 128), BF)]
        outs += [((count, 3 * HD, 128), BF), ((count, 2 * HD, 128), BF)]
        outs += [((quarter, model), BF)] * len(moved)
        ins = [spot, *arrays, gains, weight_t, weight_sib, scale_col, *moved]
        ins += [norms] if step else []
        norms, q_part, kv_part, near_part, far_part, *moved_parts = call(
            functools.partial(project_body, (len(arrays), count, len(moved), slot)),
            outs,
            ins,
            specs=[vmem_spec] * (len(arrays) + 4) + [any_spec] * (len(moved) + bool(step)),
            out_specs=[any_spec] + [vmem_spec] * (len(outs) - 1),
            scratch=[
                pltpu.VMEM((count, dev_rows, model), BF),
                pltpu.SemaphoreType.DMA((max(1, len(moved)),)),
                pltpu.SemaphoreType.DMA,
            ],
            smem=1,
            after=[(), out_xs[1:]][step],
            aliases={len(ins) - 1: 0} if step else None,
            name="project",
            us=[3, 3][step],
            mib=60,
        )
        slot += count
        queries.append(q_part)
        keys.append(kv_part)
        far_keys += [swap_x(kv_part), swap_far(far_part)]
        near.append(swap_core(near_part))
    hid_part, ret_part = moved_parts
    norms_sib = swap_core(norms)
    parts = [w_output]
    for out_x in out_xs:
        out_x = gate(out_x, [norms])
        parts += [out_x, swap_core(out_x)]
    hid_x = swap_x(gate(hid_part, far_keys))
    ret_x = swap_x(gate(ret_part, far_keys))

    arrays, places = [], []
    at = 0
    for step, q_part in enumerate(queries):
        mine, theirs = (q_part, keys[step], far_keys[2 * step]), (near[step], far_keys[2 * step + 1])
        count = q_part.shape[0]
        for entries, blocks_of in ((OWN_ENTRIES, mine), (SIB_ENTRIES, theirs)):
            for j in range(count):
                entry = entries[at + j]
                last = len(arrays) + len(blocks_of) - 1
                places.append(("q", len(arrays), j, entry, 0))
                places.append(("kv", last - 1, j, entry, 0))
                places.append(("kv", last, j, entry, 1))
            arrays += blocks_of
        at += count
    if groups > 1:
        order = OWN_ENTRIES + SIB_ENTRIES
        mine = jnp.concatenate([*keys, *[a[:, HD:] for a in near]], axis=0)
        theirs = jnp.concatenate([*far_keys[::2], *far_keys[1::2]], axis=0)
        for by in range(1, groups):
            for side, a in enumerate((mine, theirs)):
                places += [
                    ("kv", len(arrays), j, by * GROUP + order[j], side) for j in range(GROUP)
                ]
                arrays.append(turn_groups(a, by))
    pieces, q_t, k_t, k_rows, v_rows, att, lse = call(
        functools.partial(forward_body, {"arrays": len(arrays), "blocks": places}, chunks),
        [
            ((GROUP, HD, 128), BF),
            ((tiles, HD, width), BF),
            ((chunks, HD, 512), BF),
            ((chunks, 512, HD), BF),
            ((chunks, 512, HD), BF),
            ((tiles, HD, width), F32),
            ((tiles, 1, width), F32),
        ],
        [slots_q, slots_k, slots_out, full, total, qblock, *arrays],
        scratch=[
            pltpu.VMEM((2 * GROUP, HD, 64), BF),
            pltpu.VMEM((2, blocks, 2 * HD, 64), BF),
            pltpu.VMEM((chunks, HD + 16, 512), BF),
            pltpu.VMEM((chunks, 512, width), F32),
            pltpu.VMEM((2 * GROUP, HD, 64), BF),
        ],
        smem=5,
        name="attention_forward",
        us=20,
        mib=60,
    )
    (pieces,) = gates([pieces], [parts[2], parts[4]])
    att_t = exchange(pieces).reshape(model, dev_rows)
    hid_x, ret_x = gates([hid_x, ret_x], [att_t])
    for w, first in ((w_hidden, hid_x), (w_return, ret_x)):
        parts += [w, first, swap_core(first)]

    g_sib, g_x = swap_core(g_rows), swap_x(gate(g_rows, [pieces]))

    left_rows = 15 * (half // CHIPS)
    share_rows = left_rows + 2 * (model // 128) * dev_rows + 16
    stream, dy, datt_t, f_own, f_sib, f_x, f_xs = call(
        rows_body,
        [
            ((dev_rows, model), BF),
            ((dev_rows, model), F32),
            ((model, dev_rows), BF),
            ((share_rows, 128), BF),
            ((share_rows, 128), BF),
            ((share_rows, 128), BF),
            ((left_rows, 128), BF),
        ],
        [spot, att_t, x, g_rows, gains, *parts],
        specs=[vmem_spec] * 4 + [any_spec] * 11,
        scratch=[pltpu.VMEM((model, model), BF)] * 3
        + [pltpu.VMEM((3, model, dev_rows), BF), pltpu.SemaphoreType.DMA((3, 5))],
        smem=1,
        name="row_part",
        mib=60,
        us=10,
    )
    datt_t, g_x = gates([datt_t, g_x], ())
    grads = exchange(datt_t.reshape(GROUP, HD, dev_rows))
    g_xs = swap_core(g_x)

    from_x = swap_x(f_x)
    forward = swap_core(f_xs)
    from_sib, from_xs = swap_core(f_sib), swap_x(forward)

    def chunk_call(table, body, chunk, ins, outs, name, after):
        return call(
            body,
            outs,
            [spot, table, *ins],
            specs=[pl.BlockSpec((1, 256, model), lambda i, spot: (chunk, 0, 0))]
            + [whole(a.shape) for a in ins],
            out_specs=[whole(shape) for shape, _ in outs],
            smem=1,
            grid=(1,),
            after=after,
            name=name,
            us=2,
            mib=16,
        )

    def reduce_step(table, step, received, after):
        outs = chunk_call(
            table,
            functools.partial(reduce_step_body, step),
            4 - step,
            received,
            [((256, model if step else model // 2), BF)],
            "reduce_step",
            after,
        )
        return [ring_by_core(outs[0])], outs

    own, other, dq_pieces, scale_sum = call(
        backward_body,
        [
            ((chunks, 2 * HD, 256), F32),
            ((chunks, 2 * HD, 256), BF),
            ((GROUP, HD, 128), BF),
            ((HD, width), F32),
        ],
        [slots_out, begin, clear, qblock, scale_col, grads, q_t, att, lse, k_t, k_rows, v_rows],
        specs=[vmem_spec] * 6 + [any_spec] * 3,
        scratch=[
            pltpu.VMEM((tiles, HD, width), BF),
            pltpu.VMEM((tiles, 1, width), F32),
            pltpu.VMEM((tiles, HD, width), F32),
            pltpu.VMEM((2 * GROUP, HD, 64), BF),
            pltpu.VMEM((chunks, HD, 512), BF),
            pltpu.VMEM((chunks, 512, HD), BF),
            pltpu.VMEM((chunks, 512, HD), BF),
            pltpu.SemaphoreType.DMA((3,)),
        ],
        smem=3,
        after=[forward],
        name="attention_backward",
        us=25,
        mib=60,
    )
    other_x = swap_x(other)
    from_x, from_sib, from_xs, g_xs, norms_sib = gates(
        [from_x, from_sib, from_xs, g_xs, norms_sib], [own]
    )
    (partial,) = call(
        pooled_grad_body,
        [((5, 256, model), BF)],
        [f_own, from_sib, from_x, from_xs, swap_core(from_x), g_rows, g_sib, g_x, g_xs],
        name="pooled_grads",
        us=3,
        mib=40,
    )
    received, done = reduce_step(partial, 0, (), ())
    if groups > 1:
        own = sum_groups(own + other_x.astype(F32), BF)
        other_x = jnp.zeros_like(other_x)
    received, done = reduce_step(partial, 1, received, ())
    d_pieces, d_other = call(
        join_body,
        [((GROUP, 3 * HD, 128), BF), ((10, 3 * HD, 128), BF)],
        [slots_ctx, spot, dq_pieces, own, other_x],
        scratch=[pltpu.VMEM((blocks, 2 * HD, 64), BF)],
        smem=2,
        after=done,
        name="join",
        us=2,
        mib=24 if groups == 1 else 60,
    )
    d_near = swap_core(d_other)
    own_share, other_share = call(
        qkv_grad_body,
        [((3 * HD + 16, half), F32), ((3 * HD + 16, half), BF)],
        [place, spot, d_pieces, scale_sum, norms, norms_sib],
        scratch=[pltpu.VMEM((3 * HD, model), F32)],
        smem=2,
        name="qkv_grads",
        us=4.7,
        mib=24,
    )
    share_x = swap_x(other_share)
    received, done = reduce_step(partial, 2, received, [own_share])

    (table,) = call(
        products_body,
        [((5, 256, model), BF)],
        [spot, d_pieces, d_near, weight_t, weight_sib],
        smem=1,
        after=done,
        name="products",
        us=4,
        mib=24,
    )
    first, done = reduce_step(table, 0, (), ())
    (share,) = call(
        qkv_sum_body,
        [((3 * HD + 16, half), BF)],
        [own_share, share_x, slab],
        after=done,
        name="qkv_sum",
        us=1,
        mib=8,
    )
    share = sum_groups(share.astype(F32), BF).astype(BF) if groups > 1 else share
    share_near = swap_core(share)
    received, done = reduce_step(partial, 3, received, [share])
    received_near = swap_core(received[0])
    (chip_share,) = call(
        chip_pack_body,
        [((2 * (3 * HD + 16), half), BF)],
        [spot, share, share_near],
        smem=1,
        after=done,
        name="chip_pack",
        us=1,
        mib=8,
    )
    q_steps = [chip_share, ring_by_core(chip_share)]
    first, done = reduce_step(table, 1, first, [chip_share])
    (mine,) = chunk_call(
        partial,
        reduce_end_body,
        0,
        (*received, received_near),
        [((256, model), BF)],
        "reduce_end",
        [chip_share],
    )
    first, done = reduce_step(table, 2, first, [mine])
    mine = sum_groups(mine.astype(F32), BF).astype(BF) if groups > 1 else mine
    m_steps = [mine, ring_by_core(mine)]
    q_steps.append(ring_by_core(q_steps[-1]))
    first, done = reduce_step(table, 3, first, [*done, q_steps[2]])
    m_steps.append(ring_by_core(m_steps[-1]))
    q_steps.append(ring_by_core(q_steps[-1]))
    m_steps.append(ring_by_core(m_steps[-1]))
    q_near = [swap_core(a) for a in q_steps[1:3]]
    m_near = [swap_core(a) for a in m_steps[1:3]]
    elements = float(ctx_count * 2 * dev_rows * model)
    chunk = half // CHIPS
    grads_shape = [((half, model), F32)] * 3
    *rows_grads, gain_sums, tails = call(
        functools.partial(rows_place_body, True, elements),
        [*grads_shape, ((half, 128), F32), ((8, 128), F32)],
        [spot, *m_steps[:3], *m_near, w_hidden],
        out_specs=[any_spec] * 3 + [vmem_spec] * 2,
        scratch=[pltpu.VMEM((5, 3, chunk, model), F32), pltpu.SemaphoreType.DMA((5, 3))],
        smem=1,
        name="rows_place",
        us=4,
        mib=40,
    )

    first_near = swap_core(first[0])
    (d_in,) = chunk_call(
        table,
        inputs_grad_body,
        0,
        (*first, first_near, x, dy, gains),
        [((dev_rows, model), BF)],
        "inputs_grad",
        [m_steps[2], tails],
    )

    def last_step(a, axis):
        size = a.shape[axis] // 2
        return ring_by_core(lax.dynamic_slice_in_dim(a, k * size, size, axis))

    q_last = last_step(q_steps[-1], 0)
    m_held = m_steps[-1]
    m_last = last_step(m_held, 1)
    q_near += [swap_core(a) for a in q_steps[3:]]
    m_near += [swap_core(m_held)]
    grad_query, grad_key, grad_value, gain_one_grad, scale_grad = call(
        qkv_place_body,
        [((half, model), F32)] * 3 + [((half,), F32), ((part,), F32)],
        [spot, *q_steps, *q_near, q_last, swap_core(q_last), gain_attn, scale_row],
        scratch=[pltpu.VMEM((3, model, half), BF)],
        smem=1,
        name="qkv_place",
        us=6,
        mib=40,
    )
    (m_last,) = gates([m_last], [grad_query, d_in])
    ins = [spot, m_held, m_near[2], m_last, swap_core(m_last), w_hidden, gain_mlp, gain_sums, tails]
    grad_output, grad_hidden, grad_return, gain_two_grad, root_means = call(
        functools.partial(rows_place_body, False, elements),
        [*grads_shape, ((half,), F32), ((2,), F32)],
        [*ins, *rows_grads],
        specs=[vmem_spec] * (len(ins) - 1) + [any_spec] * 3,
        out_specs=[any_spec] * 3 + [vmem_spec] * 2,
        scratch=[
            pltpu.VMEM((3, 3, chunk, model), F32),
            pltpu.VMEM((half, 128), F32),
            pltpu.SemaphoreType.DMA((3, 3)),
        ],
        smem=1,
        aliases={len(ins) + at: at for at in range(3)},
        name="rows_place",
        us=3,
        mib=40,
    )
    return (
        stream.reshape(stream_in.shape),
        d_in.reshape(stream_in.shape),
        grad_query,
        grad_key,
        grad_value,
        grad_output,
        grad_hidden,
        grad_return,
        gain_one_grad,
        gain_two_grad,
        scale_grad,
        root_means,
    )


def solution(mesh):
    rows = P(None, ("ctx", "fsdp"), None)
    weight, vector = P("fsdp", None), P("fsdp")
    return jax.shard_map(
        functools.partial(per_device, mesh.shape["ctx"]),
        mesh=mesh,
        in_specs=(rows, P(), *([weight] * 6), *([vector] * 3), rows),
        out_specs=(rows, rows, *([weight] * 6), *([vector] * 3), P()),
        check_vma=False,
    )
```
